32 devices in a mesh: freq: 4 (over x, core), tile: 8 (over z, y).
Axes of the slice: x: 2, y: 2, z: 4, core: 2. Of those that a mesh axis runs over, the one named last changes fastest.
Arguments:
- visibilities: bfloat16 [8, 8, 64, 4096], P('tile', None, None, 'freq'), may hold values from -6 to 6
- uv_rows: float32 [8, 2, 4096], P('tile', None, 'freq'), may hold values from -5.76 to 5.76
- chan_scale: float32 [64], replicated, may hold values from 0.7 to 1.4
- valid_rows: int32 [8, 4], P('tile', 'freq'), may hold values from 512 to 1024
- aterm: float32 [4, 512, 2, 1024], P('freq'), may hold values from -4 to 4
- taper: float32 [32, 32], replicated, may hold values from 0.25 to 1.75
- stations: int32 [8, 4, 32, 2], P('tile', 'freq'), may hold values from 0 to 511, all different within a row
- owner: int32 [8, 4, 32, 1], P('tile', 'freq'), may hold values from 0 to 31; in each aligned block of 32 rows (0 to 31, 32 to 63, ..., all dimensions but the last counted through in order) at most 2 rows name the same one
- u_offset: int32 [8, 4, 32, 1], P('tile', 'freq'), may hold values from 0 to 255
- v_start: int32 [8, 4, 32, 1], P('tile', 'freq'), may hold values from 0 to 224
Outputs:
- uv_band: float32 [8, 8192, 256], P(None, ('freq', 'tile'))
The draws below stay inside these ranges and needn't reach their ends.
Inputs may be any that keep to these rules, and one draw needn't show every extreme that they name: `owner`: among the 32 subgrids of one index of tile and one of freq, no tile is named more than 2 times; in every draw some tile is named exactly 2 times by some of them. The two stations of a subgrid differ.
All inputs are finite; a program needn't handle non-finite values.
Results may differ from the reference program's by a relative error of at most 0.0047.
Values may be sent and summed in bfloat16 or wider, within the bound.
No kernel may reach another device: no remote copies, remote signals or barrier semaphores. Data moves between devices by JAX's collectives and lax.ppermute only.
A program may use at most 128 MiB of HBM per device.

```python
import math
import jax
import jax.numpy as jnp
import numpy as np
from jax import lax

STATIONS = 512
SG = 32
TSTEP = 128
CHAN_G = 16
ROWS_DEV = 1024
TILE_W = 256
BAND_V = 256
GROUPS = 4
SHARDS = 8
CHAN = 64
ROWS_T = 4096
S_D = 32
CAP = 2
GRID_U = 8192
DEVICES = 32


def place_ends(array, own_key, smallest, top_value):
    longest = array.shape.index(max(array.shape))
    spots = []
    for shift in (0, 1):
        where = [jax.random.randint(jax.random.fold_in(own_key, axis), (), 0, length) for axis, length in enumerate(array.shape)]
        where[longest] = (where[longest] + shift) % array.shape[longest]
        spots.append(tuple(where))
    return array.at[spots[0]].set(smallest).at[spots[1]].set(top_value)


def steps_of(key, dims, cuts, smallest, top_value):
    factor_of, own = 1.0, jax.random.fold_in(key, 6)
    for dim, parts in cuts:
        draws = jnp.exp(jax.random.uniform(jax.random.fold_in(own, dim), (parts,), jnp.float32, smallest / len(cuts), top_value / len(cuts)))
        factor_of = factor_of * jnp.repeat(draws, dims[dim] // parts).reshape([-1 if axis == dim else 1 for axis in range(len(dims))])
    return factor_of


def picks_of(key, rows, amount, top, lift):
    ranking = jax.random.permutation(jax.random.fold_in(key, 1), amount)
    pull = ranking
    for power in range(3):
        pull = pull * pull // amount
    pull = pull * lift // amount
    chance = jax.random.randint(jax.random.fold_in(key, 2), (rows, amount), 0, 4096) + pull
    holders = jax.random.permutation(jax.random.fold_in(key, 3), rows)[jnp.arange(amount) % rows]
    chance = jnp.where(jnp.arange(rows)[:, None] == holders[None, :], 1 << 14, chance)
    score = chance * amount + jnp.arange(amount)
    return lax.top_k(score.astype(jnp.int32), top)[1].astype(jnp.int32)


def deal_out(own_key, own, number, rows, count, top, bound, lean):
    order = jax.random.permutation(own_key, count)
    packed, usual = load_shares(count, rows * top, bound, lean, True), load_shares(count, rows * top, bound, lean, False)
    places = jnp.arange(count)

    def named(sizes, rotation):
        used = int((sizes > 0).sum())
        fixed = max(1, used // 4)
        passed = fixed + (places - fixed + rotation * (used - fixed)) % max(1, count - fixed)
        return jnp.zeros((count,), jnp.int32).at[order[jnp.where(places < fixed, places, passed)]].set(jnp.asarray(sizes, jnp.int32))

    sizes = jnp.where(number % 4 == 0, named(packed, number // 4), named(usual, number - number // 4 - 1))
    mixed = jax.random.permutation(jax.random.fold_in(own, 3), count)
    source_of, receiver = mixed[0:count // 2 * 2:2], mixed[1:count // 2 * 2:2]
    slack = jnp.minimum(sizes[source_of] - 1, bound - sizes[receiver]) // 2
    slack = jnp.where((source_of == order[0]) | (receiver == order[0]) | (sizes[receiver] == 0), 0, jnp.maximum(slack, 0))
    passed = jax.random.randint(jax.random.fold_in(own, 4), (count // 2,), 0, 1 << 20) % (slack + 1)
    sizes = sizes.at[source_of].add(-passed).at[receiver].add(passed)
    items = jnp.searchsorted(jnp.cumsum(sizes), jnp.arange(rows * top), side="right").astype(jnp.int32)
    table = items.reshape(top, rows).T
    table = table[jax.random.permutation(jax.random.fold_in(own, 1), rows)]
    rotation = jax.random.randint(jax.random.fold_in(own, 2), (rows, 1), 0, top)
    return jnp.take_along_axis(table, (jnp.arange(top)[None, :] + rotation) % top, axis=1)


def load_shares(amount, total, most, slope, full):
    loads = [(1 << 20) // math.isqrt(standing ** slope) + 1 for standing in range(1, amount + 1)]
    largest = most if full else min(most, max(-(-total // amount), total * loads[0] // sum(loads)))
    least = 1 if total - largest >= amount - 1 else 0
    counts, rest = [largest] + [least] * (amount - 1), total - largest - least * (amount - 1)
    while rest > 0:
        free = [i for i in range(1, amount) if counts[i] < largest] or [i for i in range(1, amount) if counts[i] < most]
        mass, left = sum([loads[i] for i in free]), rest
        for i in free:
            addition = min(most - counts[i], max(1, left * loads[i] // mass), rest)
            counts[i] = counts[i] + addition
            rest = rest - addition
    return np.array(counts)


def noise(stream_key, extent, width, bound, cuts=(), kind=jnp.bfloat16):
    factor_of = steps_of(stream_key, extent, cuts, -0.22, 0.18) if cuts else 1.0
    values = jax.random.normal(stream_key, extent, jnp.float32) * width * factor_of
    return jnp.minimum(jnp.maximum(values, -bound), bound).astype(kind)


def setup_inputs(seed: int = 0) -> dict:
    key_list = jax.random.split(jax.random.key(seed), 11)
    visibilities = noise(key_list[0], (SHARDS, 8, CHAN, ROWS_T), 1.0, 6.0, ((0, 8), (3, 4)))
    uv_rows = jnp.clip(jax.random.uniform(key_list[1], (SHARDS, 2, ROWS_T), jnp.float32, -5.76, 5.76) * steps_of(key_list[1], (SHARDS, 2, ROWS_T), ((0, 8), (2, 4)), -0.4, 0.0), -5.76, 5.76)
    chan_scale = jnp.clip(jnp.exp(jax.random.uniform(key_list[2], (CHAN,), jnp.float32, math.log(0.7), math.log(1.4))), 0.7, 1.4)
    valid_rows = place_ends(jax.random.randint(key_list[3], (SHARDS, GROUPS), ROWS_DEV // 2, ROWS_DEV + 1), jax.random.fold_in(key_list[3], 1), ROWS_DEV // 2, ROWS_DEV).astype(jnp.int32)
    aterm = noise(key_list[4], (GROUPS, STATIONS, 2, SG * SG), 0.7, 4.0, ((0, 4),), jnp.float32)
    taper = jnp.clip(1.0 + 0.15 * jax.random.normal(key_list[5], (SG, SG), jnp.float32), 0.25, 1.75)
    stations = picks_of(key_list[6], SHARDS * GROUPS * S_D, STATIONS, 2, 0).reshape((SHARDS, GROUPS, S_D, 2))
    owner_keys = jax.random.split(jax.random.fold_in(key_list[7], 1), SHARDS * GROUPS * S_D // S_D)
    owner_turns = jax.random.permutation(jax.random.fold_in(key_list[7], 3), SHARDS * GROUPS * S_D // S_D)
    owner = jax.vmap(lambda own, number: deal_out(jax.random.fold_in(key_list[7], 2), own, number, S_D, DEVICES, 1, CAP, 2))(owner_keys, owner_turns).reshape((SHARDS, GROUPS, S_D, 1))
    u_offset = place_ends(jax.random.randint(key_list[8], (SHARDS, GROUPS, S_D, 1), 0, TILE_W), jax.random.fold_in(key_list[8], 1), 0, TILE_W - 1).astype(jnp.int32)
    v_start = place_ends(jax.random.randint(key_list[9], (SHARDS, GROUPS, S_D, 1), 0, BAND_V - SG + 1), jax.random.fold_in(key_list[9], 1), 0, BAND_V - SG).astype(jnp.int32)
    return {"visibilities": visibilities, "uv_rows": uv_rows, "chan_scale": chan_scale, "valid_rows": valid_rows, "aterm": aterm, "taper": taper, "stations": stations, "owner": owner, "u_offset": u_offset, "v_start": v_start}


def first_pass(matrix, values):
    return jnp.einsum('al,splm->spam', matrix, values, precision=lax.Precision.HIGHEST)

def second_pass(matrix, values):
    return jnp.einsum('bm,spam->spab', matrix, values, precision=lax.Precision.HIGHEST)

def make_subgrids(vis_blocks, uv_blocks, scale_group, aterm_group, taper, station_pairs):
    sub_count = vis_blocks.shape[0]
    fan_width = vis_blocks.shape[2]
    centred = jnp.arange(SG, dtype=jnp.float32) - SG // 2
    coeffs = centred * (2.0 * math.pi / SG)
    u_shift = (uv_blocks[:, 0, None, :] * scale_group[None, :, None]).reshape(sub_count, fan_width)
    v_shift = (uv_blocks[:, 1, None, :] * scale_group[None, :, None]).reshape(sub_count, fan_width)
    angle_u = coeffs[None, :, None] * u_shift[:, None, :]
    cos_u = jnp.cos(angle_u)
    sin_u = jnp.sin(angle_u)
    vis_re = vis_blocks[:, :4, :].astype(jnp.float32)
    vis_im = vis_blocks[:, 4:, :].astype(jnp.float32)
    inv_root = 1.0 / math.sqrt(fan_width)
    factor_re = (cos_u[:, None] * vis_re[:, :, None] - sin_u[:, None] * vis_im[:, :, None]) * inv_root
    factor_im = (cos_u[:, None] * vis_im[:, :, None] + sin_u[:, None] * vis_re[:, :, None]) * inv_root
    factors = jnp.stack([factor_re, factor_im], 1).astype(jnp.bfloat16).reshape(sub_count, 8 * SG, fan_width)
    angle_v = coeffs[None, :, None] * v_shift[:, None, :]
    table_v = jnp.stack([jnp.cos(angle_v), jnp.sin(angle_v)], 1).astype(jnp.bfloat16).reshape(sub_count, 2 * SG, fan_width)
    products = jnp.einsum('smk,snk->smn', table_v.astype(jnp.float32), factors.astype(jnp.float32))
    products = products.reshape(sub_count, 2, SG, 2, 4, SG)
    image_re = (products[:, 0, :, 0] - products[:, 1, :, 1]).transpose(0, 2, 3, 1)
    image_im = (products[:, 0, :, 1] + products[:, 1, :, 0]).transpose(0, 2, 3, 1)
    station_one = aterm_group[station_pairs[:, 0]].reshape(sub_count, 2, SG, SG)
    station_two = aterm_group[station_pairs[:, 1]].reshape(sub_count, 2, SG, SG)
    gain_re = (station_one[:, 0] * station_two[:, 0] + station_one[:, 1] * station_two[:, 1]) * taper
    gain_im = (station_one[:, 1] * station_two[:, 0] - station_one[:, 0] * station_two[:, 1]) * taper
    shaped_re = image_re * gain_re[:, None] - image_im * gain_im[:, None]
    shaped_im = image_re * gain_im[:, None] + image_im * gain_re[:, None]
    offsets_cell = jnp.arange(SG, dtype=jnp.int32) - SG // 2
    phase_int = offsets_cell[:, None] * offsets_cell[None, :] % SG
    angles = phase_int.astype(jnp.float32) * (2.0 * math.pi / SG)
    unit_scale = 1.0 / math.sqrt(SG)
    four_cos = jnp.cos(angles) * unit_scale
    four_sin = -jnp.sin(angles) * unit_scale
    first_re = first_pass(four_cos, shaped_re) - first_pass(four_sin, shaped_im)
    first_im = first_pass(four_cos, shaped_im) + first_pass(four_sin, shaped_re)
    second_re = second_pass(four_cos, first_re) - second_pass(four_sin, first_im)
    second_im = second_pass(four_cos, first_im) + second_pass(four_sin, first_re)
    return jnp.concatenate([second_re, second_im], 1).astype(jnp.bfloat16)

def reference(visibilities, uv_rows, chan_scale, valid_rows, aterm, taper, stations, owner, u_offset, v_start):
    uv_grid = jnp.zeros((8, GRID_U, BAND_V), jnp.float32)
    row_numbers = jnp.arange(ROWS_T, dtype=jnp.int32)
    local_row = row_numbers % ROWS_DEV
    source = row_numbers // ROWS_DEV
    cell_steps = jnp.arange(SG, dtype=jnp.int32)
    block_size = min(8, S_D)

    def one_pair(grid_sum, pair_index):
        shard_index = pair_index // GROUPS
        group_index = pair_index % GROUPS
        vis_shard = lax.dynamic_index_in_dim(visibilities, shard_index, 0, False)
        counts_shard = lax.dynamic_index_in_dim(valid_rows, shard_index, 0, False)
        live_rows = local_row < counts_shard[source]
        vis_group = lax.dynamic_slice_in_dim(vis_shard, (group_index * CHAN_G).astype(jnp.int32), CHAN_G, 1)
        vis_group = jnp.where(live_rows[None, None, :], vis_group, jnp.zeros((), jnp.bfloat16))
        vis_blocks = vis_group.reshape(8, CHAN_G, S_D, TSTEP).transpose(2, 0, 1, 3).reshape(S_D, 8, CHAN_G * TSTEP)
        uv_shard = lax.dynamic_index_in_dim(uv_rows, shard_index, 0, False)
        uv_blocks = uv_shard.reshape(2, S_D, TSTEP).transpose(1, 0, 2)
        scale_group = lax.dynamic_slice_in_dim(chan_scale, (group_index * CHAN_G).astype(jnp.int32), CHAN_G, 0)
        aterm_group = lax.dynamic_index_in_dim(aterm, group_index, 0, False)
        pick = lambda table_in: lax.dynamic_index_in_dim(lax.dynamic_index_in_dim(table_in, shard_index, 0, False), group_index, 0, False)
        station_pairs = pick(stations)
        owners = pick(owner)[:, 0]
        start_u = owners * TILE_W + pick(u_offset)[:, 0]
        start_v = pick(v_start)[:, 0]
        blocks_n = S_D // block_size

        def one_block(pieces):
            return make_subgrids(pieces[0], pieces[1], scale_group, aterm_group, taper, pieces[2])
        subgrids = lax.map(one_block, (vis_blocks.reshape(blocks_n, block_size, 8, CHAN_G * TSTEP), uv_blocks.reshape(blocks_n, block_size, 2, TSTEP), station_pairs.reshape(blocks_n, block_size, 2)))
        subgrids = subgrids.reshape(S_D, 8, SG, SG)
        column_ids = (start_u[:, None, None] + cell_steps[None, :, None]) % GRID_U
        row_ids = start_v[:, None, None] + cell_steps[None, None, :]
        grid_sum = grid_sum.at[:, column_ids, row_ids].add(subgrids.astype(jnp.float32).transpose(1, 0, 2, 3))
        return (grid_sum, None)
    uv_grid, _ = lax.scan(one_pair, uv_grid, jnp.arange(SHARDS * GROUPS, dtype=jnp.int32))
    return uv_grid
```

```python
import functools
import math

import jax
import jax.numpy as jnp
import ml_dtypes
import numpy as np
from jax import lax
from jax.experimental import pallas as pl
from jax.experimental.pallas import tpu as pltpu
from jax.sharding import PartitionSpec as P

SG = 32
HALF = SG // 2
TSTEP = 128
CHAN_G = 16
FAN = CHAN_G * TSTEP
TILE_W = 256
BAND_V = 256
LANES = 128
COMPS = 8
POL = 4
POS_ROWS = 16
SUB_ROWS = 2 * SG
CAP = 2
VMEM_LIMIT = 48 << 20
f32 = jnp.float32
bf16 = jnp.bfloat16


def vmem():
    return pl.BlockSpec(memory_space=pltpu.VMEM)


def smem():
    return pl.BlockSpec(memory_space=pltpu.SMEM)


IMAGE_ROWS = np.array([HALF + i for i in range(HALF)] + [0] + [HALF - i for i in range(1, HALF)])


def split(matrix):
    high = matrix.astype(np.float32).astype(ml_dtypes.bfloat16)
    low = (matrix - high.astype(np.float64)).astype(np.float32).astype(ml_dtypes.bfloat16)
    return high, low


def fourier():
    cells = np.arange(SG) - HALF
    angles = (cells[:, None] * cells[None, :] % SG) * (2.0 * math.pi / SG)
    return np.cos(angles), -np.sin(angles)


def lane_transform():
    cos, sin = fourier()
    table = np.zeros((2, 2, 2, SG, 2, 2, 2, SG))
    for p in range(2):
        y_re = {(0, 0): cos, (1, 1): -cos, (1, 0): -sin, (0, 1): -sin}
        y_im = {(0, 0): sin, (1, 1): -sin, (1, 0): cos, (0, 1): cos}
        for gain in range(2):
            for part in range(2):
                re, im = y_re[gain, part].T, y_im[gain, part].T
                table[gain, p, part, :, 0, p, 0, :] = re
                table[gain, p, part, :, 0, p, 1, :] = im
                table[gain, p, part, :, 1, p, 0, :] = -im
                table[gain, p, part, :, 1, p, 1, :] = re
    return split(table.reshape(256, 256))


def row_transform():
    cos, sin = fourier()
    high, low = split(np.concatenate([cos[:, IMAGE_ROWS], sin[:, IMAGE_ROWS]], 1))
    return np.concatenate([high, high, low], 1)


def lane_tiles():
    table = np.zeros((POL, SG, POL, POL, SG))
    for q in range(POL):
        for copy in range(POL):
            table[q, :, q, copy, :] = np.eye(SG)
    table = table.reshape(LANES, POL * LANES)
    return np.concatenate([table] * 3, 0).astype(ml_dtypes.bfloat16)


def unit_powers(theta):
    half = theta * 0.5
    square = half * half
    sin_h = half * (
        1.0 + square * (-1.0 / 6 + square * (1.0 / 120 + square * (-1.0 / 5040 + square * (1.0 / 362880))))
    )
    cos_h = 1.0 + square * (
        -0.5 + square * (1.0 / 24 + square * (-1.0 / 720 + square * (1.0 / 40320 + square * (-1.0 / 3628800))))
    )
    powers = {0: (jnp.ones_like(theta), jnp.zeros_like(theta))}
    powers[1] = (1.0 - 2.0 * sin_h * sin_h, 2.0 * sin_h * cos_h)
    for n in range(2, HALF + 1):
        (ca, sa), (cb, sb) = powers[n // 2], powers[n - n // 2]
        if n % 2 == 0:
            powers[n] = (1.0 - 2.0 * sa * sa, 2.0 * sa * ca)
        else:
            powers[n] = (ca * cb - sa * sb, ca * sb + sa * cb)
    return powers


def image_kernel(
    scalars, vis_ref, uv_ref, scale_ref, out_ref, u_tab, v_tab, w_tab, lhs_a, lhs_b, rhs_a, rhs_b
):
    count = out_ref.shape[0]
    lane = lax.broadcasted_iota(jnp.int32, (CHAN_G, TSTEP), 1)
    out_lane = lax.broadcasted_iota(jnp.int32, (SG, LANES), 1)
    is_re = out_lane % (2 * SG) < SG
    first_row = lax.broadcasted_iota(jnp.int32, (HALF, LANES), 0) == 0

    def build(s, lhs, rhs):
        part = pl.ds(s * TSTEP, TSTEP)
        scale = scale_ref[...] * (2.0 * math.pi / SG)
        live = lane + s * TSTEP < scalars[1]
        for c in range(COMPS):
            values = vis_ref[c, :, part].astype(f32)
            w_tab[c] = jnp.where(live, values, 0.0)
        powers = unit_powers(uv_ref[0:1, part] * scale)
        for n in range(HALF):
            u_tab[:, n, :] = powers[n][0]
            u_tab[:, HALF + n, :] = powers[n][1]
        u_tab[:, SG, :] = powers[HALF][0]
        u_tab[:, SG + 1, :] = powers[HALF][1]
        powers = unit_powers(uv_ref[1:2, part] * scale)
        for m in range(SG):
            cos, sin = powers[abs(m - HALF)]
            v_tab[:, m, :] = cos
            v_tab[:, SG + m, :] = sin if m >= HALF else -sin
        for h in range(CHAN_G):
            cols = pl.ds(h * TSTEP, TSTEP)
            rhs[:, cols] = v_tab[h].astype(bf16)
            u_rows = u_tab[h, 0:SG, :]
            for c in range(COMPS):
                lhs[c * SG : (c + 1) * SG, cols] = (u_rows * w_tab[c, h : h + 1, :]).astype(bf16)
            w_all = w_tab[:, h, :]
            last = jnp.concatenate(
                [w_all * u_tab[h, SG : SG + 1, :], w_all * u_tab[h, SG + 1 : SG + 2, :]], 0
            )
            lhs[COMPS * SG :, cols] = last.astype(bf16)

    def finish(s, lhs, rhs):
        sums = lax.dot_general(
            lhs[...], rhs[...], (((1,), (1,)), ((), ())), preferred_element_type=f32
        )

        def rows(c):
            return jnp.concatenate([sums[c * SG : (c + 1) * SG], sums[(c + 1) * SG : (c + 2) * SG]], 1)

        def extra(c):
            c = c + COMPS * SG
            return jnp.concatenate([sums[c : c + 1], sums[c + 1 : c + 2]], 1)

        for pair in range(2):
            x, y = rows(2 * pair), rows(POL + 2 * pair)
            xc, xs, yc, ys = x[:HALF], x[HALF:], y[:HALF], y[HALF:]
            exc, eyc = extra(2 * pair), extra(POL + 2 * pair)
            exs, eys = extra(COMPS + 2 * pair), extra(COMPS + POL + 2 * pair)
            low_re = jnp.where(first_row, exc + eys, xc + ys)
            low_im = jnp.where(first_row, eyc - exs, yc - xs)
            f_re = jnp.concatenate([xc - ys, low_re], 0)
            f_im = jnp.concatenate([yc + xs, low_im], 0)
            swapped = jnp.where(is_re, -pltpu.roll(f_im, LANES - SG, 1), pltpu.roll(f_im, SG, 1))
            out_ref[s, pair * SG : (pair + 1) * SG, :] = (f_re + swapped).astype(bf16)

    bufs = ((lhs_a, rhs_a), (lhs_b, rhs_b))
    build(0, *bufs[0])
    for s in range(count):
        if s + 1 < count:
            build(s + 1, *bufs[(s + 1) % 2])
        finish(s, *bufs[s % 2])


def images(vis, uv, scale, group, live_rows):
    rows = vis.shape[2]
    count = rows // TSTEP
    scalars = jnp.stack([group, live_rows]).astype(jnp.int32)
    return pl.pallas_call(
        image_kernel,
        out_shape=jax.ShapeDtypeStruct((count, SUB_ROWS, LANES), bf16),
        grid_spec=pltpu.PrefetchScalarGridSpec(
            num_scalar_prefetch=1,
            grid=(1,),
            in_specs=[
                pl.BlockSpec((COMPS, CHAN_G, rows), lambda i, at: (0, at[0], 0)),
                pl.BlockSpec((2, rows), lambda i, at: (0, 0)),
                pl.BlockSpec((CHAN_G, LANES), lambda i, at: (at[0], 0)),
            ],
            out_specs=pl.BlockSpec((count, SUB_ROWS, LANES), lambda i, at: (0, 0, 0)),
            scratch_shapes=[
                pltpu.VMEM((CHAN_G, SG + 8, LANES), f32),
                pltpu.VMEM((CHAN_G, 2 * SG, LANES), f32),
                pltpu.VMEM((COMPS, CHAN_G, LANES), f32),
                pltpu.VMEM((COMPS * SG + 16, FAN), bf16),
                pltpu.VMEM((COMPS * SG + 16, FAN), bf16),
                pltpu.VMEM((2 * SG, FAN), bf16),
                pltpu.VMEM((2 * SG, FAN), bf16),
            ],
        ),
        compiler_params=pltpu.CompilerParams(vmem_limit_bytes=VMEM_LIMIT),
        name="images",
    )(scalars, vis, uv, scale)


def gain_kernel(stations, aterm, taper, tiles, out_ref, rows, sems):
    count = rows.shape[0] // 2

    def copy(i):
        return pltpu.make_async_copy(
            aterm.at[stations[i % count, i // count]], rows.at[i], sems.at[i]
        )

    def start(i, _):
        copy(i).start()
        return 0

    def wait(i, _):
        copy(i).wait()
        return 0

    lax.fori_loop(0, 2 * count, start, 0)
    lax.fori_loop(0, 2 * count, wait, 0)
    for r in range(SG * SG // LANES):
        cols = pl.ds(r * LANES, LANES)
        one_re, one_im = rows[0:count, 0, cols], rows[0:count, 1, cols]
        two_re, two_im = rows[count:, 0, cols], rows[count:, 1, cols]
        shape = taper[0:1, cols] * (1.0 / (math.sqrt(FAN) * SG))
        gain = jnp.concatenate(
            [(one_re * two_re + one_im * two_im) * shape, (one_im * two_re - one_re * two_im) * shape], 0
        )
        high = gain.astype(bf16)
        rest = gain - high.astype(f32)
        mid = rest.astype(bf16)
        low = (rest - mid.astype(f32)).astype(bf16)
        tiled = jnp.dot(
            jnp.concatenate([high, mid, low], 1), tiles[...], preferred_element_type=f32
        )
        for q in range(POL):
            row = list(IMAGE_ROWS).index(POL * r + q)
            lanes = tiled[:, q * LANES : (q + 1) * LANES]
            out_ref[0, row] = lanes[:count]
            out_ref[1, row] = lanes[count:]


def gains(stations, aterm, taper):
    count = stations.shape[0]
    return pl.pallas_call(
        gain_kernel,
        out_shape=jax.ShapeDtypeStruct((2, SG, count, LANES), f32),
        in_specs=[smem(), pl.BlockSpec(memory_space=pl.ANY), vmem(), vmem()],
        out_specs=vmem(),
        scratch_shapes=[
            pltpu.VMEM((2 * count, 2, SG * SG), f32),
            pltpu.SemaphoreType.DMA((2 * count,)),
        ],
        compiler_params=pltpu.CompilerParams(vmem_limit_bytes=VMEM_LIMIT),
        name="gains",
    )(stations, aterm, taper, lane_tiles())


def subgrid_kernel(
    chunks_n, mine, owner, place, gain, w_high, w_low, f_rows, *refs
):
    chunks = refs[:chunks_n]
    out_ref, d_high, d_low, y_ref, pos, taken = refs[chunks_n:]
    block = chunks[0].shape[0]
    lane = lax.broadcasted_iota(jnp.int32, (1, LANES), 1)

    def clear(i, _):
        taken[i] = 0
        return 0

    lax.fori_loop(0, taken.shape[0], clear, 0)
    pos[...] = jnp.zeros_like(pos)
    for k in range(chunks_n):
        base = (mine[0] ^ k) * block

        def shape(i, _):
            gain_re, gain_im = gain[0, :, base + i, :], gain[1, :, base + i, :]
            for pair in range(2):
                image = chunks[k][i, pair * SG : (pair + 1) * SG, :].astype(f32)
                both = jnp.concatenate([image * gain_re, image * gain_im], 1)
                high = both.astype(bf16)
                at = pl.ds(pl.multiple_of(((k * block + i) * 2 + pair) * SG, SG), SG)
                d_high[at, :] = high
                d_low[at, :] = (both - high.astype(f32)).astype(bf16)
            return 0

        lax.fori_loop(0, block, shape, 0, unroll=2)
    step = 512
    for i in range(d_high.shape[0] // step):
        at = pl.ds(i * step, step)
        high = d_high[at, :]
        y_ref[at, :] = (
            jnp.dot(high, w_high[...], preferred_element_type=f32)
            + jnp.dot(d_low[at, :], w_high[...], preferred_element_type=f32)
            + jnp.dot(high, w_low[...], preferred_element_type=f32)
        )
    for k in range(chunks_n):
        base = (mine[0] ^ k) * block

        def transform(i, _):
            at = pl.multiple_of((k * block + i) * 2 * SG, 2 * SG)
            one, two = y_ref[pl.ds(at, SG), :], y_ref[pl.ds(at + SG, SG), :]
            rows = jnp.concatenate(
                [
                    jnp.concatenate([one[:, :LANES], two[:, :LANES]], 1),
                    jnp.concatenate([one[:, LANES:], two[:, LANES:]], 1),
                ],
                0,
            )
            high = rows.astype(bf16)
            low = (rows - high.astype(f32)).astype(bf16)
            cells = jnp.dot(
                f_rows[...], jnp.concatenate([high, low, high], 0), preferred_element_type=f32
            ).astype(bf16)
            s = base + i
            dest = owner[s]
            slot = taken[dest]
            taken[dest] = slot + 1
            slot = jnp.minimum(slot, CAP - 1)
            start = pl.multiple_of(slot * SUB_ROWS, SUB_ROWS)
            out_ref[dest, pl.ds(start, SG), :] = cells[:, :LANES]
            out_ref[dest, pl.ds(start + SG, SG), :] = cells[:, LANES:]
            row = jnp.where(lane == 0, place[s, 0], jnp.where(lane == 1, place[s, 1], 1))
            pos[dest, pl.ds(slot, 1), :] = row.astype(f32)
            return 0

        lax.fori_loop(0, block, transform, 0, unroll=2)
    out_ref[:, CAP * SUB_ROWS :, :] = pos[...].astype(bf16)


def subgrids(chunks, mine, owner, place, gain, devices_n):
    count = owner.shape[0]
    return pl.pallas_call(
        functools.partial(subgrid_kernel, len(chunks)),
        out_shape=jax.ShapeDtypeStruct((devices_n, CAP * SUB_ROWS + POS_ROWS, LANES), bf16),
        in_specs=[smem()] * 3 + [vmem()] * (4 + len(chunks)),
        out_specs=vmem(),
        scratch_shapes=[
            pltpu.VMEM((count * 2 * SG, 2 * LANES), bf16),
            pltpu.VMEM((count * 2 * SG, 2 * LANES), bf16),
            pltpu.VMEM((count * 2 * SG, 2 * LANES), f32),
            pltpu.VMEM((devices_n, POS_ROWS, LANES), f32),
            pltpu.SMEM((devices_n,), jnp.int32),
        ],
        compiler_params=pltpu.CompilerParams(vmem_limit_bytes=VMEM_LIMIT),
        name="subgrids",
    )(mine, owner, place, gain, *lane_transform(), row_transform(), *chunks)


def place_kernel(pos, arrived, main_ref, margin_ref, acc):
    slots = arrived.shape[0] * CAP
    acc[...] = jnp.zeros_like(acc)
    columns = lax.broadcasted_iota(jnp.int32, (SG, BAND_V), 1) - lax.broadcasted_iota(
        jnp.int32, (SG, BAND_V), 0
    )

    def add(i, _):
        @pl.when(pos[i, 2] > 0)
        def _():
            source, slot = i // CAP, i % CAP
            start = pl.multiple_of(slot * SUB_ROWS, SUB_ROWS)
            cells = arrived[source, pl.ds(start, SUB_ROWS), :]
            stacked = jnp.concatenate([cells[:, SG * k : SG * (k + 1)] for k in range(POL)], 0)
            hot = jnp.where(columns == pos[i, 1], 1.0, 0.0).astype(bf16)
            placed = jnp.dot(stacked, hot, preferred_element_type=f32)
            u = pos[i, 0]
            for k in range(POL):
                for pair in range(2):
                    comp = (k % 2) * POL + pair * 2 + k // 2
                    at = (k * 2 + pair) * SG
                    for side in range(BAND_V // LANES):
                        acc[comp, side, pl.ds(u, SG), :] += placed[
                            at : at + SG, side * LANES : (side + 1) * LANES
                        ]

        return 0

    lax.fori_loop(0, slots, add, 0)
    for side in range(BAND_V // LANES):
        lanes = pl.ds(side * LANES, LANES)
        main_ref[:, :, lanes] = acc[:, side, :TILE_W, :]
        margin_ref[:, :, lanes] = acc[:, side, TILE_W:, :]


def place_all(pos, arrived):
    return pl.pallas_call(
        place_kernel,
        out_shape=(
            jax.ShapeDtypeStruct((COMPS, TILE_W, BAND_V), f32),
            jax.ShapeDtypeStruct((COMPS, SG, BAND_V), f32),
        ),
        in_specs=[smem(), vmem()],
        out_specs=(vmem(), vmem()),
        scratch_shapes=[pltpu.VMEM((COMPS, BAND_V // LANES, TILE_W + SG, LANES), f32)],
        compiler_params=pltpu.CompilerParams(vmem_limit_bytes=VMEM_LIMIT),
        name="placing",
    )(pos, arrived)


def on_device(
    visibilities, uv_rows, chan_scale, valid_rows, aterm, taper, stations, owner, u_offset, v_start
):
    groups_n = lax.axis_size("freq")
    shards_n = lax.axis_size("tile")
    devices_n = groups_n * shards_n
    me = lax.axis_index("freq")
    scale = jnp.broadcast_to(chan_scale[:, None], (chan_scale.shape[0], LANES))
    chunks = {}
    for k in list(range(groups_n - 1, 0, -1)) + [0]:
        part = images(visibilities[0], uv_rows[0], scale, me ^ k, valid_rows[0, 0])
        if k:
            part = lax.ppermute(part, "freq", [(i, i ^ k) for i in range(groups_n)])
        chunks[k] = part
    gain = gains(stations[0, 0], aterm[0], taper.reshape(1, SG * SG))
    place = jnp.concatenate([u_offset[0, 0], v_start[0, 0]], 1)
    outgoing = subgrids(
        [chunks[k] for k in range(groups_n)],
        me[None].astype(jnp.int32),
        owner[0, 0, :, 0],
        place,
        gain,
        devices_n,
    )
    arrived = lax.all_to_all(
        outgoing, ("freq", "tile"), split_axis=0, concat_axis=0, tiled=True
    )
    pos = arrived[:, CAP * SUB_ROWS : CAP * SUB_ROWS + CAP, :3].reshape(devices_n * CAP, 3)
    main, margin = place_all(pos.astype(jnp.int32), arrived)
    incoming = lax.ppermute(
        margin, ("freq", "tile"), [(i, (i + 1) % devices_n) for i in range(devices_n)]
    )
    return main.at[:, :SG, :].add(incoming)


def solution(mesh):
    in_specs = (
        P("tile", None, None, "freq"),
        P("tile", None, "freq"),
        P(),
        P("tile", "freq"),
        P("freq", None, None, None),
        P(),
        P("tile", "freq", None, None),
        P("tile", "freq", None, None),
        P("tile", "freq", None, None),
        P("tile", "freq", None, None),
    )
    out_specs = P(None, ("freq", "tile"), None)
    return jax.shard_map(
        on_device, mesh=mesh, in_specs=in_specs, out_specs=out_specs, check_vma=False
    )
```

```python
import functools
import math

import jax
import jax.numpy as jnp
import ml_dtypes
import numpy as np
from jax import lax
from jax.experimental import pallas as pl
from jax.experimental.pallas import tpu as pltpu
from jax.sharding import PartitionSpec as P

SG = 32
HALF = SG // 2
TSTEP = 128
CHAN_G = 16
FAN = CHAN_G * TSTEP
TILE_W = 256
BAND_V = 256
LANES = 128
COMPS = 8
POL = 4
POS_ROWS = 16
SUB_ROWS = 2 * SG
CAP = 2
U_STEP = SG + 3
V_STEP = 2 * SG + 1
W_STEP = CHAN_G + 1
VMEM_LIMIT = 60 << 20
f32 = jnp.float32
bf16 = jnp.bfloat16


def vmem():
    return pl.BlockSpec(memory_space=pltpu.VMEM)


def smem():
    return pl.BlockSpec(memory_space=pltpu.SMEM)


IMAGE_ROWS = np.array([HALF + i for i in range(HALF)] + [0] + [HALF - i for i in range(1, HALF)])


def split(matrix):
    high = matrix.astype(np.float32).astype(ml_dtypes.bfloat16)
    low = (matrix - high.astype(np.float64)).astype(np.float32).astype(ml_dtypes.bfloat16)
    return high, low


def fourier():
    cells = np.arange(SG) - HALF
    angles = (cells[:, None] * cells[None, :] % SG) * (2.0 * math.pi / SG)
    return np.cos(angles), -np.sin(angles)


def lane_transform():
    cos, sin = fourier()
    table = np.zeros((2, 2, 2, SG, 2, 2, 2, SG))
    for p in range(2):
        y_re = {(0, 0): cos, (1, 1): -cos, (1, 0): -sin, (0, 1): -sin}
        y_im = {(0, 0): sin, (1, 1): -sin, (1, 0): cos, (0, 1): cos}
        for gain in range(2):
            for part in range(2):
                re, im = y_re[gain, part].T, y_im[gain, part].T
                table[gain, p, part, :, 0, p, 0, :] = re
                table[gain, p, part, :, 0, p, 1, :] = im
                table[gain, p, part, :, 1, p, 0, :] = -im
                table[gain, p, part, :, 1, p, 1, :] = re
    return split(table.reshape(256, 256))


def row_transform():
    cos, sin = fourier()
    high, low = split(np.concatenate([cos[:, IMAGE_ROWS], sin[:, IMAGE_ROWS]], 1))
    return np.concatenate([high, high, low], 1)


def lane_tiles():
    table = np.zeros((POL, SG, POL, POL, SG))
    for q in range(POL):
        for copy in range(POL):
            table[q, :, q, copy, :] = np.eye(SG)
    table = table.reshape(LANES, POL * LANES)
    return np.concatenate([table] * 3, 0).astype(ml_dtypes.bfloat16)


def unit_powers(theta):
    half = theta * 0.5
    square = half * half
    sin_h = half * (
        1.0 + square * (-1.0 / 6 + square * (1.0 / 120 + square * (-1.0 / 5040 + square * (1.0 / 362880))))
    )
    cos_h = 1.0 + square * (
        -0.5 + square * (1.0 / 24 + square * (-1.0 / 720 + square * (1.0 / 40320 + square * (-1.0 / 3628800))))
    )
    powers = {0: (jnp.ones_like(theta), jnp.zeros_like(theta))}
    powers[1] = (1.0 - 2.0 * sin_h * sin_h, 2.0 * sin_h * cos_h)
    for n in range(2, HALF + 1):
        (ca, sa), (cb, sb) = powers[n // 2], powers[n - n // 2]
        if n % 2 == 0:
            powers[n] = (1.0 - 2.0 * sa * sa, 2.0 * sa * ca)
        else:
            powers[n] = (ca * cb - sa * sb, ca * sb + sa * cb)
    return powers


def image_kernel(
    scalars, vis_ref, uv_ref, scale_ref, out_ref, u_tab, v_tab, w_tab, lhs_a, lhs_b, rhs_a, rhs_b
):
    count = out_ref.shape[0]
    lane = lax.broadcasted_iota(jnp.int32, (CHAN_G, TSTEP), 1)
    out_lane = lax.broadcasted_iota(jnp.int32, (SG, LANES), 1)
    is_re = out_lane % (2 * SG) < SG
    first_row = lax.broadcasted_iota(jnp.int32, (HALF, LANES), 0) == 0

    def build(s, lhs, rhs):
        part = pl.ds(s * TSTEP, TSTEP)
        scale = scale_ref[...] * (2.0 * math.pi / SG)
        live = lane + s * TSTEP < scalars[1]
        for c in range(COMPS):
            values = vis_ref[c, :, part].astype(f32)
            w_tab[pl.ds(c * W_STEP, CHAN_G), :] = jnp.where(live, values, 0.0)
        powers = unit_powers(uv_ref[0:1, part] * scale)
        for n in range(HALF):
            u_tab[pl.ds(n, CHAN_G, U_STEP), :] = powers[n][0]
            u_tab[pl.ds(HALF + n, CHAN_G, U_STEP), :] = powers[n][1]
        u_tab[pl.ds(SG, CHAN_G, U_STEP), :] = powers[HALF][0]
        u_tab[pl.ds(SG + 1, CHAN_G, U_STEP), :] = powers[HALF][1]
        powers = unit_powers(uv_ref[1:2, part] * scale)
        for m in range(SG):
            cos, sin = powers[abs(m - HALF)]
            v_tab[pl.ds(m, CHAN_G, V_STEP), :] = cos
            v_tab[pl.ds(SG + m, CHAN_G, V_STEP), :] = sin if m >= HALF else -sin
        for h in range(CHAN_G):
            cols = pl.ds(h * TSTEP, TSTEP)
            rhs[:, cols] = v_tab[pl.ds(h * V_STEP, 2 * SG), :].astype(bf16)
            u_rows = u_tab[pl.ds(h * U_STEP, SG), :]
            for c in range(COMPS):
                lhs[c * SG : (c + 1) * SG, cols] = (u_rows * w_tab[pl.ds(c * W_STEP + h, 1), :]).astype(bf16)
            w_all = w_tab[pl.ds(h, COMPS, W_STEP), :]
            last = jnp.concatenate(
                [w_all * u_tab[pl.ds(h * U_STEP + SG, 1), :], w_all * u_tab[pl.ds(h * U_STEP + SG + 1, 1), :]], 0
            )
            lhs[COMPS * SG :, cols] = last.astype(bf16)

    def finish(s, lhs, rhs):
        sums = lax.dot_general(
            lhs[...], rhs[...], (((1,), (1,)), ((), ())), preferred_element_type=f32
        )

        def rows(c):
            return jnp.concatenate([sums[c * SG : (c + 1) * SG], sums[(c + 1) * SG : (c + 2) * SG]], 1)

        def extra(c):
            c = c + COMPS * SG
            return jnp.concatenate([sums[c : c + 1], sums[c + 1 : c + 2]], 1)

        for pair in range(2):
            x, y = rows(2 * pair), rows(POL + 2 * pair)
            xc, xs, yc, ys = x[:HALF], x[HALF:], y[:HALF], y[HALF:]
            exc, eyc = extra(2 * pair), extra(POL + 2 * pair)
            exs, eys = extra(COMPS + 2 * pair), extra(COMPS + POL + 2 * pair)
            low_re = jnp.where(first_row, exc + eys, xc + ys)
            low_im = jnp.where(first_row, eyc - exs, yc - xs)
            f_re = jnp.concatenate([xc - ys, low_re], 0)
            f_im = jnp.concatenate([yc + xs, low_im], 0)
            swapped = jnp.where(is_re, -pltpu.roll(f_im, LANES - SG, 1), pltpu.roll(f_im, SG, 1))
            out_ref[s, pair * SG : (pair + 1) * SG, :] = (f_re + swapped).astype(bf16)

    bufs = ((lhs_a, rhs_a), (lhs_b, rhs_b))
    build(0, *bufs[0])
    for s in range(count):
        if s + 1 < count:
            build(s + 1, *bufs[(s + 1) % 2])
        finish(s, *bufs[s % 2])


def images(vis, uv, scale, group, live_rows):
    rows = vis.shape[2]
    count = rows // TSTEP
    scalars = jnp.stack([group, live_rows]).astype(jnp.int32)
    return pl.pallas_call(
        image_kernel,
        out_shape=jax.ShapeDtypeStruct((count, SUB_ROWS, LANES), bf16),
        grid_spec=pltpu.PrefetchScalarGridSpec(
            num_scalar_prefetch=1,
            grid=(1,),
            in_specs=[
                pl.BlockSpec((COMPS, CHAN_G, rows), lambda i, at: (0, at[0], 0)),
                pl.BlockSpec((2, rows), lambda i, at: (0, 0)),
                pl.BlockSpec((CHAN_G, LANES), lambda i, at: (at[0], 0)),
            ],
            out_specs=pl.BlockSpec((count, SUB_ROWS, LANES), lambda i, at: (0, 0, 0)),
            scratch_shapes=[
                pltpu.VMEM((CHAN_G * U_STEP, LANES), f32),
                pltpu.VMEM((CHAN_G * V_STEP, LANES), f32),
                pltpu.VMEM((COMPS * W_STEP, LANES), f32),
                pltpu.VMEM((COMPS * SG + 16, FAN), bf16),
                pltpu.VMEM((COMPS * SG + 16, FAN), bf16),
                pltpu.VMEM((2 * SG, FAN), bf16),
                pltpu.VMEM((2 * SG, FAN), bf16),
            ],
        ),
        compiler_params=pltpu.CompilerParams(vmem_limit_bytes=VMEM_LIMIT),
        name="images",
    )(scalars, vis, uv, scale)


def gain_kernel(stations, aterm, taper, tiles, out_ref, rows, sems):
    count = rows.shape[0] // 2

    def copy(i):
        return pltpu.make_async_copy(
            aterm.at[stations[i % count, i // count]], rows.at[i], sems.at[i]
        )

    def start(i, _):
        copy(i).start()
        return 0

    def wait(i, _):
        copy(i).wait()
        return 0

    lax.fori_loop(0, 2 * count, start, 0)
    lax.fori_loop(0, 2 * count, wait, 0)
    for r in range(SG * SG // LANES):
        cols = pl.ds(r * LANES, LANES)
        one_re, one_im = rows[0:count, 0, cols], rows[0:count, 1, cols]
        two_re, two_im = rows[count:, 0, cols], rows[count:, 1, cols]
        shape = taper[0:1, cols] * (1.0 / (math.sqrt(FAN) * SG))
        gain = jnp.concatenate(
            [(one_re * two_re + one_im * two_im) * shape, (one_im * two_re - one_re * two_im) * shape], 0
        )
        high = gain.astype(bf16)
        rest = gain - high.astype(f32)
        mid = rest.astype(bf16)
        low = (rest - mid.astype(f32)).astype(bf16)
        tiled = jnp.dot(
            jnp.concatenate([high, mid, low], 1), tiles[...], preferred_element_type=f32
        )
        for q in range(POL):
            row = list(IMAGE_ROWS).index(POL * r + q)
            lanes = tiled[:, q * LANES : (q + 1) * LANES]
            out_ref[0, row] = lanes[:count]
            out_ref[1, row] = lanes[count:]


def gains(stations, aterm, taper):
    count = stations.shape[0]
    return pl.pallas_call(
        gain_kernel,
        out_shape=jax.ShapeDtypeStruct((2, SG, count, LANES), f32),
        in_specs=[smem(), pl.BlockSpec(memory_space=pl.ANY), vmem(), vmem()],
        out_specs=vmem(),
        scratch_shapes=[
            pltpu.VMEM((2 * count, 2, SG * SG), f32),
            pltpu.SemaphoreType.DMA((2 * count,)),
        ],
        compiler_params=pltpu.CompilerParams(vmem_limit_bytes=VMEM_LIMIT),
        name="gains",
    )(stations, aterm, taper, lane_tiles())


def subgrid_kernel(
    chunks_n, mine, owner, place, gain, w_high, w_low, f_rows, *refs
):
    chunks = refs[:chunks_n]
    out_ref, d_high, d_low, y_ref, pos, taken = refs[chunks_n:]
    block = chunks[0].shape[0]
    lane = lax.broadcasted_iota(jnp.int32, (1, LANES), 1)

    def clear(i, _):
        taken[i] = 0
        return 0

    lax.fori_loop(0, taken.shape[0], clear, 0)
    pos[...] = jnp.zeros_like(pos)
    for k in range(chunks_n):
        base = (mine[0] ^ k) * block

        def shape(i, _):
            gain_re, gain_im = gain[0, :, base + i, :], gain[1, :, base + i, :]
            for pair in range(2):
                image = chunks[k][i, pair * SG : (pair + 1) * SG, :].astype(f32)
                both = jnp.concatenate([image * gain_re, image * gain_im], 1)
                high = both.astype(bf16)
                at = pl.ds(pl.multiple_of(((k * block + i) * 2 + pair) * SG, SG), SG)
                d_high[at, :] = high
                d_low[at, :] = (both - high.astype(f32)).astype(bf16)
            return 0

        lax.fori_loop(0, block, shape, 0, unroll=2)
    step = 512
    for i in range(d_high.shape[0] // step):
        at = pl.ds(i * step, step)
        high = d_high[at, :]
        y_ref[at, :] = (
            jnp.dot(high, w_high[...], preferred_element_type=f32)
            + jnp.dot(d_low[at, :], w_high[...], preferred_element_type=f32)
            + jnp.dot(high, w_low[...], preferred_element_type=f32)
        )
    for k in range(chunks_n):
        base = (mine[0] ^ k) * block

        def transform(i, _):
            at = pl.multiple_of((k * block + i) * 2 * SG, 2 * SG)
            one, two = y_ref[pl.ds(at, SG), :], y_ref[pl.ds(at + SG, SG), :]
            rows = jnp.concatenate(
                [
                    jnp.concatenate([one[:, :LANES], two[:, :LANES]], 1),
                    jnp.concatenate([one[:, LANES:], two[:, LANES:]], 1),
                ],
                0,
            )
            high = rows.astype(bf16)
            low = (rows - high.astype(f32)).astype(bf16)
            cells = jnp.dot(
                f_rows[...], jnp.concatenate([high, low, high], 0), preferred_element_type=f32
            ).astype(bf16)
            s = base + i
            dest = owner[s]
            slot = taken[dest]
            taken[dest] = slot + 1
            slot = jnp.minimum(slot, CAP - 1)
            start = pl.multiple_of(slot * SUB_ROWS, SUB_ROWS)
            out_ref[dest, pl.ds(start, SG), :] = cells[:, :LANES]
            out_ref[dest, pl.ds(start + SG, SG), :] = cells[:, LANES:]
            row = jnp.where(lane == 0, place[s, 0], jnp.where(lane == 1, place[s, 1], 1))
            pos[dest, pl.ds(slot, 1), :] = row.astype(f32)
            return 0

        lax.fori_loop(0, block, transform, 0, unroll=2)
    out_ref[:, CAP * SUB_ROWS :, :] = pos[...].astype(bf16)


def subgrids(chunks, mine, owner, place, gain, devices_n):
    count = owner.shape[0]
    return pl.pallas_call(
        functools.partial(subgrid_kernel, len(chunks)),
        out_shape=jax.ShapeDtypeStruct((devices_n, CAP * SUB_ROWS + POS_ROWS, LANES), bf16),
        in_specs=[smem()] * 3 + [vmem()] * (4 + len(chunks)),
        out_specs=vmem(),
        scratch_shapes=[
            pltpu.VMEM((count * 2 * SG, 2 * LANES), bf16),
            pltpu.VMEM((count * 2 * SG, 2 * LANES), bf16),
            pltpu.VMEM((count * 2 * SG, 2 * LANES), f32),
            pltpu.VMEM((devices_n, POS_ROWS, LANES), f32),
            pltpu.SMEM((devices_n,), jnp.int32),
        ],
        compiler_params=pltpu.CompilerParams(vmem_limit_bytes=VMEM_LIMIT),
        name="subgrids",
    )(mine, owner, place, gain, *lane_transform(), row_transform(), *chunks)


def place_kernel(margin, pos, arrived, out_ref, acc):
    slots = arrived.shape[0] * CAP
    first = TILE_W - SG if margin else 0
    acc[...] = jnp.zeros_like(acc)
    columns = lax.broadcasted_iota(jnp.int32, (SG, BAND_V), 1) - lax.broadcasted_iota(
        jnp.int32, (SG, BAND_V), 0
    )

    def add(i, _):
        u = pos[i, 0]

        @pl.when((pos[i, 2] > 0) & (u > first if margin else True))
        def _():
            source, slot = i // CAP, i % CAP
            start = pl.multiple_of(slot * SUB_ROWS, SUB_ROWS)
            cells = arrived[source, pl.ds(start, SUB_ROWS), :]
            stacked = jnp.concatenate([cells[:, SG * k : SG * (k + 1)] for k in range(POL)], 0)
            hot = jnp.where(columns == pos[i, 1], 1.0, 0.0).astype(bf16)
            placed = jnp.dot(stacked, hot, preferred_element_type=f32)
            for k in range(POL):
                for pair in range(2):
                    comp = (k % 2) * POL + pair * 2 + k // 2
                    at = (k * 2 + pair) * SG
                    for side in range(BAND_V // LANES):
                        acc[comp, side, pl.ds(u - first, SG), :] += placed[
                            at : at + SG, side * LANES : (side + 1) * LANES
                        ]

        return 0

    lax.fori_loop(0, slots, add, 0)
    rows = pl.ds(SG, SG) if margin else pl.ds(0, TILE_W)
    for side in range(BAND_V // LANES):
        lanes = pl.ds(side * LANES, LANES)
        out_ref[:, :, lanes] = acc[:, side, rows, :].astype(out_ref.dtype)


def placed(pos, arrived, margin):
    return pl.pallas_call(
        functools.partial(place_kernel, margin),
        out_shape=jax.ShapeDtypeStruct(
            (COMPS, SG if margin else TILE_W, BAND_V), bf16 if margin else f32
        ),
        in_specs=[smem(), vmem()],
        out_specs=vmem(),
        scratch_shapes=[
            pltpu.VMEM((COMPS, BAND_V // LANES, (SG if margin else TILE_W) + SG, LANES), f32)
        ],
        compiler_params=pltpu.CompilerParams(vmem_limit_bytes=VMEM_LIMIT),
        cost_estimate=pl.CostEstimate(flops=10**9, bytes_accessed=4 << 20, transcendentals=0),
        name="margin" if margin else "tile",
    )(pos, arrived)


def on_device(
    visibilities, uv_rows, chan_scale, valid_rows, aterm, taper, stations, owner, u_offset, v_start
):
    groups_n = lax.axis_size("freq")
    shards_n = lax.axis_size("tile")
    devices_n = groups_n * shards_n
    me = lax.axis_index("freq")
    scale = jnp.broadcast_to(chan_scale[:, None], (chan_scale.shape[0], LANES))
    chunks = {}
    for k in list(range(groups_n - 1, 0, -1)) + [0]:
        part = images(visibilities[0], uv_rows[0], scale, me ^ k, valid_rows[0, 0])
        if k:
            part = lax.ppermute(part, "freq", [(i, i ^ k) for i in range(groups_n)])
        chunks[k] = part
    gain = gains(stations[0, 0], aterm[0], taper.reshape(1, SG * SG))
    place = jnp.concatenate([u_offset[0, 0], v_start[0, 0]], 1)
    outgoing = subgrids(
        [chunks[k] for k in range(groups_n)],
        me[None].astype(jnp.int32),
        owner[0, 0, :, 0],
        place,
        gain,
        devices_n,
    )
    arrived = lax.all_to_all(
        outgoing, ("freq", "tile"), split_axis=0, concat_axis=0, tiled=True
    )
    pos = arrived[:, CAP * SUB_ROWS : CAP * SUB_ROWS + CAP, :3].reshape(devices_n * CAP, 3)
    pos = pos.astype(jnp.int32)
    incoming = lax.ppermute(
        placed(pos, arrived, True),
        ("freq", "tile"),
        [(i, (i + 1) % devices_n) for i in range(devices_n)],
    )
    return placed(pos, arrived, False).at[:, :SG, :].add(incoming.astype(f32))


def solution(mesh):
    in_specs = (
        P("tile", None, None, "freq"),
        P("tile", None, "freq"),
        P(),
        P("tile", "freq"),
        P("freq", None, None, None),
        P(),
        P("tile", "freq", None, None),
        P("tile", "freq", None, None),
        P("tile", "freq", None, None),
        P("tile", "freq", None, None),
    )
    out_specs = P(None, ("freq", "tile"), None)
    return jax.shard_map(
        on_device, mesh=mesh, in_specs=in_specs, out_specs=out_specs, check_vma=False
    )
```

```python
import functools
import math

import jax
import jax.numpy as jnp
import ml_dtypes
import numpy as np
from jax import lax
from jax.experimental import pallas as pl
from jax.experimental.pallas import tpu as pltpu
from jax.sharding import PartitionSpec as P

SG = 32
HALF = SG // 2
TSTEP = 128
CHAN_G = 16
FAN = CHAN_G * TSTEP
TILE_W = 256
BAND_V = 256
LANES = 128
COMPS = 8
POL = 4
POS_ROWS = 16
CAP = 2
U_STEP = SG + 3
V_STEP = 2 * SG + 1
W_STEP = CHAN_G + 1
VMEM_LIMIT = 60 << 20
f32 = jnp.float32
bf16 = jnp.bfloat16


def vmem():
    return pl.BlockSpec(memory_space=pltpu.VMEM)


def smem():
    return pl.BlockSpec(memory_space=pltpu.SMEM)


IMAGE_ROWS = np.array([HALF + i for i in range(HALF)] + [0] + [HALF - i for i in range(1, HALF)])


def split(matrix):
    high = matrix.astype(np.float32).astype(ml_dtypes.bfloat16)
    low = (matrix - high.astype(np.float64)).astype(np.float32).astype(ml_dtypes.bfloat16)
    return high, low


def fourier():
    cells = np.arange(SG) - HALF
    angles = (cells[:, None] * cells[None, :] % SG) * (2.0 * math.pi / SG)
    return np.cos(angles), -np.sin(angles)


def lane_transform():
    cos, sin = fourier()
    table = np.zeros((2, 2, 2, SG, 2, 2, 2, SG))
    for p in range(2):
        y_re = {(0, 0): cos, (1, 1): -cos, (1, 0): -sin, (0, 1): -sin}
        y_im = {(0, 0): sin, (1, 1): -sin, (1, 0): cos, (0, 1): cos}
        for gain in range(2):
            for part in range(2):
                re, im = y_re[gain, part].T, y_im[gain, part].T
                table[gain, p, part, :, 0, p, 0, :] = re
                table[gain, p, part, :, 0, p, 1, :] = im
                table[gain, p, part, :, 1, p, 0, :] = -im
                table[gain, p, part, :, 1, p, 1, :] = re
    return split(table.reshape(256, 256))


def row_transform():
    cos, sin = fourier()
    high, low = split(np.concatenate([cos[:, IMAGE_ROWS], sin[:, IMAGE_ROWS]], 1))
    return np.concatenate([high, high, low], 1)


def lane_tiles():
    table = np.zeros((POL, SG, POL, POL, SG))
    for q in range(POL):
        for copy in range(POL):
            table[q, :, q, copy, :] = np.eye(SG)
    table = table.reshape(LANES, POL * LANES)
    return np.concatenate([table] * 3, 0).astype(ml_dtypes.bfloat16)


def unit_powers(theta):
    half = theta * 0.5
    square = half * half
    sin_h = half * (
        1.0 + square * (-1.0 / 6 + square * (1.0 / 120 + square * (-1.0 / 5040 + square * (1.0 / 362880))))
    )
    cos_h = 1.0 + square * (
        -0.5 + square * (1.0 / 24 + square * (-1.0 / 720 + square * (1.0 / 40320 + square * (-1.0 / 3628800))))
    )
    powers = {0: (jnp.ones_like(theta), jnp.zeros_like(theta))}
    powers[1] = (1.0 - 2.0 * sin_h * sin_h, 2.0 * sin_h * cos_h)
    for n in range(2, HALF + 1):
        (ca, sa), (cb, sb) = powers[n // 2], powers[n - n // 2]
        if n % 2 == 0:
            powers[n] = (1.0 - 2.0 * sa * sa, 2.0 * sa * ca)
        else:
            powers[n] = (ca * cb - sa * sb, ca * sb + sa * cb)
    return powers


PAIRS = 2
PAIR_COMPS = 4


def image_kernel(pair, ks, me, valid, scales, *refs):
    blocks, uv_ref, outs = refs[: len(ks)], refs[len(ks)], refs[len(ks) + 1 : 2 * len(ks) + 1]
    u_tab, v_tab, w_tab, scale_tab = refs[2 * len(ks) + 1 :]
    lane = lax.broadcasted_iota(jnp.int32, (CHAN_G, TSTEP), 1)
    out_lane = lax.broadcasted_iota(jnp.int32, (SG, LANES), 1)
    is_re = out_lane % (2 * SG) < SG
    first_row = lax.broadcasted_iota(jnp.int32, (HALF, LANES), 0) == 0

    def build(vis_ref, s, scale):
        part = pl.ds(s * TSTEP, TSTEP)
        live = lane + s * TSTEP < valid[0, 0]
        for c in range(PAIR_COMPS):
            values = vis_ref[c // 2, c % 2, :, part].astype(f32)
            w_tab[pl.ds(c * W_STEP, CHAN_G), :] = jnp.where(live, values, 0.0)
        powers = unit_powers(uv_ref[0, 0:1, part] * scale)
        for n in range(HALF):
            u_tab[pl.ds(n, CHAN_G, U_STEP), :] = powers[n][0]
            u_tab[pl.ds(HALF + n, CHAN_G, U_STEP), :] = powers[n][1]
        u_tab[pl.ds(SG, CHAN_G, U_STEP), :] = powers[HALF][0]
        u_tab[pl.ds(SG + 1, CHAN_G, U_STEP), :] = powers[HALF][1]
        powers = unit_powers(uv_ref[0, 1:2, part] * scale)
        for m in range(SG):
            cos, sin = powers[abs(m - HALF)]
            v_tab[pl.ds(m, CHAN_G, V_STEP), :] = cos
            v_tab[pl.ds(SG + m, CHAN_G, V_STEP), :] = sin if m >= HALF else -sin
        sums = None
        step = 4
        for start in range(0, CHAN_G, step):
            left, right = [], []
            for h in range(start, start + step):
                right.append(v_tab[pl.ds(h * V_STEP, 2 * SG), :].astype(bf16))
                u_rows = u_tab[pl.ds(h * U_STEP, SG), :]
                column = [
                    (u_rows * w_tab[pl.ds(c * W_STEP + h, 1), :]).astype(bf16)
                    for c in range(PAIR_COMPS)
                ]
                w_all = w_tab[pl.ds(h, PAIR_COMPS, W_STEP), :]
                last = [w_all * u_tab[pl.ds(h * U_STEP + SG + i, 1), :] for i in range(2)]
                pad = jnp.zeros((2 * PAIR_COMPS, TSTEP), f32)
                column.append(jnp.concatenate(last + [pad], 0).astype(bf16))
                left.append(jnp.concatenate(column, 0))
            term = lax.dot_general(
                jnp.concatenate(left, 1),
                jnp.concatenate(right, 1),
                (((1,), (1,)), ((), ())),
                preferred_element_type=f32,
            )
            sums = term if sums is None else sums + term
        return sums

    def finish(out_ref, s, sums):
        def rows(part):
            at = part * 2 * SG
            return jnp.concatenate([sums[at : at + SG], sums[at + SG : at + 2 * SG]], 1)

        def extra(sine, part):
            at = PAIR_COMPS * SG + PAIR_COMPS * sine + 2 * part
            return jnp.concatenate([sums[at : at + 1], sums[at + 1 : at + 2]], 1)

        x, y = rows(0), rows(1)
        xc, xs, yc, ys = x[:HALF], x[HALF:], y[:HALF], y[HALF:]
        low_re = jnp.where(first_row, extra(0, 0) + extra(1, 1), xc + ys)
        low_im = jnp.where(first_row, extra(0, 1) - extra(1, 0), yc - xs)
        f_re = jnp.concatenate([xc - ys, low_re], 0)
        f_im = jnp.concatenate([yc + xs, low_im], 0)
        swapped = jnp.where(is_re, -pltpu.roll(f_im, LANES - SG, 1), pltpu.roll(f_im, SG, 1))
        out_ref[s] = (f_re + swapped).astype(bf16)

    for i, k in enumerate(ks):
        group = me[0] ^ k
        for h in range(CHAN_G):
            scale_tab[h : h + 1, :] = jnp.full((1, LANES), scales[group * CHAN_G + h], f32)
        scale = scale_tab[...] * (2.0 * math.pi / SG)
        for s in range(outs[i].shape[0]):
            finish(outs[i], s, build(blocks[i], s, scale))


def images(pair, ks, me, valid, scales, vis, uv):
    rows = vis.shape[3]
    count = rows // TSTEP
    block = (2, 2, CHAN_G, rows)
    whole = pl.BlockSpec((count, SG, LANES), lambda i, at: (0, 0, 0))
    return pl.pallas_call(
        functools.partial(image_kernel, pair, ks),
        out_shape=[jax.ShapeDtypeStruct((count, SG, LANES), bf16)] * len(ks),
        grid_spec=pltpu.PrefetchScalarGridSpec(
            num_scalar_prefetch=1,
            grid=(1,),
            in_specs=[smem(), smem()]
            + [pl.BlockSpec(block, lambda i, at, k=k: (0, pair, at[0] ^ k, 0)) for k in ks]
            + [pl.BlockSpec((1, 2, rows), lambda i, at: (0, 0, 0))],
            out_specs=[whole] * len(ks),
            scratch_shapes=[
                pltpu.VMEM((CHAN_G * U_STEP, LANES), f32),
                pltpu.VMEM((CHAN_G * V_STEP, LANES), f32),
                pltpu.VMEM((PAIR_COMPS * W_STEP, LANES), f32),
                pltpu.VMEM((CHAN_G, LANES), f32),
            ],
        ),
        compiler_params=pltpu.CompilerParams(vmem_limit_bytes=VMEM_LIMIT),
        cost_estimate=pl.CostEstimate(
            flops=len(ks) * count * FAN * 40000, bytes_accessed=1 << 20, transcendentals=0
        ),
        name="images",
    )(me, valid, scales, *([vis] * len(ks)), uv)


def gain_kernel(stations, aterm, taper, tiles, out_ref, rows, sems):
    count = rows.shape[0] // 2

    def copy(i):
        return pltpu.make_async_copy(
            aterm.at[0, stations[0, 0, i % count, i // count]], rows.at[i], sems.at[i]
        )

    def start(i, _):
        copy(i).start()
        return 0

    def wait(i, _):
        copy(i).wait()
        return 0

    lax.fori_loop(0, 2 * count, start, 0, unroll=8)
    lax.fori_loop(0, 2 * count, wait, 0, unroll=8)
    for r in range(SG * SG // LANES):
        cols = pl.ds(r * LANES, LANES)
        one_re, one_im = rows[0:count, 0, cols], rows[0:count, 1, cols]
        two_re, two_im = rows[count:, 0, cols], rows[count:, 1, cols]
        shape = jnp.concatenate(
            [taper[POL * r + q : POL * r + q + 1, :] for q in range(POL)], 1
        ) * (1.0 / (math.sqrt(FAN) * SG))
        gain = jnp.concatenate(
            [(one_re * two_re + one_im * two_im) * shape, (one_im * two_re - one_re * two_im) * shape], 0
        )
        high = gain.astype(bf16)
        rest = gain - high.astype(f32)
        mid = rest.astype(bf16)
        low = (rest - mid.astype(f32)).astype(bf16)
        tiled = jnp.dot(
            jnp.concatenate([high, mid, low], 1), tiles[...], preferred_element_type=f32
        )
        for q in range(POL):
            row = list(IMAGE_ROWS).index(POL * r + q)
            lanes = tiled[:, q * LANES : (q + 1) * LANES]
            out_ref[0, row] = lanes[:count]
            out_ref[1, row] = lanes[count:]


def gains(stations, aterm, taper):
    count = stations.shape[2]
    return pl.pallas_call(
        gain_kernel,
        out_shape=jax.ShapeDtypeStruct((2, SG, count, LANES), f32),
        in_specs=[smem(), pl.BlockSpec(memory_space=pl.ANY), vmem(), vmem()],
        out_specs=vmem(),
        scratch_shapes=[
            pltpu.VMEM((2 * count, 2, SG * SG), f32),
            pltpu.SemaphoreType.DMA((2 * count,)),
        ],
        compiler_params=pltpu.CompilerParams(vmem_limit_bytes=VMEM_LIMIT),
        name="gains",
    )(stations, aterm, taper, lane_tiles())


def subgrid_kernel(chunks_n, me, owner, u_offset, v_start, gain, w_high, w_low, f_rows, *refs):
    chunks = refs[:chunks_n]
    out_ref, d_high, d_low, y_ref, pos, taken = refs[chunks_n:]
    block = chunks[0].shape[0]
    with_places = out_ref.shape[1] > CAP * SG
    lane = lax.broadcasted_iota(jnp.int32, (1, LANES), 1)

    def clear(i, _):
        taken[i] = 0
        return 0

    lax.fori_loop(0, taken.shape[0], clear, 0, unroll=8)
    if with_places:
        pos[...] = jnp.zeros_like(pos)
    for k in range(chunks_n):
        base = (me[0] ^ k) * block
        for i in range(block):
            image = chunks[k][i].astype(f32)
            both = jnp.concatenate([image * gain[0, :, base + i, :], image * gain[1, :, base + i, :]], 1)
            high = both.astype(bf16)
            at = pl.ds((k * block + i) * SG, SG)
            d_high[at, :] = high
            d_low[at, :] = (both - high.astype(f32)).astype(bf16)
    step = 256
    for i in range(d_high.shape[0] // step):
        at = pl.ds(i * step, step)
        high = d_high[at, :]
        y_ref[at, :] = (
            jnp.dot(high, w_high[...], preferred_element_type=f32)
            + jnp.dot(d_low[at, :], w_high[...], preferred_element_type=f32)
            + jnp.dot(high, w_low[...], preferred_element_type=f32)
        )
    for k in range(chunks_n):
        base = (me[0] ^ k) * block
        for i in range(0, block, 2):
            ys = [y_ref[pl.ds((k * block + i + j) * SG, SG), :] for j in range(2)]
            rows = jnp.concatenate(
                [
                    jnp.concatenate([y[:, :LANES] for y in ys], 1),
                    jnp.concatenate([y[:, LANES:] for y in ys], 1),
                ],
                0,
            )
            high = rows.astype(bf16)
            low = (rows - high.astype(f32)).astype(bf16)
            cells = jnp.dot(
                f_rows[...], jnp.concatenate([high, low, high], 0), preferred_element_type=f32
            ).astype(bf16)
            for j in range(2):
                s = base + i + j
                dest = owner[0, 0, s, 0]
                slot = jnp.minimum(taken[dest], CAP - 1)
                taken[dest] = slot + 1
                at = pl.multiple_of(slot * SG, SG)
                out_ref[dest, pl.ds(at, SG), :] = cells[:, j * LANES : (j + 1) * LANES]
                if with_places:
                    u, v = u_offset[0, 0, s, 0], v_start[0, 0, s, 0]
                    row = jnp.where(lane == 0, u, jnp.where(lane == 1, v, 1))
                    pos[dest, pl.ds(slot, 1), :] = row.astype(f32)
    if with_places:
        out_ref[:, CAP * SG :, :] = pos[...].astype(bf16)


def subgrids(with_places, chunks, me, owner, u_offset, v_start, gain, devices_n):
    count = owner.shape[2]
    rows = CAP * SG + (POS_ROWS if with_places else 0)
    return pl.pallas_call(
        functools.partial(subgrid_kernel, len(chunks)),
        out_shape=jax.ShapeDtypeStruct((devices_n, rows, LANES), bf16),
        in_specs=[smem()] * 4 + [vmem()] * (4 + len(chunks)),
        out_specs=vmem(),
        scratch_shapes=[
            pltpu.VMEM((count * SG, 2 * LANES), bf16),
            pltpu.VMEM((count * SG, 2 * LANES), bf16),
            pltpu.VMEM((count * SG, 2 * LANES), f32),
            pltpu.VMEM((devices_n, POS_ROWS, LANES), f32),
            pltpu.SMEM((devices_n,), jnp.int32),
        ],
        compiler_params=pltpu.CompilerParams(vmem_limit_bytes=VMEM_LIMIT),
        cost_estimate=pl.CostEstimate(flops=4 * 10**9, bytes_accessed=4 << 20, transcendentals=0),
        name="subgrids",
    )(me, owner, u_offset, v_start, gain, *lane_transform(), row_transform(), *chunks)


def place_kernel(margin, pair, pos, arrived, *refs):
    out_ref, acc = refs[-2:]
    slots = arrived.shape[0] * CAP
    first = TILE_W - SG if margin else 0
    acc[...] = jnp.zeros_like(acc)
    columns = lax.broadcasted_iota(jnp.int32, (SG, BAND_V), 1) - lax.broadcasted_iota(
        jnp.int32, (SG, BAND_V), 0
    )

    def add(i, _):
        u = pos[i, 0]

        @pl.when((pos[i, 2] > 0) & (u > first if margin else True))
        def _():
            source, slot = i // CAP, i % CAP
            cells = arrived[source, pl.ds(pl.multiple_of(slot * SG, SG), SG), :]
            stacked = jnp.concatenate([cells[:, SG * k : SG * (k + 1)] for k in range(PAIR_COMPS)], 0)
            hot = jnp.where(columns == pos[i, 1], 1.0, 0.0).astype(bf16)
            spread = jnp.dot(stacked, hot, preferred_element_type=f32)
            for k in range(PAIR_COMPS):
                for side in range(BAND_V // LANES):
                    acc[k, side, pl.ds(u - first, SG), :] += spread[
                        k * SG : (k + 1) * SG, side * LANES : (side + 1) * LANES
                    ]

        return 0

    lax.fori_loop(0, slots, add, 0)
    rows = pl.ds(SG, SG) if margin else pl.ds(0, TILE_W)
    for k in range(PAIR_COMPS):
        for side in range(BAND_V // LANES):
            lanes = pl.ds(side * LANES, LANES)
            out_ref[k % 2, 0, k // 2, :, lanes] = acc[k, side, rows, :].astype(out_ref.dtype)


def placed(margin, pair, pos, arrived, total=None):
    columns = SG if margin else TILE_W
    pairs = 1 if margin else PAIRS
    block = (2, 1, 2, columns, BAND_V)
    more = [] if total is None else [total]
    return pl.pallas_call(
        functools.partial(place_kernel, margin, pair),
        out_shape=jax.ShapeDtypeStruct((2, pairs, 2, columns, BAND_V), bf16 if margin else f32),
        grid=(1,),
        in_specs=[smem(), pl.BlockSpec(arrived.shape, lambda i: (0, 0, 0))]
        + [pl.BlockSpec(memory_space=pl.ANY)] * len(more),
        out_specs=pl.BlockSpec(block, lambda i: (0, 0 if margin else pair, 0, 0, 0)),
        scratch_shapes=[pltpu.VMEM((PAIR_COMPS, BAND_V // LANES, columns + SG, LANES), f32)],
        input_output_aliases={2: 0} if more else {},
        compiler_params=pltpu.CompilerParams(vmem_limit_bytes=VMEM_LIMIT),
        cost_estimate=pl.CostEstimate(flops=10**9, bytes_accessed=4 << 20, transcendentals=0),
        name="margin" if margin else "tile",
    )(pos, arrived, *more)


def on_device(
    visibilities, uv_rows, chan_scale, valid_rows, aterm, taper, stations, owner, u_offset, v_start
):
    groups_n = lax.axis_size("freq")
    devices_n = groups_n * lax.axis_size("tile")
    me = lax.axis_index("freq")[None].astype(jnp.int32)
    vis = visibilities.reshape((2, POL) + visibilities.shape[2:])
    far = list(range(groups_n - 1, 1, -1))
    near = [k for k in (1, 0) if k < groups_n]

    def make_images(pair, vis):
        chunks = {}
        for ks in (far, near):
            if ks:
                parts = images(pair, ks, me, valid_rows, chan_scale, vis, uv_rows)
                for k, part in zip(ks, parts):
                    if k:
                        part = lax.ppermute(part, "freq", [(i, i ^ k) for i in range(groups_n)])
                    chunks[k] = part
        return [chunks[k] for k in range(groups_n)]

    def send(pair, chunks, gain):
        outgoing = subgrids(pair == 0, chunks, me, owner, u_offset, v_start, gain, devices_n)
        arrived = lax.all_to_all(
            outgoing, ("freq", "tile"), split_axis=0, concat_axis=0, tiled=True
        )
        return outgoing, arrived

    def send_margin(pair, pos, arrived):
        return lax.ppermute(
            placed(True, pair, pos, arrived),
            ("freq", "tile"),
            [(i, (i + 1) % devices_n) for i in range(devices_n)],
        )

    chunks = make_images(0, vis)
    gain = gains(stations, aterm, taper)
    outgoing, first = send(0, chunks, gain)
    vis, _ = lax.optimization_barrier((vis, outgoing))
    _, second = send(1, make_images(1, vis), gain)
    pos = first[:, CAP * SG : CAP * SG + CAP, :3].reshape(devices_n * CAP, 3).astype(jnp.int32)
    margins = [send_margin(0, pos, first)]
    tile = placed(False, 0, pos, first)
    margins.append(send_margin(1, pos, second))
    tile = placed(False, 1, pos, second, tile)
    incoming = jnp.concatenate(margins, 1).astype(f32)
    return tile.at[:, :, :, :SG, :].add(incoming).reshape(COMPS, TILE_W, BAND_V)


def solution(mesh):
    in_specs = (
        P("tile", None, None, "freq"),
        P("tile", None, "freq"),
        P(),
        P("tile", "freq"),
        P("freq", None, None, None),
        P(),
        P("tile", "freq", None, None),
        P("tile", "freq", None, None),
        P("tile", "freq", None, None),
        P("tile", "freq", None, None),
    )
    out_specs = P(None, ("freq", "tile"), None)
    return jax.shard_map(
        on_device, mesh=mesh, in_specs=in_specs, out_specs=out_specs, check_vma=False
    )
```

```python
import functools
import math

import jax
import jax.numpy as jnp
import ml_dtypes
import numpy as np
from jax import lax
from jax.experimental import pallas as pl
from jax.experimental.pallas import tpu as pltpu
from jax.sharding import PartitionSpec as P

SG = 32
HALF = SG // 2
TSTEP = 128
CHAN_G = 16
FAN = CHAN_G * TSTEP
TILE_W = 256
BAND_V = 256
LANES = 128
COMPS = 8
POL = 4
POS_ROWS = 8
NO_PLACE = 512.0
CAP = 2
U_STEP = SG + 3
V_STEP = 2 * SG + 1
W_STEP = CHAN_G + 1
VMEM_LIMIT = 60 << 20
f32 = jnp.float32
bf16 = jnp.bfloat16


def vmem():
    return pl.BlockSpec(memory_space=pltpu.VMEM)


def smem():
    return pl.BlockSpec(memory_space=pltpu.SMEM)


IMAGE_ROWS = np.array([HALF + i for i in range(HALF)] + [0] + [HALF - i for i in range(1, HALF)])


def split(matrix):
    high = matrix.astype(np.float32).astype(ml_dtypes.bfloat16)
    low = (matrix - high.astype(np.float64)).astype(np.float32).astype(ml_dtypes.bfloat16)
    return high, low


def fourier():
    cells = np.arange(SG) - HALF
    angles = (cells[:, None] * cells[None, :] % SG) * (2.0 * math.pi / SG)
    return np.cos(angles), -np.sin(angles)


def lane_transform():
    cos, sin = fourier()
    table = np.zeros((2, 2, 2, SG, 2, 2, 2, SG))
    for p in range(2):
        y_re = {(0, 0): cos, (1, 1): -cos, (1, 0): -sin, (0, 1): -sin}
        y_im = {(0, 0): sin, (1, 1): -sin, (1, 0): cos, (0, 1): cos}
        for gain in range(2):
            for part in range(2):
                re, im = y_re[gain, part].T, y_im[gain, part].T
                table[gain, p, part, :, 0, p, 0, :] = re
                table[gain, p, part, :, 0, p, 1, :] = im
                table[gain, p, part, :, 1, p, 0, :] = -im
                table[gain, p, part, :, 1, p, 1, :] = re
    return split(table.reshape(256, 256))


def row_transform():
    cos, sin = fourier()
    high, low = split(np.concatenate([cos[:, IMAGE_ROWS], sin[:, IMAGE_ROWS]], 1))
    return np.concatenate([high, high, low], 1)


def lane_tiles():
    table = np.zeros((POL, SG, POL, POL, SG))
    for q in range(POL):
        for copy in range(POL):
            table[q, :, q, copy, :] = np.eye(SG)
    table = table.reshape(LANES, POL * LANES)
    return np.concatenate([table] * 3, 0).astype(ml_dtypes.bfloat16)


def unit_powers(theta):
    half = theta * 0.5
    square = half * half
    sin_h = half * (
        1.0 + square * (-1.0 / 6 + square * (1.0 / 120 + square * (-1.0 / 5040 + square * (1.0 / 362880))))
    )
    cos_h = 1.0 + square * (
        -0.5 + square * (1.0 / 24 + square * (-1.0 / 720 + square * (1.0 / 40320 + square * (-1.0 / 3628800))))
    )
    powers = {0: (jnp.ones_like(theta), jnp.zeros_like(theta))}
    powers[1] = (1.0 - 2.0 * sin_h * sin_h, 2.0 * sin_h * cos_h)
    for n in range(2, HALF + 1):
        (ca, sa), (cb, sb) = powers[n // 2], powers[n - n // 2]
        if n % 2 == 0:
            powers[n] = (1.0 - 2.0 * sa * sa, 2.0 * sa * ca)
        else:
            powers[n] = (ca * cb - sa * sb, ca * sb + sa * cb)
    return powers


def image_kernel(ks, me, valid, scales, *refs):
    blocks, uv_ref, outs = refs[: len(ks)], refs[len(ks)], refs[len(ks) + 1 : 2 * len(ks) + 1]
    u_tab, v_tab, w_tab, scale_tab = refs[2 * len(ks) + 1 :]
    lane = lax.broadcasted_iota(jnp.int32, (CHAN_G, TSTEP), 1)
    out_lane = lax.broadcasted_iota(jnp.int32, (SG, LANES), 1)
    is_re = out_lane % (2 * SG) < SG
    first_row = lax.broadcasted_iota(jnp.int32, (HALF, LANES), 0) == 0

    def build(vis_ref, s, scale):
        part = pl.ds(s * TSTEP, TSTEP)
        live = lane + s * TSTEP < valid[0, 0]
        for c in range(COMPS):
            values = vis_ref[c, :, part].astype(f32)
            w_tab[pl.ds(c * W_STEP, CHAN_G), :] = jnp.where(live, values, 0.0)
        powers = unit_powers(uv_ref[0, 0:1, part] * scale)
        for n in range(HALF):
            u_tab[pl.ds(n, CHAN_G, U_STEP), :] = powers[n][0]
            u_tab[pl.ds(HALF + n, CHAN_G, U_STEP), :] = powers[n][1]
        u_tab[pl.ds(SG, CHAN_G, U_STEP), :] = powers[HALF][0]
        u_tab[pl.ds(SG + 1, CHAN_G, U_STEP), :] = powers[HALF][1]
        powers = unit_powers(uv_ref[0, 1:2, part] * scale)
        for m in range(SG):
            cos, sin = powers[abs(m - HALF)]
            v_tab[pl.ds(m, CHAN_G, V_STEP), :] = cos
            v_tab[pl.ds(SG + m, CHAN_G, V_STEP), :] = sin if m >= HALF else -sin
        sums = None
        step = 4
        for start in range(0, CHAN_G, step):
            left, right = [], []
            for h in range(start, start + step):
                right.append(v_tab[pl.ds(h * V_STEP, 2 * SG), :].astype(bf16))
                u_rows = u_tab[pl.ds(h * U_STEP, SG), :]
                column = [
                    (u_rows * w_tab[pl.ds(c * W_STEP + h, 1), :]).astype(bf16)
                    for c in range(COMPS)
                ]
                w_all = w_tab[pl.ds(h, COMPS, W_STEP), :]
                last = [w_all * u_tab[pl.ds(h * U_STEP + SG + i, 1), :] for i in range(2)]
                column.append(jnp.concatenate(last, 0).astype(bf16))
                left.append(jnp.concatenate(column, 0))
            term = lax.dot_general(
                jnp.concatenate(left, 1),
                jnp.concatenate(right, 1),
                (((1,), (1,)), ((), ())),
                preferred_element_type=f32,
            )
            sums = term if sums is None else sums + term
        return sums

    def finish(out_ref, s, sums):
        def rows(part, pair):
            at = (part * POL + 2 * pair) * SG
            return jnp.concatenate([sums[at : at + SG], sums[at + SG : at + 2 * SG]], 1)

        def extra(sine, part, pair):
            at = COMPS * SG + COMPS * sine + part * POL + 2 * pair
            return jnp.concatenate([sums[at : at + 1], sums[at + 1 : at + 2]], 1)

        for pair in range(2):
            combine(out_ref, s, pair, rows(0, pair), rows(1, pair), functools.partial(extra, pair=pair))

    def combine(out_ref, s, pair, x, y, extra):
        xc, xs, yc, ys = x[:HALF], x[HALF:], y[:HALF], y[HALF:]
        low_re = jnp.where(first_row, extra(0, 0) + extra(1, 1), xc + ys)
        low_im = jnp.where(first_row, extra(0, 1) - extra(1, 0), yc - xs)
        f_re = jnp.concatenate([xc - ys, low_re], 0)
        f_im = jnp.concatenate([yc + xs, low_im], 0)
        swapped = jnp.where(is_re, -pltpu.roll(f_im, LANES - SG, 1), pltpu.roll(f_im, SG, 1))
        out_ref[s, pair * SG : (pair + 1) * SG, :] = (f_re + swapped).astype(bf16)

    for i, k in enumerate(ks):
        group = me[0] ^ k
        for h in range(CHAN_G):
            scale_tab[h : h + 1, :] = jnp.full((1, LANES), scales[group * CHAN_G + h], f32)
        scale = scale_tab[...] * (2.0 * math.pi / SG)
        for s in range(outs[i].shape[0]):
            finish(outs[i], s, build(blocks[i], s, scale))


def images(ks, me, valid, scales, vis, uv):
    rows = vis.shape[2]
    count = rows // TSTEP
    block = (COMPS, CHAN_G, rows)
    whole = pl.BlockSpec((count, 2 * SG, LANES), lambda i, at: (0, 0, 0))
    return pl.pallas_call(
        functools.partial(image_kernel, ks),
        out_shape=[jax.ShapeDtypeStruct((count, 2 * SG, LANES), bf16)] * len(ks),
        grid_spec=pltpu.PrefetchScalarGridSpec(
            num_scalar_prefetch=1,
            grid=(1,),
            in_specs=[smem(), smem()]
            + [pl.BlockSpec(block, lambda i, at, k=k: (0, at[0] ^ k, 0)) for k in ks]
            + [pl.BlockSpec((1, 2, rows), lambda i, at: (0, 0, 0))],
            out_specs=[whole] * len(ks),
            scratch_shapes=[
                pltpu.VMEM((CHAN_G * U_STEP, LANES), f32),
                pltpu.VMEM((CHAN_G * V_STEP, LANES), f32),
                pltpu.VMEM((COMPS * W_STEP, LANES), f32),
                pltpu.VMEM((CHAN_G, LANES), f32),
            ],
        ),
        compiler_params=pltpu.CompilerParams(vmem_limit_bytes=VMEM_LIMIT),
        cost_estimate=pl.CostEstimate(
            flops=len(ks) * count * FAN * 40000, bytes_accessed=1 << 20, transcendentals=0
        ),
        name="images",
    )(me, valid, scales, *([vis] * len(ks)), uv)


def gain_kernel(stations, aterm, taper, tiles, out_ref, rows, sems):
    count = rows.shape[0] // 2

    def copy(i):
        return pltpu.make_async_copy(
            aterm.at[0, stations[0, 0, i // count, i % count]], rows.at[i], sems.at[i]
        )

    def start(i, _):
        copy(i).start()
        return 0

    def wait(i, _):
        copy(i).wait()
        return 0

    lax.fori_loop(0, 2 * count, start, 0, unroll=8)
    lax.fori_loop(0, 2 * count, wait, 0, unroll=8)
    for r in range(SG * SG // LANES):
        cols = pl.ds(r * LANES, LANES)
        one_re, one_im = rows[0:count, 0, cols], rows[0:count, 1, cols]
        two_re, two_im = rows[count:, 0, cols], rows[count:, 1, cols]
        shape = jnp.concatenate(
            [taper[POL * r + q : POL * r + q + 1, :] for q in range(POL)], 1
        ) * (1.0 / (math.sqrt(FAN) * SG))
        gain = jnp.concatenate(
            [(one_re * two_re + one_im * two_im) * shape, (one_im * two_re - one_re * two_im) * shape], 0
        )
        high = gain.astype(bf16)
        rest = gain - high.astype(f32)
        mid = rest.astype(bf16)
        low = (rest - mid.astype(f32)).astype(bf16)
        tiled = jnp.dot(
            jnp.concatenate([high, mid, low], 1), tiles[...], preferred_element_type=f32
        )
        for q in range(POL):
            row = list(IMAGE_ROWS).index(POL * r + q)
            lanes = tiled[:, q * LANES : (q + 1) * LANES]
            out_ref[0, row] = lanes[:count]
            out_ref[1, row] = lanes[count:]


def gains(stations, aterm, taper):
    count = stations.shape[3]
    return pl.pallas_call(
        gain_kernel,
        out_shape=jax.ShapeDtypeStruct((2, SG, count, LANES), f32),
        in_specs=[smem(), pl.BlockSpec(memory_space=pl.ANY), vmem(), vmem()],
        out_specs=vmem(),
        scratch_shapes=[
            pltpu.VMEM((2 * count, 2, SG * SG), f32),
            pltpu.SemaphoreType.DMA((2 * count,)),
        ],
        compiler_params=pltpu.CompilerParams(vmem_limit_bytes=VMEM_LIMIT),
        name="gains",
    )(stations, aterm, taper, lane_tiles())


def subgrid_kernel(chunks_n, me, owner, u_offset, v_start, gain, w_high, w_low, f_rows, *refs):
    chunks = refs[:chunks_n]
    out_ref, d_high, d_low, y_ref, pos, taken = refs[chunks_n:]
    block = chunks[0].shape[0]
    row = lax.broadcasted_iota(jnp.int32, (POS_ROWS, LANES), 0)

    def clear(i, _):
        taken[i] = 0
        return 0

    lax.fori_loop(0, taken.shape[0], clear, 0, unroll=8)
    out_ref[...] = jnp.zeros_like(out_ref)
    pos[...] = jnp.full(pos.shape, NO_PLACE, f32)
    for k in range(chunks_n):
        base = (me[0] ^ k) * block
        for i in range(block):
            gain_re, gain_im = gain[0, :, base + i, :], gain[1, :, base + i, :]
            for pair in range(2):
                image = chunks[k][i, pair * SG : (pair + 1) * SG, :].astype(f32)
                both = jnp.concatenate([image * gain_re, image * gain_im], 1)
                high = both.astype(bf16)
                at = pl.ds(((k * block + i) * 2 + pair) * SG, SG)
                d_high[at, :] = high
                d_low[at, :] = (both - high.astype(f32)).astype(bf16)
    step = 256
    for i in range(d_high.shape[0] // step):
        at = pl.ds(i * step, step)
        high = d_high[at, :]
        y_ref[at, :] = (
            jnp.dot(high, w_high[...], preferred_element_type=f32)
            + jnp.dot(d_low[at, :], w_high[...], preferred_element_type=f32)
            + jnp.dot(high, w_low[...], preferred_element_type=f32)
        )
    for k in range(chunks_n):
        base = (me[0] ^ k) * block
        for i in range(block):
            at = (k * block + i) * 2 * SG
            ys = [y_ref[pl.ds(at + pair * SG, SG), :] for pair in range(2)]
            rows = jnp.concatenate(
                [
                    jnp.concatenate([y[:, :LANES] for y in ys], 1),
                    jnp.concatenate([y[:, LANES:] for y in ys], 1),
                ],
                0,
            )
            high = rows.astype(bf16)
            low = (rows - high.astype(f32)).astype(bf16)
            cells = jnp.dot(
                f_rows[...], jnp.concatenate([high, low, high], 0), preferred_element_type=f32
            ).astype(bf16)
            s = base + i
            dest = owner[0, 0, 0, s]
            slot = jnp.minimum(taken[dest], CAP - 1)
            taken[dest] = slot + 1
            for pair in range(2):
                start = pl.multiple_of((slot * 2 + pair) * SG, SG)
                out_ref[dest, pl.ds(start, SG), :] = cells[:, pair * LANES : (pair + 1) * LANES]
            u, v = u_offset[0, 0, 0, s].astype(f32), v_start[0, 0, 0, s].astype(f32)
            pos[dest] = jnp.where(row == 2 * slot, u, jnp.where(row == 2 * slot + 1, v, pos[dest]))
    out_ref[:, CAP * 2 * SG :, :] = pos[...].astype(bf16)


def subgrids(chunks, me, owner, u_offset, v_start, gain, devices_n):
    count = owner.shape[3]
    return pl.pallas_call(
        functools.partial(subgrid_kernel, len(chunks)),
        out_shape=jax.ShapeDtypeStruct((devices_n, CAP * 2 * SG + POS_ROWS, LANES), bf16),
        in_specs=[smem()] * 4 + [vmem()] * (4 + len(chunks)),
        out_specs=vmem(),
        scratch_shapes=[
            pltpu.VMEM((count * 2 * SG, 2 * LANES), bf16),
            pltpu.VMEM((count * 2 * SG, 2 * LANES), bf16),
            pltpu.VMEM((count * 2 * SG, 2 * LANES), f32),
            pltpu.VMEM((devices_n, POS_ROWS, LANES), f32),
            pltpu.SMEM((devices_n,), jnp.int32),
        ],
        compiler_params=pltpu.CompilerParams(vmem_limit_bytes=VMEM_LIMIT),
        cost_estimate=pl.CostEstimate(flops=4 * 10**9, bytes_accessed=4 << 20, transcendentals=0),
        name="subgrids",
    )(me, owner, u_offset, v_start, gain, *lane_transform(), row_transform(), *chunks)


def place_kernel(arrived, out_ref, margin_ref, columns, spread, places):
    sources = arrived.shape[0]
    per_lanes = LANES // SG
    places[...] = arrived[:, CAP * 2 * SG :, :].astype(f32)
    lane = lax.broadcasted_iota(jnp.int32, (1, LANES), 1)
    u_index = lax.broadcasted_iota(jnp.int32, (TILE_W + SG, LANES), 0).astype(f32)
    step_a = (lane % SG).astype(f32)
    for j in range(sources * CAP // per_lanes):
        target = None
        for q in range(per_lanes):
            slot = j * per_lanes + q
            u = places[slot // CAP, 2 * (slot % CAP) : 2 * (slot % CAP) + 1, :]
            target = u if target is None else jnp.where(lane < q * SG, target, u)
        hot = jnp.where(u_index == target + step_a, 1.0, 0.0)
        columns[:, j * LANES : (j + 1) * LANES] = hot.astype(bf16)
    v_index = (
        lax.broadcasted_iota(jnp.int32, (SG, BAND_V), 1) - lax.broadcasted_iota(jnp.int32, (SG, BAND_V), 0)
    ).astype(f32)

    def along_v(source, _):
        for slot in range(CAP):
            cells = arrived[source, slot * 2 * SG : (slot + 1) * 2 * SG, :]
            stacked = jnp.concatenate([cells[:, SG * k : SG * (k + 1)] for k in range(POL)], 0)
            v = places[source, 2 * slot + 1 : 2 * slot + 2, :]
            hot = jnp.where(v_index == jnp.concatenate([v, v], 1), 1.0, 0.0).astype(bf16)
            wide = jnp.dot(stacked, hot, preferred_element_type=f32).astype(bf16)
            at = pl.ds(pl.multiple_of((source * CAP + slot) * SG, SG), SG)
            for k in range(POL):
                for pair in range(2):
                    comp = (k % 2) * POL + pair * 2 + k // 2
                    start = (k * 2 + pair) * SG
                    spread[at, comp * BAND_V : (comp + 1) * BAND_V] = wide[start : start + SG]
        return 0

    lax.fori_loop(0, sources, along_v, 0, unroll=4)
    for comp in range(COMPS):
        total = jnp.dot(
            columns[...], spread[:, comp * BAND_V : (comp + 1) * BAND_V], preferred_element_type=f32
        )
        out_ref[comp] = total[:TILE_W]
        margin_ref[comp] = total[TILE_W:].astype(bf16)


def placed(arrived):
    cells = arrived.shape[0] * CAP * SG
    return pl.pallas_call(
        place_kernel,
        out_shape=(
            jax.ShapeDtypeStruct((COMPS, TILE_W, BAND_V), f32),
            jax.ShapeDtypeStruct((COMPS, SG, BAND_V), bf16),
        ),
        in_specs=[vmem()],
        out_specs=(vmem(), vmem()),
        scratch_shapes=[
            pltpu.VMEM((TILE_W + SG, cells), bf16),
            pltpu.VMEM((cells, COMPS * BAND_V), bf16),
            pltpu.VMEM((arrived.shape[0], POS_ROWS, LANES), f32),
        ],
        compiler_params=pltpu.CompilerParams(vmem_limit_bytes=VMEM_LIMIT),
        name="tile",
    )(arrived)


def on_device(
    visibilities, uv_rows, chan_scale, valid_rows, aterm, taper, stations, owner, u_offset, v_start
):
    groups_n = lax.axis_size("freq")
    devices_n = groups_n * lax.axis_size("tile")
    me = lax.axis_index("freq")[None].astype(jnp.int32)
    far = list(range(groups_n - 1, 1, -1))
    near = [k for k in (1, 0) if k < groups_n]
    chunks = {}
    for ks in (far, near):
        if ks:
            parts = images(ks, me, valid_rows, chan_scale, visibilities[0], uv_rows)
            for k, part in zip(ks, parts):
                if k:
                    part = lax.ppermute(part, "freq", [(i, i ^ k) for i in range(groups_n)])
                chunks[k] = part
    stations, owner, u_offset, v_start = (
        jnp.swapaxes(index, 2, 3) for index in (stations, owner, u_offset, v_start)
    )
    gain = gains(stations, aterm, taper)
    outgoing = subgrids(
        [chunks[k] for k in range(groups_n)], me, owner, u_offset, v_start, gain, devices_n
    )
    arrived = lax.all_to_all(
        outgoing, ("freq", "tile"), split_axis=0, concat_axis=0, tiled=True
    )
    tile, margin = placed(arrived)
    incoming = lax.ppermute(
        margin, ("freq", "tile"), [(i, (i + 1) % devices_n) for i in range(devices_n)]
    )
    return tile.at[:, :SG, :].add(incoming.astype(f32))


def solution(mesh):
    in_specs = (
        P("tile", None, None, "freq"),
        P("tile", None, "freq"),
        P(),
        P("tile", "freq"),
        P("freq", None, None, None),
        P(),
        P("tile", "freq", None, None),
        P("tile", "freq", None, None),
        P("tile", "freq", None, None),
        P("tile", "freq", None, None),
    )
    out_specs = P(None, ("freq", "tile"), None)
    return jax.shard_map(
        on_device, mesh=mesh, in_specs=in_specs, out_specs=out_specs, check_vma=False
    )
```

```python
import functools
import math

import jax
import jax.numpy as jnp
import ml_dtypes
import numpy as np
from jax import lax
from jax.experimental import pallas as pl
from jax.experimental.pallas import tpu as pltpu
from jax.sharding import PartitionSpec as P

SG = 32
HALF = SG // 2
TSTEP = 128
CHAN_G = 16
FAN = CHAN_G * TSTEP
TILE_W = 256
BAND_V = 256
LANES = 128
COMPS = 8
POL = 4
POS_ROWS = 8
NO_PLACE = 512.0
CAP = 2
U_STEP = SG + 3
V_STEP = 2 * SG + 1
W_STEP = CHAN_G + 1
VMEM_LIMIT = 60 << 20
f32 = jnp.float32
bf16 = jnp.bfloat16


def vmem():
    return pl.BlockSpec(memory_space=pltpu.VMEM)


def smem():
    return pl.BlockSpec(memory_space=pltpu.SMEM)


IMAGE_ROWS = np.array([HALF + i for i in range(HALF)] + [0] + [HALF - i for i in range(1, HALF)])


def split(matrix):
    high = matrix.astype(np.float32).astype(ml_dtypes.bfloat16)
    low = (matrix - high.astype(np.float64)).astype(np.float32).astype(ml_dtypes.bfloat16)
    return high, low


def fourier():
    cells = np.arange(SG) - HALF
    angles = (cells[:, None] * cells[None, :] % SG) * (2.0 * math.pi / SG)
    return np.cos(angles), -np.sin(angles)


def lane_transform():
    cos, sin = fourier()
    table = np.zeros((2, 2, 2, SG, 2, 2, 2, SG))
    for p in range(2):
        y_re = {(0, 0): cos, (1, 1): -cos, (1, 0): -sin, (0, 1): -sin}
        y_im = {(0, 0): sin, (1, 1): -sin, (1, 0): cos, (0, 1): cos}
        for gain in range(2):
            for part in range(2):
                re, im = y_re[gain, part].T, y_im[gain, part].T
                table[gain, p, part, :, 0, p, 0, :] = re
                table[gain, p, part, :, 0, p, 1, :] = im
                table[gain, p, part, :, 1, p, 0, :] = -im
                table[gain, p, part, :, 1, p, 1, :] = re
    return split(table.reshape(256, 256))


def row_transform():
    cos, sin = fourier()
    high, low = split(np.concatenate([cos[:, IMAGE_ROWS], sin[:, IMAGE_ROWS]], 1))
    return np.concatenate([high, high, low], 1)


def lane_tiles():
    table = np.zeros((POL, SG, POL, POL, SG))
    for q in range(POL):
        for copy in range(POL):
            table[q, :, q, copy, :] = np.eye(SG)
    table = table.reshape(LANES, POL * LANES)
    return np.concatenate([table] * 3, 0).astype(ml_dtypes.bfloat16)


def unit_powers(theta):
    half = theta * 0.5
    square = half * half
    sin_h = half * (
        1.0 + square * (-1.0 / 6 + square * (1.0 / 120 + square * (-1.0 / 5040 + square * (1.0 / 362880))))
    )
    cos_h = 1.0 + square * (
        -0.5 + square * (1.0 / 24 + square * (-1.0 / 720 + square * (1.0 / 40320 + square * (-1.0 / 3628800))))
    )
    powers = {0: (jnp.ones_like(theta), jnp.zeros_like(theta))}
    powers[1] = (1.0 - 2.0 * sin_h * sin_h, 2.0 * sin_h * cos_h)
    for n in range(2, HALF + 1):
        (ca, sa), (cb, sb) = powers[n // 2], powers[n - n // 2]
        if n % 2 == 0:
            powers[n] = (1.0 - 2.0 * sa * sa, 2.0 * sa * ca)
        else:
            powers[n] = (ca * cb - sa * sb, ca * sb + sa * cb)
    return powers


def gain_copies(stations, aterm, rows, sems):
    count = rows.shape[0] // 2
    return [
        pltpu.make_async_copy(
            aterm.at[0, stations[0, 0, i // count, i % count]], rows.at[i], sems.at[i]
        )
        for i in range(2 * count)
    ]


def make_gains(taper, tiles, out_ref, rows):
    count = rows.shape[0] // 2
    for r in range(SG * SG // LANES):
        cols = pl.ds(r * LANES, LANES)
        one_re, one_im = rows[0:count, 0, cols], rows[0:count, 1, cols]
        two_re, two_im = rows[count:, 0, cols], rows[count:, 1, cols]
        shape = jnp.concatenate(
            [taper[POL * r + q : POL * r + q + 1, :] for q in range(POL)], 1
        ) * (1.0 / (math.sqrt(FAN) * SG))
        gain = jnp.concatenate(
            [(one_re * two_re + one_im * two_im) * shape, (one_im * two_re - one_re * two_im) * shape], 0
        )
        high = gain.astype(bf16)
        rest = gain - high.astype(f32)
        mid = rest.astype(bf16)
        low = (rest - mid.astype(f32)).astype(bf16)
        tiled = jnp.dot(
            jnp.concatenate([high, mid, low], 1), tiles[...], preferred_element_type=f32
        )
        for q in range(POL):
            row = list(IMAGE_ROWS).index(POL * r + q)
            lanes = tiled[:, q * LANES : (q + 1) * LANES]
            out_ref[0, row] = lanes[:count]
            out_ref[1, row] = lanes[count:]


def image_kernel(ks, with_gains, me, valid, scales, *refs):
    refs = list(refs)
    take = lambda count: [refs.pop(0) for _ in range(count)]
    stations = take(1)[0] if with_gains else None
    blocks, (uv_ref,) = take(len(ks)), take(1)
    aterm, taper, tiles = take(3) if with_gains else (None, None, None)
    outs = take(len(ks))
    gain_ref = take(1)[0] if with_gains else None
    u_tab, v_tab, w_tab, scale_tab = take(4)
    copies = []
    if with_gains:
        copies = gain_copies(stations, aterm, *refs)
    for copy in copies:
        copy.start()
    lane = lax.broadcasted_iota(jnp.int32, (CHAN_G, TSTEP), 1)
    out_lane = lax.broadcasted_iota(jnp.int32, (SG, LANES), 1)
    is_re = out_lane % (2 * SG) < SG
    first_row = lax.broadcasted_iota(jnp.int32, (HALF, LANES), 0) == 0

    def build(vis_ref, s, scale):
        part = pl.ds(s * TSTEP, TSTEP)
        live = lane + s * TSTEP < valid[0, 0]
        for c in range(COMPS):
            values = vis_ref[c, :, part].astype(f32)
            w_tab[pl.ds(c * W_STEP, CHAN_G), :] = jnp.where(live, values, 0.0)
        powers = unit_powers(uv_ref[0, 0:1, part] * scale)
        for n in range(HALF):
            u_tab[pl.ds(n, CHAN_G, U_STEP), :] = powers[n][0]
            u_tab[pl.ds(HALF + n, CHAN_G, U_STEP), :] = powers[n][1]
        u_tab[pl.ds(SG, CHAN_G, U_STEP), :] = powers[HALF][0]
        u_tab[pl.ds(SG + 1, CHAN_G, U_STEP), :] = powers[HALF][1]
        powers = unit_powers(uv_ref[0, 1:2, part] * scale)
        for m in range(SG):
            cos, sin = powers[abs(m - HALF)]
            v_tab[pl.ds(m, CHAN_G, V_STEP), :] = cos
            v_tab[pl.ds(SG + m, CHAN_G, V_STEP), :] = sin if m >= HALF else -sin
        sums = None
        step = 4
        for start in range(0, CHAN_G, step):
            left, right = [], []
            for h in range(start, start + step):
                right.append(v_tab[pl.ds(h * V_STEP, 2 * SG), :].astype(bf16))
                u_rows = u_tab[pl.ds(h * U_STEP, SG), :]
                column = [
                    (u_rows * w_tab[pl.ds(c * W_STEP + h, 1), :]).astype(bf16)
                    for c in range(COMPS)
                ]
                w_all = w_tab[pl.ds(h, COMPS, W_STEP), :]
                last = [w_all * u_tab[pl.ds(h * U_STEP + SG + i, 1), :] for i in range(2)]
                column.append(jnp.concatenate(last, 0).astype(bf16))
                left.append(jnp.concatenate(column, 0))
            term = lax.dot_general(
                jnp.concatenate(left, 1),
                jnp.concatenate(right, 1),
                (((1,), (1,)), ((), ())),
                preferred_element_type=f32,
            )
            sums = term if sums is None else sums + term
        return sums

    def finish(out_ref, s, sums):
        def rows(part, pair):
            at = (part * POL + 2 * pair) * SG
            return jnp.concatenate([sums[at : at + SG], sums[at + SG : at + 2 * SG]], 1)

        def extra(sine, part, pair):
            at = COMPS * SG + COMPS * sine + part * POL + 2 * pair
            return jnp.concatenate([sums[at : at + 1], sums[at + 1 : at + 2]], 1)

        for pair in range(2):
            combine(out_ref, s, pair, rows(0, pair), rows(1, pair), functools.partial(extra, pair=pair))

    def combine(out_ref, s, pair, x, y, extra):
        xc, xs, yc, ys = x[:HALF], x[HALF:], y[:HALF], y[HALF:]
        low_re = jnp.where(first_row, extra(0, 0) + extra(1, 1), xc + ys)
        low_im = jnp.where(first_row, extra(0, 1) - extra(1, 0), yc - xs)
        f_re = jnp.concatenate([xc - ys, low_re], 0)
        f_im = jnp.concatenate([yc + xs, low_im], 0)
        swapped = jnp.where(is_re, -pltpu.roll(f_im, LANES - SG, 1), pltpu.roll(f_im, SG, 1))
        out_ref[s, pair * SG : (pair + 1) * SG, :] = (f_re + swapped).astype(bf16)

    for i, k in enumerate(ks):
        group = me[0] ^ k
        for h in range(CHAN_G):
            scale_tab[h : h + 1, :] = jnp.full((1, LANES), scales[group * CHAN_G + h], f32)
        scale = scale_tab[...] * (2.0 * math.pi / SG)
        for s in range(outs[i].shape[0]):
            finish(outs[i], s, build(blocks[i], s, scale))
            if with_gains and i == len(ks) - 1 and s == outs[i].shape[0] - 3:
                for copy in copies:
                    copy.wait()
                make_gains(taper, tiles, gain_ref, refs[0])


def images(ks, me, valid, scales, vis, uv, gain_args=()):
    rows = vis.shape[2]
    count = rows // TSTEP
    block = (COMPS, CHAN_G, rows)
    whole = pl.BlockSpec((count, 2 * SG, LANES), lambda i, at: (0, 0, 0))
    out_shape = [jax.ShapeDtypeStruct((count, 2 * SG, LANES), bf16)] * len(ks)
    out_specs = [whole] * len(ks)
    in_specs = [pl.BlockSpec(block, lambda i, at, k=k: (0, at[0] ^ k, 0)) for k in ks]
    in_specs += [pl.BlockSpec((1, 2, rows), lambda i, at: (0, 0, 0))]
    scratch = [
        pltpu.VMEM((CHAN_G * U_STEP, LANES), f32),
        pltpu.VMEM((CHAN_G * V_STEP, LANES), f32),
        pltpu.VMEM((COMPS * W_STEP, LANES), f32),
        pltpu.VMEM((CHAN_G, LANES), f32),
    ]
    operands = [vis] * len(ks) + [uv]
    if gain_args:
        stations, aterm, taper = gain_args
        subs = stations.shape[3]
        tiles = lane_tiles()
        operands = [stations] + operands + [aterm, taper, tiles]
        in_specs = [smem()] + in_specs + [
            pl.BlockSpec(memory_space=pl.ANY),
            pl.BlockSpec(taper.shape, lambda i, at: (0, 0)),
            pl.BlockSpec(tiles.shape, lambda i, at: (0, 0)),
        ]
        out_shape += [jax.ShapeDtypeStruct((2, SG, subs, LANES), f32)]
        out_specs += [pl.BlockSpec((2, SG, subs, LANES), lambda i, at: (0, 0, 0, 0))]
        scratch += [pltpu.VMEM((2 * subs, 2, SG * SG), f32), pltpu.SemaphoreType.DMA((2 * subs,))]
    return pl.pallas_call(
        functools.partial(image_kernel, ks, bool(gain_args)),
        out_shape=out_shape,
        grid_spec=pltpu.PrefetchScalarGridSpec(
            num_scalar_prefetch=1,
            grid=(1,),
            in_specs=[smem(), smem()] + in_specs,
            out_specs=out_specs,
            scratch_shapes=scratch,
        ),
        compiler_params=pltpu.CompilerParams(vmem_limit_bytes=VMEM_LIMIT),
        cost_estimate=pl.CostEstimate(
            flops=len(ks) * count * FAN * 40000, bytes_accessed=1 << 20, transcendentals=0
        ),
        name="images",
    )(me, valid, scales, *operands)


def subgrid_kernel(chunks_n, me, owner, u_offset, v_start, gain, w_high, w_low, f_rows, *refs):
    chunks = refs[:chunks_n]
    out_ref, d_high, d_low, y_ref, pos, taken = refs[chunks_n:]
    block = chunks[0].shape[0]
    row = lax.broadcasted_iota(jnp.int32, (POS_ROWS, LANES), 0)

    def clear(i, _):
        taken[i] = 0
        return 0

    lax.fori_loop(0, taken.shape[0], clear, 0, unroll=8)
    out_ref[...] = jnp.zeros_like(out_ref)
    pos[...] = jnp.full(pos.shape, NO_PLACE, f32)
    for k in range(chunks_n):
        base = (me[0] ^ k) * block
        for i in range(block):
            gain_re, gain_im = gain[0, :, base + i, :], gain[1, :, base + i, :]
            for pair in range(2):
                image = chunks[k][i, pair * SG : (pair + 1) * SG, :].astype(f32)
                both = jnp.concatenate([image * gain_re, image * gain_im], 1)
                high = both.astype(bf16)
                at = pl.ds(((k * block + i) * 2 + pair) * SG, SG)
                d_high[at, :] = high
                d_low[at, :] = (both - high.astype(f32)).astype(bf16)
    step = 256
    for i in range(d_high.shape[0] // step):
        at = pl.ds(i * step, step)
        high = d_high[at, :]
        y_ref[at, :] = (
            jnp.dot(high, w_high[...], preferred_element_type=f32)
            + jnp.dot(d_low[at, :], w_high[...], preferred_element_type=f32)
            + jnp.dot(high, w_low[...], preferred_element_type=f32)
        )
    for k in range(chunks_n):
        base = (me[0] ^ k) * block
        for i in range(block):
            at = (k * block + i) * 2 * SG
            ys = [y_ref[pl.ds(at + pair * SG, SG), :] for pair in range(2)]
            rows = jnp.concatenate(
                [
                    jnp.concatenate([y[:, :LANES] for y in ys], 1),
                    jnp.concatenate([y[:, LANES:] for y in ys], 1),
                ],
                0,
            )
            high = rows.astype(bf16)
            low = (rows - high.astype(f32)).astype(bf16)
            cells = jnp.dot(
                f_rows[...], jnp.concatenate([high, low, high], 0), preferred_element_type=f32
            ).astype(bf16)
            s = base + i
            dest = owner[0, 0, 0, s]
            slot = jnp.minimum(taken[dest], CAP - 1)
            taken[dest] = slot + 1
            for pair in range(2):
                start = pl.multiple_of((slot * 2 + pair) * SG, SG)
                out_ref[dest, pl.ds(start, SG), :] = cells[:, pair * LANES : (pair + 1) * LANES]
            u, v = u_offset[0, 0, 0, s].astype(f32), v_start[0, 0, 0, s].astype(f32)
            pos[dest] = jnp.where(row == 2 * slot, u, jnp.where(row == 2 * slot + 1, v, pos[dest]))
    out_ref[:, CAP * 2 * SG :, :] = pos[...].astype(bf16)


def subgrids(chunks, me, owner, u_offset, v_start, gain, devices_n):
    count = owner.shape[3]
    return pl.pallas_call(
        functools.partial(subgrid_kernel, len(chunks)),
        out_shape=jax.ShapeDtypeStruct((devices_n, CAP * 2 * SG + POS_ROWS, LANES), bf16),
        in_specs=[smem()] * 4 + [vmem()] * (4 + len(chunks)),
        out_specs=vmem(),
        scratch_shapes=[
            pltpu.VMEM((count * 2 * SG, 2 * LANES), bf16),
            pltpu.VMEM((count * 2 * SG, 2 * LANES), bf16),
            pltpu.VMEM((count * 2 * SG, 2 * LANES), f32),
            pltpu.VMEM((devices_n, POS_ROWS, LANES), f32),
            pltpu.SMEM((devices_n,), jnp.int32),
        ],
        compiler_params=pltpu.CompilerParams(vmem_limit_bytes=VMEM_LIMIT),
        cost_estimate=pl.CostEstimate(flops=4 * 10**9, bytes_accessed=4 << 20, transcendentals=0),
        name="subgrids",
    )(me, owner, u_offset, v_start, gain, *lane_transform(), row_transform(), *chunks)


def along_v(arrived, places, source, slot, v_index):
    cells = arrived[source, pl.ds(slot * 2 * SG, 2 * SG), :]
    stacked = jnp.concatenate([cells[:, SG * k : SG * (k + 1)] for k in range(POL)], 0)
    v = places[source, pl.ds(2 * slot + 1, 1), :]
    hot = jnp.where(v_index == jnp.concatenate([v, v], 1), 1.0, 0.0).astype(bf16)
    return jnp.dot(stacked, hot, preferred_element_type=f32)


def v_steps():
    rows = lax.broadcasted_iota(jnp.int32, (SG, BAND_V), 0)
    return (lax.broadcasted_iota(jnp.int32, (SG, BAND_V), 1) - rows).astype(f32)


def parts():
    return [
        ((k % 2) * POL + pair * 2 + k // 2, (k * 2 + pair) * SG) for k in range(POL) for pair in range(2)
    ]


def margin_kernel(arrived, out_ref, acc, places, chosen, starts):
    sources = arrived.shape[0]
    batch = 4
    first = TILE_W - SG
    acc[...] = jnp.zeros_like(acc)
    places[...] = arrived[:, CAP * 2 * SG :, :].astype(f32)
    found = jnp.int32(0)
    for source in range(sources):
        for slot in range(CAP):
            u = places[source, 2 * slot, 0].astype(jnp.int32)
            chosen[found] = source * CAP + slot
            starts[found] = u - first
            found = found + ((u > first) & (u < TILE_W)).astype(jnp.int32)
    for i in range(batch):
        chosen[found + i] = 0
        starts[found + i] = 2 * SG
    v_index = v_steps()

    def add(i, _):
        wide = []
        for j in range(batch):
            at = chosen[i * batch + j]
            wide.append(along_v(arrived, places, at // CAP, at % CAP, v_index))
        for j in range(batch):
            rows = pl.ds(starts[i * batch + j], SG)
            for comp, start in parts():
                for side in range(BAND_V // LANES):
                    acc[comp, side, rows, :] += wide[j][
                        start : start + SG, side * LANES : (side + 1) * LANES
                    ]
        return 0

    lax.fori_loop(0, (found + batch - 1) // batch, add, 0)
    for side in range(BAND_V // LANES):
        out_ref[:, :, side * LANES : (side + 1) * LANES] = acc[:, side, SG : 2 * SG, :].astype(bf16)


def margin_of(arrived):
    slots = arrived.shape[0] * CAP
    return pl.pallas_call(
        margin_kernel,
        out_shape=jax.ShapeDtypeStruct((COMPS, SG, BAND_V), bf16),
        in_specs=[vmem()],
        out_specs=vmem(),
        scratch_shapes=[
            pltpu.VMEM((COMPS, BAND_V // LANES, 3 * SG, LANES), f32),
            pltpu.VMEM((arrived.shape[0], POS_ROWS, LANES), f32),
            pltpu.SMEM((slots + 4,), jnp.int32),
            pltpu.SMEM((slots + 4,), jnp.int32),
        ],
        compiler_params=pltpu.CompilerParams(vmem_limit_bytes=VMEM_LIMIT),
        name="margin",
    )(arrived)


def tile_kernel(arrived, out_ref, columns, spread, places, result, sems):
    sources = arrived.shape[0]
    per_lanes = LANES // SG
    places[...] = arrived[:, CAP * 2 * SG :, :].astype(f32)
    lane = lax.broadcasted_iota(jnp.int32, (1, LANES), 1)
    u_index = lax.broadcasted_iota(jnp.int32, (TILE_W, LANES), 0).astype(f32)
    step_a = (lane % SG).astype(f32)
    for j in range(sources * CAP // per_lanes):
        target = None
        for q in range(per_lanes):
            slot = j * per_lanes + q
            u = places[slot // CAP, 2 * (slot % CAP) : 2 * (slot % CAP) + 1, :]
            target = u if target is None else jnp.where(lane < q * SG, target, u)
        hot = jnp.where(u_index == target + step_a, 1.0, 0.0)
        columns[:, j * LANES : (j + 1) * LANES] = hot.astype(bf16)
    v_index = v_steps()
    unrolled = min(32, sources)

    def spread_some(i, _):
        for j in range(unrolled):
            source = i * unrolled + j
            for slot in range(CAP):
                wide = along_v(arrived, places, source, slot, v_index).astype(bf16)
                at = pl.ds(pl.multiple_of((source * CAP + slot) * SG, SG), SG)
                for comp, start in parts():
                    spread[at, comp * BAND_V : (comp + 1) * BAND_V] = wide[start : start + SG]
        return 0

    lax.fori_loop(0, sources // unrolled, spread_some, 0)
    copies = []
    for comp in range(COMPS):
        result[comp] = jnp.dot(
            columns[...], spread[:, comp * BAND_V : (comp + 1) * BAND_V], preferred_element_type=f32
        )
        copies.append(pltpu.make_async_copy(result.at[comp], out_ref.at[comp], sems.at[comp]))
        copies[-1].start()
    for copy in copies:
        copy.wait()


def tile_of(arrived):
    cells = arrived.shape[0] * CAP * SG
    return pl.pallas_call(
        tile_kernel,
        out_shape=jax.ShapeDtypeStruct((COMPS, TILE_W, BAND_V), f32),
        in_specs=[vmem()],
        out_specs=pl.BlockSpec(memory_space=pl.ANY),
        scratch_shapes=[
            pltpu.VMEM((TILE_W, cells), bf16),
            pltpu.VMEM((cells, COMPS * BAND_V), bf16),
            pltpu.VMEM((arrived.shape[0], POS_ROWS, LANES), f32),
            pltpu.VMEM((COMPS, TILE_W, BAND_V), f32),
            pltpu.SemaphoreType.DMA((COMPS,)),
        ],
        compiler_params=pltpu.CompilerParams(vmem_limit_bytes=VMEM_LIMIT),
        cost_estimate=pl.CostEstimate(flops=4 * 10**9, bytes_accessed=4 << 20, transcendentals=0),
        name="tile",
    )(arrived)


def on_device(
    visibilities, uv_rows, chan_scale, valid_rows, aterm, taper, stations, owner, u_offset, v_start
):
    groups_n = lax.axis_size("freq")
    devices_n = groups_n * lax.axis_size("tile")
    me = lax.axis_index("freq")[None].astype(jnp.int32)
    far = list(range(groups_n - 1, 1, -1))
    near = [k for k in (1, 0) if k < groups_n]
    stations, owner, u_offset, v_start = (
        jnp.swapaxes(index, 2, 3) for index in (stations, owner, u_offset, v_start)
    )
    chunks = {}

    def make(ks, gain_args=()):
        made = images(ks, me, valid_rows, chan_scale, visibilities[0], uv_rows, gain_args)
        for k, part in zip(ks, made):
            if k:
                part = lax.ppermute(part, "freq", [(i, i ^ k) for i in range(groups_n)])
            chunks[k] = part
        return made[-1]

    if far:
        make(far)
    gain = make(near, (stations, aterm, taper))
    outgoing = subgrids(
        [chunks[k] for k in range(groups_n)], me, owner, u_offset, v_start, gain, devices_n
    )
    arrived = lax.all_to_all(
        outgoing, ("freq", "tile"), split_axis=0, concat_axis=0, tiled=True
    )
    incoming = lax.ppermute(
        margin_of(arrived), ("freq", "tile"), [(i, (i + 1) % devices_n) for i in range(devices_n)]
    )
    return tile_of(arrived).at[:, :SG, :].add(incoming.astype(f32))


def solution(mesh):
    in_specs = (
        P("tile", None, None, "freq"),
        P("tile", None, "freq"),
        P(),
        P("tile", "freq"),
        P("freq", None, None, None),
        P(),
        P("tile", "freq", None, None),
        P("tile", "freq", None, None),
        P("tile", "freq", None, None),
        P("tile", "freq", None, None),
    )
    out_specs = P(None, ("freq", "tile"), None)
    return jax.shard_map(
        on_device, mesh=mesh, in_specs=in_specs, out_specs=out_specs, check_vma=False
    )
```

```python
import functools
import math

import jax
import jax.numpy as jnp
import ml_dtypes
import numpy as np
from jax import lax
from jax.experimental import pallas as pl
from jax.experimental.pallas import tpu as pltpu
from jax.sharding import PartitionSpec as P

SG = 32
HALF = SG // 2
TSTEP = 128
CHAN_G = 16
FAN = CHAN_G * TSTEP
TILE_W = 256
BAND_V = 256
LANES = 128
COMPS = 8
POL = 4
POS_ROWS = 8
NO_PLACE = 512.0
COARSE = (4, 12)
FINE = 4
SUMS = 2 * (FINE + 1) * COMPS
CAP = 2
U_STEP = SG + 3
V_STEP = 13
W_STEP = CHAN_G + 1
VMEM_LIMIT = 60 << 20
f32 = jnp.float32
bf16 = jnp.bfloat16


def vmem():
    return pl.BlockSpec(memory_space=pltpu.VMEM)


def smem():
    return pl.BlockSpec(memory_space=pltpu.SMEM)


IMAGE_ROWS = np.array([HALF + i for i in range(HALF)] + [0] + [HALF - i for i in range(1, HALF)])


def split(matrix):
    high = matrix.astype(np.float32).astype(ml_dtypes.bfloat16)
    low = (matrix - high.astype(np.float64)).astype(np.float32).astype(ml_dtypes.bfloat16)
    return high, low


def fourier():
    cells = np.arange(SG) - HALF
    angles = (cells[:, None] * cells[None, :] % SG) * (2.0 * math.pi / SG)
    return np.cos(angles), -np.sin(angles)


def lane_transform():
    cos, sin = fourier()
    table = np.zeros((2, 2, 2, SG, 2, 2, 2, SG))
    for p in range(2):
        y_re = {(0, 0): cos, (1, 1): -cos, (1, 0): -sin, (0, 1): -sin}
        y_im = {(0, 0): sin, (1, 1): -sin, (1, 0): cos, (0, 1): cos}
        for gain in range(2):
            for part in range(2):
                re, im = y_re[gain, part].T, y_im[gain, part].T
                table[gain, p, part, :, 0, p, 0, :] = re
                table[gain, p, part, :, 0, p, 1, :] = im
                table[gain, p, part, :, 1, p, 0, :] = -im
                table[gain, p, part, :, 1, p, 1, :] = re
    return split(table.reshape(256, 256))


def row_transform():
    cos, sin = fourier()
    high, low = split(np.concatenate([cos[:, IMAGE_ROWS], sin[:, IMAGE_ROWS]], 1))
    return np.concatenate([high, high, low], 1)


def combine_table():
    table = np.zeros((4, 2, LANES, 2, 2, 2, SG))
    for m in range(SG):
        for a, coarse in enumerate((COARSE[0], -COARSE[0], COARSE[1], -COARSE[1])):
            b = m - HALF - coarse
            if not -FINE <= b < FINE:
                continue
            size, sign = abs(b), 1 if b > 0 else -1
            for p in range(POL):
                re, im = table[a, :, :, p // 2, p % 2, 0, m], table[a, :, :, p // 2, p % 2, 1, m]
                at = 2 * FINE * COMPS if b == 0 else (size - 1) * COMPS
                re[0, at + p], im[0, at + POL + p] = 1, 1
                re[1, at + POL + p], im[1, at + p] = -1, 1
                if b:
                    at += FINE * COMPS
                    re[0, at + POL + p], im[0, at + p] = -sign, sign
                    re[1, at + p], im[1, at + POL + p] = -sign, -sign
    return table.reshape(8 * LANES, 2 * LANES).astype(ml_dtypes.bfloat16)


def lane_tiles():
    table = np.zeros((POL, SG, POL, POL, SG))
    for q in range(POL):
        for copy in range(POL):
            table[q, :, q, copy, :] = np.eye(SG)
    table = table.reshape(LANES, POL * LANES)
    return np.concatenate([table] * 3, 0).astype(ml_dtypes.bfloat16)


def unit_powers(theta, wanted):
    half = theta * 0.5
    square = half * half
    sin_h = half * (
        1.0 + square * (-1.0 / 6 + square * (1.0 / 120 + square * (-1.0 / 5040 + square * (1.0 / 362880))))
    )
    cos_h = 1.0 + square * (
        -0.5 + square * (1.0 / 24 + square * (-1.0 / 720 + square * (1.0 / 40320 + square * (-1.0 / 3628800))))
    )
    powers = {0: (jnp.ones_like(theta), jnp.zeros_like(theta))}
    powers[1] = (1.0 - 2.0 * sin_h * sin_h, 2.0 * sin_h * cos_h)
    for n in wanted:
        if n in powers:
            continue
        first = n // 2 if n != 12 else 4
        (ca, sa), (cb, sb) = powers[first], powers[n - first]
        if 2 * first == n:
            powers[n] = (1.0 - 2.0 * sa * sa, 2.0 * sa * ca)
        else:
            powers[n] = (ca * cb - sa * sb, ca * sb + sa * cb)
    return powers


def gain_copies(stations, aterm, rows, sems):
    count = rows.shape[0] // 2
    return [
        pltpu.make_async_copy(
            aterm.at[0, stations[0, 0, i // count, i % count]],
            rows.at[i, :, pl.ds(0, SG * SG)],
            sems.at[i],
        )
        for i in range(2 * count)
    ]


def make_gains(taper, tiles, out_ref, rows):
    count = rows.shape[0] // 2
    blocks = SG * SG // LANES
    parts = []
    for r in range(blocks):
        cols = pl.ds(r * LANES, LANES)
        one_re, one_im = rows[0:count, 0, cols], rows[0:count, 1, cols]
        two_re, two_im = rows[count:, 0, cols], rows[count:, 1, cols]
        shape = jnp.concatenate(
            [taper[POL * r + q : POL * r + q + 1, :] for q in range(POL)], 1
        ) * (1.0 / (math.sqrt(FAN) * SG))
        gain = jnp.concatenate(
            [(one_re * two_re + one_im * two_im) * shape, (one_im * two_re - one_re * two_im) * shape], 0
        )
        high = gain.astype(bf16)
        rest = gain - high.astype(f32)
        mid = rest.astype(bf16)
        low = (rest - mid.astype(f32)).astype(bf16)
        parts.append(jnp.concatenate([high, mid, low], 1))
    tiled = jnp.dot(jnp.concatenate(parts, 0), tiles[...], preferred_element_type=f32)
    for r in range(blocks):
        for q in range(POL):
            row = list(IMAGE_ROWS).index(POL * r + q)
            for part in range(2):
                at = (2 * r + part) * count
                out_ref[part, row] = tiled[at : at + count, q * LANES : (q + 1) * LANES]


def image_kernel(ks, with_gains, me, valid, scales, *refs):
    refs = list(refs)
    take = lambda count: [refs.pop(0) for _ in range(count)]
    stations = take(1)[0] if with_gains else None
    vis_ref, uv_ref, combine = take(3)
    aterm, taper, tiles = take(3) if with_gains else (None, None, None)
    outs = take(len(ks))
    gain_ref = take(1)[0] if with_gains else None
    u_tabs, v_tabs, w_tabs, scale_tab, x_high, x_low = take(6)
    turn = pl.program_id(0)
    copies = gain_copies(stations, aterm, *refs) if with_gains else []

    @pl.when(turn == 0)
    def _():
        for copy in copies:
            copy.start()

    lane = lax.broadcasted_iota(jnp.int32, (CHAN_G, TSTEP), 1)
    first_row = lax.broadcasted_iota(jnp.int32, (HALF, LANES), 0) == 0

    def build(s, scale):
        u_tab, v_tab, w_tab = u_tabs.at[s % 2], v_tabs.at[s % 2], w_tabs.at[s % 2]
        part = pl.ds(s * TSTEP, TSTEP)
        live = lane + s * TSTEP < valid[0, 0]
        for c in range(COMPS):
            values = vis_ref[c, :, part].astype(f32)
            w_tab[pl.ds(c * W_STEP, CHAN_G), :] = jnp.where(live, values, 0.0)
        powers = unit_powers(uv_ref[0, 0:1, part] * scale, range(HALF + 1))
        for n in range(HALF):
            u_tab[pl.ds(n, CHAN_G, U_STEP), :] = powers[n][0]
            u_tab[pl.ds(HALF + n, CHAN_G, U_STEP), :] = powers[n][1]
        u_tab[pl.ds(SG, CHAN_G, U_STEP), :] = powers[HALF][0]
        u_tab[pl.ds(SG + 1, CHAN_G, U_STEP), :] = powers[HALF][1]
        powers = unit_powers(uv_ref[0, 1:2, part] * scale, (1, 2, 3, 4, 8, 12))
        for q, n in enumerate(COARSE):
            v_tab[pl.ds(2 * q, CHAN_G, V_STEP), :] = powers[n][0]
            v_tab[pl.ds(2 * q + 1, CHAN_G, V_STEP), :] = powers[n][1]
        for n in range(1, FINE + 1):
            v_tab[pl.ds(3 + n, CHAN_G, V_STEP), :] = powers[n][0]
            v_tab[pl.ds(3 + FINE + n, CHAN_G, V_STEP), :] = powers[n][1]
        sums = None
        step = 4
        pad = jnp.zeros((COMPS, TSTEP), f32)
        for start in range(0, CHAN_G, step):
            left, right = [], []
            for h in range(start, start + step):
                u_rows = u_tab[pl.ds(h * U_STEP, SG), :]
                column = [
                    (u_rows * v_tab[pl.ds(h * V_STEP + a, 1), :]).astype(bf16) for a in range(4)
                ]
                coarse = v_tab[pl.ds(h * V_STEP, 4), :]
                last = [coarse * u_tab[pl.ds(h * U_STEP + SG + i, 1), :] for i in range(2)]
                column.append(jnp.concatenate(last + [pad], 0).astype(bf16))
                left.append(jnp.concatenate(column, 0))
                w_all = w_tab[pl.ds(h, COMPS, W_STEP), :]
                fine = [w_all * v_tab[pl.ds(h * V_STEP + 4 + b, 1), :] for b in range(2 * FINE)]
                right.append(jnp.concatenate(fine + [w_all, pad], 0).astype(bf16))
            term = lax.dot_general(
                jnp.concatenate(left, 1),
                jnp.concatenate(right, 1),
                (((1,), (1,)), ((), ())),
                preferred_element_type=f32,
            )
            sums = term if sums is None else sums + term
        return sums

    def keep(s, sums):
        top = 4 * SG
        sums = jnp.concatenate([sums, jnp.zeros((sums.shape[0], LANES - SUMS), f32)], 1)
        for q in range(2):
            cos, sin = sums[2 * q * SG : (2 * q + 1) * SG], sums[(2 * q + 1) * SG : (2 * q + 2) * SG]
            cc, sc, cs, ss = cos[:HALF], cos[HALF:], sin[:HALF], sin[HALF:]
            ends = [sums[top + e : top + e + 1] for e in (2 * q, 4 + 2 * q, 2 * q + 1, 5 + 2 * q)]
            ecc, esc, ecs, ess = [jnp.where(first_row, e, x) for e, x in zip(ends, (cc, sc, cs, ss))]
            for d, (zero, one) in enumerate(
                (
                    ((cc - ss, ecc + ess), (sc + cs, ecs - esc)),
                    ((cc + ss, ecc - ess), (sc - cs, -esc - ecs)),
                )
            ):
                for x, values in enumerate((zero, one)):
                    both = jnp.concatenate(values, 0)
                    high = both.astype(bf16)
                    at = ((2 * q + d) * 2 + x) * LANES
                    x_high[s * SG : (s + 1) * SG, at : at + LANES] = high
                    x_low[s * SG : (s + 1) * SG, at : at + LANES] = (both - high.astype(f32)).astype(bf16)

    group = me[0] ^ (ks[0] - turn)
    for h in range(CHAN_G):
        scale_tab[h : h + 1, :] = jnp.full((1, LANES), scales[group * CHAN_G + h], f32)
    scale = scale_tab[...] * (2.0 * math.pi / SG)
    count = outs[0].shape[0]
    for s in range(count):
        keep(s, build(s, scale))
    image = (
        jnp.dot(x_high[...], combine[...], preferred_element_type=f32)
        + jnp.dot(x_low[...], combine[...], preferred_element_type=f32)
    ).astype(bf16)

    def write(out_ref):
        for s in range(count):
            for pair in range(2):
                out_ref[s, pair * SG : (pair + 1) * SG, :] = image[
                    s * SG : (s + 1) * SG, pair * LANES : (pair + 1) * LANES
                ]

    for i, out_ref in enumerate(outs):
        pl.when(turn == i)(functools.partial(write, out_ref))

    if with_gains:

        @pl.when(turn == len(ks) - 1)
        def _():
            for copy in copies:
                copy.wait()
            make_gains(taper, tiles, gain_ref, refs[0])


def images(ks, me, valid, scales, vis, uv, gain_args=()):
    rows = vis.shape[2]
    count = rows // TSTEP
    block = (COMPS, CHAN_G, rows)
    whole = pl.BlockSpec((count, 2 * SG, LANES), lambda i, at: (0, 0, 0))
    out_shape = [jax.ShapeDtypeStruct((count, 2 * SG, LANES), bf16)] * len(ks)
    out_specs = [whole] * len(ks)
    in_specs = [pl.BlockSpec(block, lambda i, at: (0, at[0] ^ (ks[0] - i), 0))]
    table = combine_table()
    in_specs += [
        pl.BlockSpec((1, 2, rows), lambda i, at: (0, 0, 0)),
        pl.BlockSpec(table.shape, lambda i, at: (0, 0)),
    ]
    scratch = [
        pltpu.VMEM((2, CHAN_G * U_STEP, LANES), f32),
        pltpu.VMEM((2, CHAN_G * V_STEP, LANES), f32),
        pltpu.VMEM((2, COMPS * W_STEP, LANES), f32),
        pltpu.VMEM((CHAN_G, LANES), f32),
        pltpu.VMEM((count * SG, 8 * LANES), bf16),
        pltpu.VMEM((count * SG, 8 * LANES), bf16),
    ]
    operands = [vis, uv, table]
    if gain_args:
        stations, aterm, taper = gain_args
        subs = stations.shape[3]
        tiles = lane_tiles()
        operands = [stations] + operands + [aterm, taper, tiles]
        in_specs = [smem()] + in_specs + [
            pl.BlockSpec(memory_space=pl.ANY),
            pl.BlockSpec(taper.shape, lambda i, at: (0, 0)),
            pl.BlockSpec(tiles.shape, lambda i, at: (0, 0)),
        ]
        out_shape += [jax.ShapeDtypeStruct((2, SG, subs, LANES), f32)]
        out_specs += [pl.BlockSpec((2, SG, subs, LANES), lambda i, at: (0, 0, 0, 0))]
        scratch += [pltpu.VMEM((2 * subs, 2, SG * SG + LANES), f32), pltpu.SemaphoreType.DMA((2 * subs,))]
    return pl.pallas_call(
        functools.partial(image_kernel, ks, bool(gain_args)),
        out_shape=out_shape,
        grid_spec=pltpu.PrefetchScalarGridSpec(
            num_scalar_prefetch=1,
            grid=(len(ks),),
            in_specs=[smem(), smem()] + in_specs,
            out_specs=out_specs,
            scratch_shapes=scratch,
        ),
        compiler_params=pltpu.CompilerParams(vmem_limit_bytes=VMEM_LIMIT),
        cost_estimate=pl.CostEstimate(
            flops=len(ks) * count * FAN * 40000, bytes_accessed=1 << 20, transcendentals=0
        ),
        name="images",
    )(me, valid, scales, *operands)


def subgrid_kernel(chunks_n, me, owner, u_offset, v_start, gain, w_high, w_low, f_rows, *refs):
    chunks = refs[:chunks_n]
    out_ref, d_high, d_low, y_ref, pos, taken = refs[chunks_n:]
    block = chunks[0].shape[0]
    row = lax.broadcasted_iota(jnp.int32, (POS_ROWS, LANES), 0)

    def clear(i, _):
        taken[i] = 0
        return 0

    lax.fori_loop(0, taken.shape[0], clear, 0, unroll=8)
    out_ref[...] = jnp.zeros_like(out_ref)
    pos[...] = jnp.full(pos.shape, NO_PLACE, f32)
    for k in range(chunks_n):
        base = (me[0] ^ k) * block
        for i in range(block):
            gain_re, gain_im = gain[0, :, base + i, :], gain[1, :, base + i, :]
            for pair in range(2):
                image = chunks[k][i, pair * SG : (pair + 1) * SG, :].astype(f32)
                both = jnp.concatenate([image * gain_re, image * gain_im], 1)
                high = both.astype(bf16)
                at = pl.ds(((k * block + i) * 2 + pair) * SG, SG)
                d_high[at, :] = high
                d_low[at, :] = (both - high.astype(f32)).astype(bf16)
    step = 256
    for i in range(d_high.shape[0] // step):
        at = pl.ds(i * step, step)
        high = d_high[at, :]
        y_ref[at, :] = (
            jnp.dot(high, w_high[...], preferred_element_type=f32)
            + jnp.dot(d_low[at, :], w_high[...], preferred_element_type=f32)
            + jnp.dot(high, w_low[...], preferred_element_type=f32)
        )
    for k in range(chunks_n):
        base = (me[0] ^ k) * block
        for i in range(block):
            at = (k * block + i) * 2 * SG
            ys = [y_ref[pl.ds(at + pair * SG, SG), :] for pair in range(2)]
            rows = jnp.concatenate(
                [
                    jnp.concatenate([y[:, :LANES] for y in ys], 1),
                    jnp.concatenate([y[:, LANES:] for y in ys], 1),
                ],
                0,
            )
            high = rows.astype(bf16)
            low = (rows - high.astype(f32)).astype(bf16)
            cells = jnp.dot(
                f_rows[...], jnp.concatenate([high, low, high], 0), preferred_element_type=f32
            ).astype(bf16)
            s = base + i
            dest = owner[0, 0, 0, s]
            slot = jnp.minimum(taken[dest], CAP - 1)
            taken[dest] = slot + 1
            for pair in range(2):
                start = pl.multiple_of((slot * 2 + pair) * SG, SG)
                out_ref[dest, pl.ds(start, SG), :] = cells[:, pair * LANES : (pair + 1) * LANES]
            u, v = u_offset[0, 0, 0, s].astype(f32), v_start[0, 0, 0, s].astype(f32)
            pos[dest] = jnp.where(row == 2 * slot, u, jnp.where(row == 2 * slot + 1, v, pos[dest]))
    out_ref[:, CAP * 2 * SG :, :] = pos[...].astype(bf16)


def subgrids(chunks, me, owner, u_offset, v_start, gain, devices_n):
    count = owner.shape[3]
    return pl.pallas_call(
        functools.partial(subgrid_kernel, len(chunks)),
        out_shape=jax.ShapeDtypeStruct((devices_n, CAP * 2 * SG + POS_ROWS, LANES), bf16),
        in_specs=[smem()] * 4 + [vmem()] * (4 + len(chunks)),
        out_specs=vmem(),
        scratch_shapes=[
            pltpu.VMEM((count * 2 * SG, 2 * LANES), bf16),
            pltpu.VMEM((count * 2 * SG, 2 * LANES), bf16),
            pltpu.VMEM((count * 2 * SG, 2 * LANES), f32),
            pltpu.VMEM((devices_n, POS_ROWS, LANES), f32),
            pltpu.SMEM((devices_n,), jnp.int32),
        ],
        compiler_params=pltpu.CompilerParams(vmem_limit_bytes=24 << 20),
        cost_estimate=pl.CostEstimate(flops=4 * 10**9, bytes_accessed=4 << 20, transcendentals=0),
        name="subgrids",
    )(me, owner, u_offset, v_start, gain, *lane_transform(), row_transform(), *chunks)


def along_v(arrived, places, source, slot, v_index):
    cells = arrived[source, pl.ds(slot * 2 * SG, 2 * SG), :]
    stacked = jnp.concatenate([cells[:, SG * k : SG * (k + 1)] for k in range(POL)], 0)
    v = places[source, pl.ds(2 * slot + 1, 1), :]
    hot = jnp.where(v_index == jnp.concatenate([v, v], 1), 1.0, 0.0).astype(bf16)
    return jnp.dot(stacked, hot, preferred_element_type=f32)


def v_steps():
    rows = lax.broadcasted_iota(jnp.int32, (SG, BAND_V), 0)
    return (lax.broadcasted_iota(jnp.int32, (SG, BAND_V), 1) - rows).astype(f32)


def parts():
    return [
        ((k % 2) * POL + pair * 2 + k // 2, (k * 2 + pair) * SG) for k in range(POL) for pair in range(2)
    ]


def margin_kernel(arrived, out_ref, acc, places, chosen, starts):
    sources = arrived.shape[0]
    batch = 4
    first = TILE_W - SG
    acc[...] = jnp.zeros_like(acc)
    places[...] = arrived[:, CAP * 2 * SG :, :].astype(f32)
    found = jnp.int32(0)
    for source in range(sources):
        for slot in range(CAP):
            u = places[source, 2 * slot, 0].astype(jnp.int32)
            chosen[found] = source * CAP + slot
            starts[found] = u - first
            found = found + ((u > first) & (u < TILE_W)).astype(jnp.int32)
    for i in range(batch):
        chosen[found + i] = 0
        starts[found + i] = 2 * SG
    v_index = v_steps()

    def add(i, _):
        wide = []
        for j in range(batch):
            at = chosen[i * batch + j]
            wide.append(along_v(arrived, places, at // CAP, at % CAP, v_index))
        for j in range(batch):
            rows = pl.ds(starts[i * batch + j], SG)
            for comp, start in parts():
                for side in range(BAND_V // LANES):
                    acc[comp, side, rows, :] += wide[j][
                        start : start + SG, side * LANES : (side + 1) * LANES
                    ]
        return 0

    lax.fori_loop(0, (found + batch - 1) // batch, add, 0)
    for side in range(BAND_V // LANES):
        out_ref[:, :, side * LANES : (side + 1) * LANES] = acc[:, side, SG : 2 * SG, :].astype(bf16)


def margin_of(arrived):
    slots = arrived.shape[0] * CAP
    return pl.pallas_call(
        margin_kernel,
        out_shape=jax.ShapeDtypeStruct((COMPS, SG, BAND_V), bf16),
        in_specs=[vmem()],
        out_specs=vmem(),
        scratch_shapes=[
            pltpu.VMEM((COMPS, BAND_V // LANES, 3 * SG, LANES), f32),
            pltpu.VMEM((arrived.shape[0], POS_ROWS, LANES), f32),
            pltpu.SMEM((slots + 4,), jnp.int32),
            pltpu.SMEM((slots + 4,), jnp.int32),
        ],
        compiler_params=pltpu.CompilerParams(vmem_limit_bytes=16 << 20),
        name="margin",
    )(arrived)


def tile_kernel(arrived, out_ref, columns, spread, places, result, sems):
    sources = arrived.shape[0]
    per_lanes = LANES // SG
    places[...] = arrived[:, CAP * 2 * SG :, :].astype(f32)
    lane = lax.broadcasted_iota(jnp.int32, (1, LANES), 1)
    u_index = lax.broadcasted_iota(jnp.int32, (TILE_W, LANES), 0).astype(f32)
    step_a = (lane % SG).astype(f32)
    for j in range(sources * CAP // per_lanes):
        target = None
        for q in range(per_lanes):
            slot = j * per_lanes + q
            u = places[slot // CAP, 2 * (slot % CAP) : 2 * (slot % CAP) + 1, :]
            target = u if target is None else jnp.where(lane < q * SG, target, u)
        hot = jnp.where(u_index == target + step_a, 1.0, 0.0)
        columns[:, j * LANES : (j + 1) * LANES] = hot.astype(bf16)
    v_index = v_steps()
    unrolled = min(32, sources)

    def spread_some(i, _):
        for j in range(unrolled):
            source = i * unrolled + j
            for slot in range(CAP):
                wide = along_v(arrived, places, source, slot, v_index).astype(bf16)
                at = pl.ds(pl.multiple_of((source * CAP + slot) * SG, SG), SG)
                for comp, start in parts():
                    spread[at, comp * BAND_V : (comp + 1) * BAND_V] = wide[start : start + SG]
        return 0

    lax.fori_loop(0, sources // unrolled, spread_some, 0)
    copies = []
    for comp in range(COMPS):
        result[comp] = jnp.dot(
            columns[...], spread[:, comp * BAND_V : (comp + 1) * BAND_V], preferred_element_type=f32
        )
        copies.append(pltpu.make_async_copy(result.at[comp], out_ref.at[comp], sems.at[comp]))
        copies[-1].start()
    for copy in copies:
        copy.wait()


def tile_of(arrived):
    cells = arrived.shape[0] * CAP * SG
    return pl.pallas_call(
        tile_kernel,
        out_shape=jax.ShapeDtypeStruct((COMPS, TILE_W, BAND_V), f32),
        in_specs=[vmem()],
        out_specs=pl.BlockSpec(memory_space=pl.ANY),
        scratch_shapes=[
            pltpu.VMEM((TILE_W, cells), bf16),
            pltpu.VMEM((cells, COMPS * BAND_V), bf16),
            pltpu.VMEM((arrived.shape[0], POS_ROWS, LANES), f32),
            pltpu.VMEM((COMPS, TILE_W, BAND_V), f32),
            pltpu.SemaphoreType.DMA((COMPS,)),
        ],
        compiler_params=pltpu.CompilerParams(vmem_limit_bytes=(10 << 20) + 2 * cells * (COMPS * BAND_V + 2 * TILE_W)),
        cost_estimate=pl.CostEstimate(flops=4 * 10**9, bytes_accessed=4 << 20, transcendentals=0),
        name="tile",
    )(arrived)


def on_device(
    visibilities, uv_rows, chan_scale, valid_rows, aterm, taper, stations, owner, u_offset, v_start
):
    groups_n = lax.axis_size("freq")
    devices_n = groups_n * lax.axis_size("tile")
    me = lax.axis_index("freq")[None].astype(jnp.int32)
    far = list(range(groups_n - 1, 1, -1))
    near = [k for k in (1, 0) if k < groups_n]
    stations, owner, u_offset, v_start = (
        jnp.swapaxes(index, 2, 3) for index in (stations, owner, u_offset, v_start)
    )
    chunks = {}

    def make(ks, gain_args=()):
        made = images(ks, me, valid_rows, chan_scale, visibilities[0], uv_rows, gain_args)
        for k, part in zip(ks, made):
            if k:
                part = lax.ppermute(part, "freq", [(i, i ^ k) for i in range(groups_n)])
            chunks[k] = part
        return made[-1]

    if far:
        make(far)
    gain = make(near, (stations, aterm, taper))
    outgoing = subgrids(
        [chunks[k] for k in range(groups_n)], me, owner, u_offset, v_start, gain, devices_n
    )
    arrived = lax.all_to_all(
        outgoing, ("freq", "tile"), split_axis=0, concat_axis=0, tiled=True
    )
    incoming = lax.ppermute(
        margin_of(arrived), ("freq", "tile"), [(i, (i + 1) % devices_n) for i in range(devices_n)]
    )
    return tile_of(arrived).at[:, :SG, :].add(incoming.astype(f32))


def solution(mesh):
    in_specs = (
        P("tile", None, None, "freq"),
        P("tile", None, "freq"),
        P(),
        P("tile", "freq"),
        P("freq", None, None, None),
        P(),
        P("tile", "freq", None, None),
        P("tile", "freq", None, None),
        P("tile", "freq", None, None),
        P("tile", "freq", None, None),
    )
    out_specs = P(None, ("freq", "tile"), None)
    return jax.shard_map(
        on_device, mesh=mesh, in_specs=in_specs, out_specs=out_specs, check_vma=False
    )
```

```python
import functools
import math

import jax
import jax.numpy as jnp
import ml_dtypes
import numpy as np
from jax import lax
from jax.experimental import pallas as pl
from jax.experimental.pallas import tpu as pltpu
from jax.sharding import PartitionSpec as P

SG = 32
HALF = SG // 2
TSTEP = 128
CHAN_G = 16
FAN = CHAN_G * TSTEP
TILE_W = 256
BAND_V = 256
LANES = 128
COMPS = 8
POL = 4
POS_ROWS = 8
NO_PLACE = 512.0
COARSE = (4, 12)
FINE = 4
SUMS = 2 * (FINE + 1) * COMPS
CAP = 2
U_STEP = SG + 3
V_STEP = 13
W_STEP = CHAN_G + 1
VMEM_LIMIT = 60 << 20
f32 = jnp.float32
bf16 = jnp.bfloat16


def vmem():
    return pl.BlockSpec(memory_space=pltpu.VMEM)


def smem():
    return pl.BlockSpec(memory_space=pltpu.SMEM)


IMAGE_ROWS = np.array([HALF + i for i in range(HALF)] + [0] + [HALF - i for i in range(1, HALF)])


def split(matrix):
    high = matrix.astype(np.float32).astype(ml_dtypes.bfloat16)
    low = (matrix - high.astype(np.float64)).astype(np.float32).astype(ml_dtypes.bfloat16)
    return high, low


def fourier():
    cells = np.arange(SG) - HALF
    angles = (cells[:, None] * cells[None, :] % SG) * (2.0 * math.pi / SG)
    return np.cos(angles), -np.sin(angles)


def lane_transform():
    cos, sin = fourier()
    table = np.zeros((2, 2, 2, SG, 2, 2, 2, SG))
    for p in range(2):
        y_re = {(0, 0): cos, (1, 1): -cos, (1, 0): -sin, (0, 1): -sin}
        y_im = {(0, 0): sin, (1, 1): -sin, (1, 0): cos, (0, 1): cos}
        for gain in range(2):
            for part in range(2):
                re, im = y_re[gain, part].T, y_im[gain, part].T
                table[gain, p, part, :, 0, p, 0, :] = re
                table[gain, p, part, :, 0, p, 1, :] = im
                table[gain, p, part, :, 1, p, 0, :] = -im
                table[gain, p, part, :, 1, p, 1, :] = re
    return split(table.reshape(256, 256))


def row_transform():
    cos, sin = fourier()
    high, low = split(np.concatenate([cos[:, IMAGE_ROWS], sin[:, IMAGE_ROWS]], 1))
    return np.concatenate([high, high, low], 1)


def combine_table():
    table = np.zeros((4, 2, LANES, 2, 2, 2, SG))
    for m in range(SG):
        for a, coarse in enumerate((COARSE[0], -COARSE[0], COARSE[1], -COARSE[1])):
            b = m - HALF - coarse
            if not -FINE <= b < FINE:
                continue
            size, sign = abs(b), 1 if b > 0 else -1
            for p in range(POL):
                re, im = table[a, :, :, p // 2, p % 2, 0, m], table[a, :, :, p // 2, p % 2, 1, m]
                at = 2 * FINE * COMPS if b == 0 else (size - 1) * COMPS
                re[0, at + p], im[0, at + POL + p] = 1, 1
                re[1, at + POL + p], im[1, at + p] = -1, 1
                if b:
                    at += FINE * COMPS
                    re[0, at + POL + p], im[0, at + p] = -sign, sign
                    re[1, at + p], im[1, at + POL + p] = -sign, -sign
    return table.reshape(8 * LANES, 2 * LANES).astype(ml_dtypes.bfloat16)


def lane_tiles():
    table = np.zeros((POL, SG, POL, POL, SG))
    for q in range(POL):
        for copy in range(POL):
            table[q, :, q, copy, :] = np.eye(SG)
    table = table.reshape(LANES, POL * LANES)
    return np.concatenate([table] * 3, 0).astype(ml_dtypes.bfloat16)


def unit_powers(theta, wanted):
    half = theta * 0.5
    square = half * half
    sin_h = half * (
        1.0 + square * (-1.0 / 6 + square * (1.0 / 120 + square * (-1.0 / 5040 + square * (1.0 / 362880))))
    )
    cos_h = 1.0 + square * (
        -0.5 + square * (1.0 / 24 + square * (-1.0 / 720 + square * (1.0 / 40320 + square * (-1.0 / 3628800))))
    )
    powers = {0: (jnp.ones_like(theta), jnp.zeros_like(theta))}
    powers[1] = (1.0 - 2.0 * sin_h * sin_h, 2.0 * sin_h * cos_h)
    for n in wanted:
        if n in powers:
            continue
        first = n // 2 if n != 12 else 4
        (ca, sa), (cb, sb) = powers[first], powers[n - first]
        if 2 * first == n:
            powers[n] = (1.0 - 2.0 * sa * sa, 2.0 * sa * ca)
        else:
            powers[n] = (ca * cb - sa * sb, ca * sb + sa * cb)
    return powers


def gain_copies(stations, aterm, rows, sems):
    count = rows.shape[0] // 2
    return [
        pltpu.make_async_copy(
            aterm.at[0, stations[0, 0, i // count, i % count]],
            rows.at[i, :, pl.ds(0, SG * SG)],
            sems.at[i],
        )
        for i in range(2 * count)
    ]


def make_gains(taper, tiles, out_ref, rows):
    count = rows.shape[0] // 2
    blocks = SG * SG // LANES
    parts = []
    for r in range(blocks):
        cols = pl.ds(r * LANES, LANES)
        one_re, one_im = rows[0:count, 0, cols], rows[0:count, 1, cols]
        two_re, two_im = rows[count:, 0, cols], rows[count:, 1, cols]
        shape = jnp.concatenate(
            [taper[POL * r + q : POL * r + q + 1, :] for q in range(POL)], 1
        ) * (1.0 / (math.sqrt(FAN) * SG))
        gain = jnp.concatenate(
            [(one_re * two_re + one_im * two_im) * shape, (one_im * two_re - one_re * two_im) * shape], 0
        )
        high = gain.astype(bf16)
        rest = gain - high.astype(f32)
        mid = rest.astype(bf16)
        low = (rest - mid.astype(f32)).astype(bf16)
        parts.append(jnp.concatenate([high, mid, low], 1))
    tiled = jnp.dot(jnp.concatenate(parts, 0), tiles[...], preferred_element_type=f32)
    for r in range(blocks):
        for q in range(POL):
            row = list(IMAGE_ROWS).index(POL * r + q)
            for part in range(2):
                at = (2 * r + part) * count
                out_ref[part, row] = tiled[at : at + count, q * LANES : (q + 1) * LANES]


def image_kernel(ks, with_gains, me, valid, scales, *refs):
    refs = list(refs)
    take = lambda count: [refs.pop(0) for _ in range(count)]
    stations = take(1)[0] if with_gains else None
    vis_ref, uv_ref, combine = take(3)
    aterm, taper, tiles = take(3) if with_gains else (None, None, None)
    outs = take(len(ks))
    gain_ref = take(1)[0] if with_gains else None
    u_tabs, v_tabs, w_tabs, scale_tab, x_high, x_low = take(6)
    turn = pl.program_id(0)
    copies = gain_copies(stations, aterm, *refs) if with_gains else []

    @pl.when(turn == 0)
    def _():
        for copy in copies:
            copy.start()

    lane = lax.broadcasted_iota(jnp.int32, (CHAN_G, TSTEP), 1)
    first_row = lax.broadcasted_iota(jnp.int32, (HALF, LANES), 0) == 0

    def build(s, scale):
        u_tab, v_tab, w_tab = u_tabs.at[s % 2], v_tabs.at[s % 2], w_tabs.at[s % 2]
        part = pl.ds(s * TSTEP, TSTEP)
        live = lane + s * TSTEP < valid[0, 0]
        for c in range(COMPS):
            values = vis_ref[c, :, part].astype(f32)
            w_tab[pl.ds(c * W_STEP, CHAN_G), :] = jnp.where(live, values, 0.0)
        powers = unit_powers(uv_ref[0, 0:1, part] * scale, range(HALF + 1))
        for n in range(HALF):
            u_tab[pl.ds(n, CHAN_G, U_STEP), :] = powers[n][0]
            u_tab[pl.ds(HALF + n, CHAN_G, U_STEP), :] = powers[n][1]
        u_tab[pl.ds(SG, CHAN_G, U_STEP), :] = powers[HALF][0]
        u_tab[pl.ds(SG + 1, CHAN_G, U_STEP), :] = powers[HALF][1]
        powers = unit_powers(uv_ref[0, 1:2, part] * scale, (1, 2, 3, 4, 8, 12))
        for q, n in enumerate(COARSE):
            v_tab[pl.ds(2 * q, CHAN_G, V_STEP), :] = powers[n][0]
            v_tab[pl.ds(2 * q + 1, CHAN_G, V_STEP), :] = powers[n][1]
        for n in range(1, FINE + 1):
            v_tab[pl.ds(3 + n, CHAN_G, V_STEP), :] = powers[n][0]
            v_tab[pl.ds(3 + FINE + n, CHAN_G, V_STEP), :] = powers[n][1]
        sums = None
        step = 4
        pad = jnp.zeros((COMPS, TSTEP), f32)
        for start in range(0, CHAN_G, step):
            left, right = [], []
            for h in range(start, start + step):
                u_rows = u_tab[pl.ds(h * U_STEP, SG), :]
                column = [
                    (u_rows * v_tab[pl.ds(h * V_STEP + a, 1), :]).astype(bf16) for a in range(4)
                ]
                coarse = v_tab[pl.ds(h * V_STEP, 4), :]
                last = [coarse * u_tab[pl.ds(h * U_STEP + SG + i, 1), :] for i in range(2)]
                column.append(jnp.concatenate(last + [pad], 0).astype(bf16))
                left.append(jnp.concatenate(column, 0))
                w_all = w_tab[pl.ds(h, COMPS, W_STEP), :]
                fine = [w_all * v_tab[pl.ds(h * V_STEP + 4 + b, 1), :] for b in range(2 * FINE)]
                right.append(jnp.concatenate(fine + [w_all, pad], 0).astype(bf16))
            term = lax.dot_general(
                jnp.concatenate(left, 1),
                jnp.concatenate(right, 1),
                (((1,), (1,)), ((), ())),
                preferred_element_type=f32,
            )
            sums = term if sums is None else sums + term
        return sums

    def keep(s, sums):
        top = 4 * SG
        sums = jnp.concatenate([sums, jnp.zeros((sums.shape[0], LANES - SUMS), f32)], 1)
        for q in range(2):
            cos, sin = sums[2 * q * SG : (2 * q + 1) * SG], sums[(2 * q + 1) * SG : (2 * q + 2) * SG]
            cc, sc, cs, ss = cos[:HALF], cos[HALF:], sin[:HALF], sin[HALF:]
            ends = [sums[top + e : top + e + 1] for e in (2 * q, 4 + 2 * q, 2 * q + 1, 5 + 2 * q)]
            ecc, esc, ecs, ess = [jnp.where(first_row, e, x) for e, x in zip(ends, (cc, sc, cs, ss))]
            for d, (zero, one) in enumerate(
                (
                    ((cc - ss, ecc + ess), (sc + cs, ecs - esc)),
                    ((cc + ss, ecc - ess), (sc - cs, -esc - ecs)),
                )
            ):
                for x, values in enumerate((zero, one)):
                    both = jnp.concatenate(values, 0)
                    high = both.astype(bf16)
                    at = ((2 * q + d) * 2 + x) * LANES
                    x_high[s * SG : (s + 1) * SG, at : at + LANES] = high
                    x_low[s * SG : (s + 1) * SG, at : at + LANES] = (both - high.astype(f32)).astype(bf16)

    group = me[0] ^ (ks[0] - turn)
    for h in range(CHAN_G):
        scale_tab[h : h + 1, :] = jnp.full((1, LANES), scales[group * CHAN_G + h], f32)
    scale = scale_tab[...] * (2.0 * math.pi / SG)
    count = outs[0].shape[0]
    for s in range(count):
        keep(s, build(s, scale))
    image = (
        jnp.dot(x_high[...], combine[...], preferred_element_type=f32)
        + jnp.dot(x_low[...], combine[...], preferred_element_type=f32)
    ).astype(bf16)

    def write(out_ref):
        for s in range(count):
            for pair in range(2):
                out_ref[s, pair * SG : (pair + 1) * SG, :] = image[
                    s * SG : (s + 1) * SG, pair * LANES : (pair + 1) * LANES
                ]

    for i, out_ref in enumerate(outs):
        pl.when(turn == i)(functools.partial(write, out_ref))

    if with_gains:

        @pl.when(turn == len(ks) - 1)
        def _():
            for copy in copies:
                copy.wait()
            make_gains(taper, tiles, gain_ref, refs[0])


def images(ks, me, valid, scales, vis, uv, gain_args=()):
    rows = vis.shape[2]
    count = rows // TSTEP
    block = (COMPS, CHAN_G, rows)
    whole = pl.BlockSpec((count, 2 * SG, LANES), lambda i, at: (0, 0, 0))
    out_shape = [jax.ShapeDtypeStruct((count, 2 * SG, LANES), bf16)] * len(ks)
    out_specs = [whole] * len(ks)
    in_specs = [pl.BlockSpec(block, lambda i, at: (0, at[0] ^ (ks[0] - i), 0))]
    table = combine_table()
    in_specs += [
        pl.BlockSpec((1, 2, rows), lambda i, at: (0, 0, 0)),
        pl.BlockSpec(table.shape, lambda i, at: (0, 0)),
    ]
    scratch = [
        pltpu.VMEM((2, CHAN_G * U_STEP, LANES), f32),
        pltpu.VMEM((2, CHAN_G * V_STEP, LANES), f32),
        pltpu.VMEM((2, COMPS * W_STEP, LANES), f32),
        pltpu.VMEM((CHAN_G, LANES), f32),
        pltpu.VMEM((count * SG, 8 * LANES), bf16),
        pltpu.VMEM((count * SG, 8 * LANES), bf16),
    ]
    operands = [vis, uv, table]
    if gain_args:
        stations, aterm, taper = gain_args
        subs = stations.shape[3]
        tiles = lane_tiles()
        operands = [stations] + operands + [aterm, taper, tiles]
        in_specs = [smem()] + in_specs + [
            pl.BlockSpec(memory_space=pltpu.HBM),
            pl.BlockSpec(taper.shape, lambda i, at: (0, 0)),
            pl.BlockSpec(tiles.shape, lambda i, at: (0, 0)),
        ]
        out_shape += [jax.ShapeDtypeStruct((2, SG, subs, LANES), f32)]
        out_specs += [pl.BlockSpec((2, SG, subs, LANES), lambda i, at: (0, 0, 0, 0))]
        scratch += [pltpu.VMEM((2 * subs, 2, SG * SG + LANES), f32), pltpu.SemaphoreType.DMA((2 * subs,))]
    return pl.pallas_call(
        functools.partial(image_kernel, ks, bool(gain_args)),
        out_shape=out_shape,
        grid_spec=pltpu.PrefetchScalarGridSpec(
            num_scalar_prefetch=1,
            grid=(len(ks),),
            in_specs=[smem(), smem()] + in_specs,
            out_specs=out_specs,
            scratch_shapes=scratch,
        ),
        compiler_params=pltpu.CompilerParams(vmem_limit_bytes=(48 << 20) if gain_args else VMEM_LIMIT),
        cost_estimate=pl.CostEstimate(
            flops=len(ks) * count * FAN * 40000, bytes_accessed=1 << 20, transcendentals=0
        ),
        name="images",
    )(me, valid, scales, *operands)


def subgrid_kernel(chunks_n, me, owner, u_offset, v_start, gain, w_high, w_low, f_rows, *refs):
    chunks = refs[:chunks_n]
    out_ref, d_high, d_low, y_ref, pos, taken = refs[chunks_n:]
    block = chunks[0].shape[0]
    row = lax.broadcasted_iota(jnp.int32, (POS_ROWS, LANES), 0)

    def clear(i, _):
        taken[i] = 0
        return 0

    lax.fori_loop(0, taken.shape[0], clear, 0, unroll=8)
    out_ref[...] = jnp.zeros_like(out_ref)
    pos[...] = jnp.full(pos.shape, NO_PLACE, f32)
    for k in range(chunks_n):
        base = (me[0] ^ k) * block
        for i in range(block):
            gain_re, gain_im = gain[0, :, base + i, :], gain[1, :, base + i, :]
            for pair in range(2):
                image = chunks[k][i, pair * SG : (pair + 1) * SG, :].astype(f32)
                both = jnp.concatenate([image * gain_re, image * gain_im], 1)
                high = both.astype(bf16)
                at = pl.ds(((k * block + i) * 2 + pair) * SG, SG)
                d_high[at, :] = high
                d_low[at, :] = (both - high.astype(f32)).astype(bf16)
    step = 256
    for i in range(d_high.shape[0] // step):
        at = pl.ds(i * step, step)
        high = d_high[at, :]
        y_ref[at, :] = (
            jnp.dot(high, w_high[...], preferred_element_type=f32)
            + jnp.dot(d_low[at, :], w_high[...], preferred_element_type=f32)
            + jnp.dot(high, w_low[...], preferred_element_type=f32)
        )
    for k in range(chunks_n):
        base = (me[0] ^ k) * block
        for i in range(block):
            at = (k * block + i) * 2 * SG
            ys = [y_ref[pl.ds(at + pair * SG, SG), :] for pair in range(2)]
            rows = jnp.concatenate(
                [
                    jnp.concatenate([y[:, :LANES] for y in ys], 1),
                    jnp.concatenate([y[:, LANES:] for y in ys], 1),
                ],
                0,
            )
            high = rows.astype(bf16)
            low = (rows - high.astype(f32)).astype(bf16)
            cells = jnp.dot(
                f_rows[...], jnp.concatenate([high, low, high], 0), preferred_element_type=f32
            ).astype(bf16)
            s = base + i
            dest = owner[0, 0, 0, s]
            slot = jnp.minimum(taken[dest], CAP - 1)
            taken[dest] = slot + 1
            for pair in range(2):
                start = pl.multiple_of((slot * 2 + pair) * SG, SG)
                out_ref[dest, pl.ds(start, SG), :] = cells[:, pair * LANES : (pair + 1) * LANES]
            u, v = u_offset[0, 0, 0, s].astype(f32), v_start[0, 0, 0, s].astype(f32)
            pos[dest] = jnp.where(row == 2 * slot, u, jnp.where(row == 2 * slot + 1, v, pos[dest]))
    out_ref[:, CAP * 2 * SG :, :] = pos[...].astype(bf16)


def subgrids(chunks, me, owner, u_offset, v_start, gain, devices_n):
    count = owner.shape[3]
    return pl.pallas_call(
        functools.partial(subgrid_kernel, len(chunks)),
        out_shape=jax.ShapeDtypeStruct((devices_n, CAP * 2 * SG + POS_ROWS, LANES), bf16),
        in_specs=[smem()] * 4 + [vmem()] * (4 + len(chunks)),
        out_specs=vmem(),
        scratch_shapes=[
            pltpu.VMEM((count * 2 * SG, 2 * LANES), bf16),
            pltpu.VMEM((count * 2 * SG, 2 * LANES), bf16),
            pltpu.VMEM((count * 2 * SG, 2 * LANES), f32),
            pltpu.VMEM((devices_n, POS_ROWS, LANES), f32),
            pltpu.SMEM((devices_n,), jnp.int32),
        ],
        compiler_params=pltpu.CompilerParams(vmem_limit_bytes=24 << 20),
        cost_estimate=pl.CostEstimate(flops=4 * 10**9, bytes_accessed=4 << 20, transcendentals=0),
        name="subgrids",
    )(me, owner, u_offset, v_start, gain, *lane_transform(), row_transform(), *chunks)


def along_v(arrived, places, source, slot, v_index):
    cells = arrived[source, pl.ds(slot * 2 * SG, 2 * SG), :]
    stacked = jnp.concatenate([cells[:, SG * k : SG * (k + 1)] for k in range(POL)], 0)
    v = places[source, pl.ds(2 * slot + 1, 1), :]
    hot = jnp.where(v_index == jnp.concatenate([v, v], 1), 1.0, 0.0).astype(bf16)
    return jnp.dot(stacked, hot, preferred_element_type=f32)


def v_steps():
    rows = lax.broadcasted_iota(jnp.int32, (SG, BAND_V), 0)
    return (lax.broadcasted_iota(jnp.int32, (SG, BAND_V), 1) - rows).astype(f32)


def parts():
    return [
        ((k % 2) * POL + pair * 2 + k // 2, (k * 2 + pair) * SG) for k in range(POL) for pair in range(2)
    ]


def margin_kernel(arrived, out_ref, acc, places, chosen, starts):
    sources = arrived.shape[0]
    batch = 4
    first = TILE_W - SG
    acc[...] = jnp.zeros_like(acc)
    places[...] = arrived[:, CAP * 2 * SG :, :].astype(f32)
    found = jnp.int32(0)
    for source in range(sources):
        for slot in range(CAP):
            u = places[source, 2 * slot, 0].astype(jnp.int32)
            chosen[found] = source * CAP + slot
            starts[found] = u - first
            found = found + ((u > first) & (u < TILE_W)).astype(jnp.int32)
    for i in range(batch):
        chosen[found + i] = 0
        starts[found + i] = 2 * SG
    v_index = v_steps()

    def add(i, _):
        wide = []
        for j in range(batch):
            at = chosen[i * batch + j]
            wide.append(along_v(arrived, places, at // CAP, at % CAP, v_index))
        for j in range(batch):
            rows = pl.ds(starts[i * batch + j], SG)
            for comp, start in parts():
                for side in range(BAND_V // LANES):
                    acc[comp, side, rows, :] += wide[j][
                        start : start + SG, side * LANES : (side + 1) * LANES
                    ]
        return 0

    lax.fori_loop(0, (found + batch - 1) // batch, add, 0)
    for side in range(BAND_V // LANES):
        out_ref[:, :, side * LANES : (side + 1) * LANES] = acc[:, side, SG : 2 * SG, :].astype(bf16)


def margin_of(arrived):
    slots = arrived.shape[0] * CAP
    return pl.pallas_call(
        margin_kernel,
        out_shape=jax.ShapeDtypeStruct((COMPS, SG, BAND_V), bf16),
        in_specs=[vmem()],
        out_specs=vmem(),
        scratch_shapes=[
            pltpu.VMEM((COMPS, BAND_V // LANES, 3 * SG, LANES), f32),
            pltpu.VMEM((arrived.shape[0], POS_ROWS, LANES), f32),
            pltpu.SMEM((slots + 4,), jnp.int32),
            pltpu.SMEM((slots + 4,), jnp.int32),
        ],
        compiler_params=pltpu.CompilerParams(vmem_limit_bytes=16 << 20),
        name="margin",
    )(arrived)


def tile_kernel(arrived, out_ref, columns, spread, places, result, sems):
    sources = arrived.shape[0]
    per_lanes = LANES // SG
    places[...] = arrived[:, CAP * 2 * SG :, :].astype(f32)
    lane = lax.broadcasted_iota(jnp.int32, (1, LANES), 1)
    u_index = lax.broadcasted_iota(jnp.int32, (TILE_W, LANES), 0).astype(f32)
    step_a = (lane % SG).astype(f32)
    for j in range(sources * CAP // per_lanes):
        target = None
        for q in range(per_lanes):
            slot = j * per_lanes + q
            u = places[slot // CAP, 2 * (slot % CAP) : 2 * (slot % CAP) + 1, :]
            target = u if target is None else jnp.where(lane < q * SG, target, u)
        hot = jnp.where(u_index == target + step_a, 1.0, 0.0)
        columns[:, j * LANES : (j + 1) * LANES] = hot.astype(bf16)
    v_index = v_steps()
    unrolled = min(32, sources)

    def spread_some(i, _):
        for j in range(unrolled):
            source = i * unrolled + j
            for slot in range(CAP):
                wide = along_v(arrived, places, source, slot, v_index).astype(bf16)
                at = pl.ds(pl.multiple_of((source * CAP + slot) * SG, SG), SG)
                for comp, start in parts():
                    spread[at, comp * BAND_V : (comp + 1) * BAND_V] = wide[start : start + SG]
        return 0

    lax.fori_loop(0, sources // unrolled, spread_some, 0)
    copies = []
    for comp in range(COMPS):
        result[comp] = jnp.dot(
            columns[...], spread[:, comp * BAND_V : (comp + 1) * BAND_V], preferred_element_type=f32
        )
        copies.append(pltpu.make_async_copy(result.at[comp], out_ref.at[comp], sems.at[comp]))
        copies[-1].start()
    for copy in copies:
        copy.wait()


def tile_of(arrived):
    cells = arrived.shape[0] * CAP * SG
    return pl.pallas_call(
        tile_kernel,
        out_shape=jax.ShapeDtypeStruct((COMPS, TILE_W, BAND_V), f32),
        in_specs=[vmem()],
        out_specs=pl.BlockSpec(memory_space=pl.ANY),
        scratch_shapes=[
            pltpu.VMEM((TILE_W, cells), bf16),
            pltpu.VMEM((cells, COMPS * BAND_V), bf16),
            pltpu.VMEM((arrived.shape[0], POS_ROWS, LANES), f32),
            pltpu.VMEM((COMPS, TILE_W, BAND_V), f32),
            pltpu.SemaphoreType.DMA((COMPS,)),
        ],
        compiler_params=pltpu.CompilerParams(vmem_limit_bytes=(10 << 20) + 2 * cells * (COMPS * BAND_V + 2 * TILE_W)),
        cost_estimate=pl.CostEstimate(flops=4 * 10**9, bytes_accessed=4 << 20, transcendentals=0),
        name="tile",
    )(arrived)


def on_device(
    visibilities, uv_rows, chan_scale, valid_rows, aterm, taper, stations, owner, u_offset, v_start
):
    groups_n = lax.axis_size("freq")
    devices_n = groups_n * lax.axis_size("tile")
    me = lax.axis_index("freq")[None].astype(jnp.int32)
    far = list(range(groups_n - 1, 1, -1))
    near = [k for k in (1, 0) if k < groups_n]
    stations, owner, u_offset, v_start = (
        jnp.swapaxes(index, 2, 3) for index in (stations, owner, u_offset, v_start)
    )
    chunks = {}

    def make(ks, gain_args=()):
        made = images(ks, me, valid_rows, chan_scale, visibilities[0], uv_rows, gain_args)
        for k, part in zip(ks, made):
            if k:
                part = lax.ppermute(part, "freq", [(i, i ^ k) for i in range(groups_n)])
            chunks[k] = part
        return made[-1]

    if far:
        make(far)
    gain = make(near, (stations, aterm, taper))
    outgoing = subgrids(
        [chunks[k] for k in range(groups_n)], me, owner, u_offset, v_start, gain, devices_n
    )
    arrived = lax.all_to_all(
        outgoing, ("freq", "tile"), split_axis=0, concat_axis=0, tiled=True
    )
    incoming = lax.ppermute(
        margin_of(arrived), ("freq", "tile"), [(i, (i + 1) % devices_n) for i in range(devices_n)]
    )
    return tile_of(arrived).at[:, :SG, :].add(incoming.astype(f32))


def solution(mesh):
    in_specs = (
        P("tile", None, None, "freq"),
        P("tile", None, "freq"),
        P(),
        P("tile", "freq"),
        P("freq", None, None, None),
        P(),
        P("tile", "freq", None, None),
        P("tile", "freq", None, None),
        P("tile", "freq", None, None),
        P("tile", "freq", None, None),
    )
    out_specs = P(None, ("freq", "tile"), None)
    return jax.shard_map(
        on_device, mesh=mesh, in_specs=in_specs, out_specs=out_specs, check_vma=False
    )
```

```python
import functools
import math

import jax
import jax.numpy as jnp
import ml_dtypes
import numpy as np
from jax import lax
from jax.experimental import pallas as pl
from jax.experimental.pallas import tpu as pltpu
from jax.sharding import PartitionSpec as P

SG = 32
HALF = SG // 2
TSTEP = 128
CHAN_G = 16
FAN = CHAN_G * TSTEP
TILE_W = 256
BAND_V = 256
LANES = 128
COMPS = 8
POL = 4
POS_ROWS = 8
NO_PLACE = 512.0
COARSE = (4, 12)
FINE = 4
SUMS = 2 * FINE * COMPS
CAP = 2
U_STEP = SG + 1
V_STEP = 13
W_STEP = CHAN_G + 1
VMEM_LIMIT = 60 << 20
f32 = jnp.float32
bf16 = jnp.bfloat16


def vmem():
    return pl.BlockSpec(memory_space=pltpu.VMEM)


def smem():
    return pl.BlockSpec(memory_space=pltpu.SMEM)


IMAGE_ROWS = np.array([HALF + i for i in range(HALF)] + [HALF - 1 - i for i in range(HALF)])


def split(matrix):
    high = matrix.astype(np.float32).astype(ml_dtypes.bfloat16)
    low = (matrix - high.astype(np.float64)).astype(np.float32).astype(ml_dtypes.bfloat16)
    return high, low


def fourier():
    cells = np.arange(SG) - HALF
    angles = (cells[:, None] * cells[None, :] % SG) * (2.0 * math.pi / SG)
    return np.cos(angles), -np.sin(angles)


def lane_transform():
    cos, sin = fourier()
    table = np.zeros((2, 2, 2, SG, 2, 2, 2, SG))
    for p in range(2):
        y_re = {(0, 0): cos, (1, 1): -cos, (1, 0): -sin, (0, 1): -sin}
        y_im = {(0, 0): sin, (1, 1): -sin, (1, 0): cos, (0, 1): cos}
        for gain in range(2):
            for part in range(2):
                re, im = y_re[gain, part].T, y_im[gain, part].T
                table[gain, p, part, :, 0, p, 0, :] = re
                table[gain, p, part, :, 0, p, 1, :] = im
                table[gain, p, part, :, 1, p, 0, :] = -im
                table[gain, p, part, :, 1, p, 1, :] = re
    return split(table.reshape(256, 256))


def row_transform():
    cos, sin = fourier()
    high, low = split(np.concatenate([cos[:, IMAGE_ROWS], sin[:, IMAGE_ROWS]], 1))
    return np.concatenate([high, high, low], 1)


def combine_table():
    table = np.zeros((4, 2, SUMS, 2, 2, 2, SG))
    for m in range(SG):
        for a, coarse in enumerate((COARSE[0], -COARSE[0], COARSE[1], -COARSE[1])):
            b = m - HALF + 0.5 - coarse
            if abs(b) > FINE:
                continue
            size, sign = int(abs(b)), 1 if b > 0 else -1
            for p in range(POL):
                re, im = table[a, :, :, p // 2, p % 2, 0, m], table[a, :, :, p // 2, p % 2, 1, m]
                at = size * COMPS
                re[0, at + p], im[0, at + POL + p] = 1, 1
                re[1, at + POL + p], im[1, at + p] = -1, 1
                at += FINE * COMPS
                re[0, at + POL + p], im[0, at + p] = -sign, sign
                re[1, at + p], im[1, at + POL + p] = -sign, -sign
    return table.reshape(4 * LANES, 2 * LANES).astype(ml_dtypes.bfloat16)


def lane_tiles():
    table = np.zeros((POL, SG, POL, POL, SG))
    for q in range(POL):
        for copy in range(POL):
            table[q, :, q, copy, :] = np.eye(SG)
    table = table.reshape(LANES, POL * LANES)
    return np.concatenate([table] * 3, 0).astype(ml_dtypes.bfloat16)


def times(one, two):
    return one[0] * two[0] - one[1] * two[1], one[0] * two[1] + one[1] * two[0]


def squared(one):
    return 1.0 - 2.0 * one[1] * one[1], 2.0 * one[1] * one[0]


def half_angle(theta):
    half = theta * 0.5
    square = half * half
    sin = half * (
        1.0 + square * (-1.0 / 6 + square * (1.0 / 120 + square * (-1.0 / 5040 + square * (1.0 / 362880))))
    )
    cos = 1.0 + square * (
        -0.5 + square * (1.0 / 24 + square * (-1.0 / 720 + square * (1.0 / 40320 + square * (-1.0 / 3628800))))
    )
    return cos, sin


def odd_halves(half, count):
    values, steps = [half], [squared(half)]
    while len(values) < count:
        values += [times(value, steps[-1]) for value in values]
        steps.append(squared(steps[-1]))
    return values, steps


def gain_copies(stations, aterm, rows, sems):
    count = rows.shape[0] // 2
    return [
        pltpu.make_async_copy(
            aterm.at[0, stations[0, 0, i // count, i % count]],
            rows.at[i, :, pl.ds(0, SG * SG)],
            sems.at[i],
        )
        for i in range(2 * count)
    ]


def make_gains(taper, tiles, out_ref, rows):
    count = rows.shape[0] // 2
    blocks = SG * SG // LANES
    parts = []
    for r in range(blocks):
        cols = pl.ds(r * LANES, LANES)
        one_re, one_im = rows[0:count, 0, cols], rows[0:count, 1, cols]
        two_re, two_im = rows[count:, 0, cols], rows[count:, 1, cols]
        shape = jnp.concatenate(
            [taper[POL * r + q : POL * r + q + 1, :] for q in range(POL)], 1
        ) * (1.0 / (math.sqrt(FAN) * SG))
        gain = jnp.concatenate(
            [(one_re * two_re + one_im * two_im) * shape, (one_im * two_re - one_re * two_im) * shape], 0
        )
        high = gain.astype(bf16)
        rest = gain - high.astype(f32)
        mid = rest.astype(bf16)
        low = (rest - mid.astype(f32)).astype(bf16)
        parts.append(jnp.concatenate([high, mid, low], 1))
    tiled = jnp.dot(jnp.concatenate(parts, 0), tiles[...], preferred_element_type=f32)
    for r in range(blocks):
        for q in range(POL):
            row = list(IMAGE_ROWS).index(POL * r + q)
            for part in range(2):
                at = (2 * r + part) * count
                out_ref[part, row] = tiled[at : at + count, q * LANES : (q + 1) * LANES]


def image_kernel(ks, with_gains, me, valid, scales, *refs):
    refs = list(refs)
    take = lambda count: [refs.pop(0) for _ in range(count)]
    stations = take(1)[0] if with_gains else None
    vis_ref, uv_ref, combine = take(3)
    aterm, taper, tiles = take(3) if with_gains else (None, None, None)
    outs = take(len(ks))
    gain_ref = take(1)[0] if with_gains else None
    u_tabs, v_tabs, w_tabs, scale_tab, x_high, x_low = take(6)
    turn = pl.program_id(0)
    copies = gain_copies(stations, aterm, *refs) if with_gains else []

    @pl.when(turn == 0)
    def _():
        for copy in copies:
            copy.start()

    lane = lax.broadcasted_iota(jnp.int32, (CHAN_G, TSTEP), 1)

    def build(s, scale):
        u_tab, v_tab, w_tab = u_tabs.at[s % 2], v_tabs.at[s % 2], w_tabs.at[s % 2]
        part = pl.ds(s * TSTEP, TSTEP)
        live = lane + s * TSTEP < valid[0, 0]
        parts = []
        for c in range(COMPS):
            values = vis_ref[c, :, part].astype(f32)
            parts.append(jnp.where(live, values, 0.0))
        u_half = half_angle(uv_ref[0, 0:1, part] * scale)
        v_half = half_angle(uv_ref[0, 1:2, part] * scale)
        cos, sin = times(u_half, v_half)
        for p in range(POL):
            re, im = parts[p], parts[POL + p]
            w_tab[pl.ds(p * W_STEP, CHAN_G), :] = re * cos + im * sin
            w_tab[pl.ds((POL + p) * W_STEP, CHAN_G), :] = im * cos - re * sin
        for n, value in enumerate(odd_halves(u_half, HALF)[0]):
            u_tab[pl.ds(n, CHAN_G, U_STEP), :] = value[0]
            u_tab[pl.ds(HALF + n, CHAN_G, U_STEP), :] = value[1]
        values, steps = odd_halves(v_half, FINE)
        for n, value in enumerate(values):
            v_tab[pl.ds(4 + n, CHAN_G, V_STEP), :] = value[0]
            v_tab[pl.ds(4 + FINE + n, CHAN_G, V_STEP), :] = value[1]
        for q, value in enumerate((steps[-1], times(steps[-1], squared(steps[-1])))):
            v_tab[pl.ds(2 * q, CHAN_G, V_STEP), :] = value[0]
            v_tab[pl.ds(2 * q + 1, CHAN_G, V_STEP), :] = value[1]
        sums = None
        step = 4
        for start in range(0, CHAN_G, step):
            left, right = [], []
            for h in range(start, start + step):
                u_rows = u_tab[pl.ds(h * U_STEP, SG), :]
                column = [
                    (u_rows * v_tab[pl.ds(h * V_STEP + a, 1), :]).astype(bf16) for a in range(4)
                ]
                left.append(jnp.concatenate(column, 0))
                w_all = w_tab[pl.ds(h, COMPS, W_STEP), :]
                fine = [w_all * v_tab[pl.ds(h * V_STEP + 4 + b, 1), :] for b in range(2 * FINE)]
                right.append(jnp.concatenate(fine, 0).astype(bf16))
            term = lax.dot_general(
                jnp.concatenate(left, 1),
                jnp.concatenate(right, 1),
                (((1,), (1,)), ((), ())),
                preferred_element_type=f32,
            )
            sums = term if sums is None else sums + term
        return sums

    def keep(s, sums):
        for q in range(2):
            cos, sin = sums[2 * q * SG : (2 * q + 1) * SG], sums[(2 * q + 1) * SG : (2 * q + 2) * SG]
            cc, sc, cs, ss = cos[:HALF], cos[HALF:], sin[:HALF], sin[HALF:]
            for d, (zero, one) in enumerate(
                (((cc - ss, cc + ss), (sc + cs, cs - sc)), ((cc + ss, cc - ss), (sc - cs, -sc - cs)))
            ):
                both = jnp.concatenate([jnp.concatenate(zero, 0), jnp.concatenate(one, 0)], 1)
                high = both.astype(bf16)
                at = (2 * q + d) * LANES
                x_high[s * SG : (s + 1) * SG, at : at + LANES] = high
                x_low[s * SG : (s + 1) * SG, at : at + LANES] = (both - high.astype(f32)).astype(bf16)

    group = me[0] ^ (ks[0] - turn)
    for h in range(CHAN_G):
        scale_tab[h : h + 1, :] = jnp.full((1, LANES), scales[group * CHAN_G + h], f32)
    scale = scale_tab[...] * (2.0 * math.pi / SG)
    count = outs[0].shape[0]
    for s in range(count):
        keep(s, build(s, scale))
    image = (
        jnp.dot(x_high[...], combine[...], preferred_element_type=f32)
        + jnp.dot(x_low[...], combine[...], preferred_element_type=f32)
    ).astype(bf16)

    def write(out_ref):
        for s in range(count):
            for pair in range(2):
                out_ref[s, pair * SG : (pair + 1) * SG, :] = image[
                    s * SG : (s + 1) * SG, pair * LANES : (pair + 1) * LANES
                ]

    for i, out_ref in enumerate(outs):
        pl.when(turn == i)(functools.partial(write, out_ref))

    if with_gains:

        @pl.when(turn == len(ks) - 1)
        def _():
            for copy in copies:
                copy.wait()
            make_gains(taper, tiles, gain_ref, refs[0])


def images(ks, me, valid, scales, vis, uv, gain_args=()):
    rows = vis.shape[2]
    count = rows // TSTEP
    block = (COMPS, CHAN_G, rows)
    whole = pl.BlockSpec((count, 2 * SG, LANES), lambda i, at: (0, 0, 0))
    out_shape = [jax.ShapeDtypeStruct((count, 2 * SG, LANES), bf16)] * len(ks)
    out_specs = [whole] * len(ks)
    in_specs = [pl.BlockSpec(block, lambda i, at: (0, at[0] ^ (ks[0] - i), 0))]
    table = combine_table()
    in_specs += [
        pl.BlockSpec((1, 2, rows), lambda i, at: (0, 0, 0)),
        pl.BlockSpec(table.shape, lambda i, at: (0, 0)),
    ]
    scratch = [
        pltpu.VMEM((2, CHAN_G * U_STEP, LANES), f32),
        pltpu.VMEM((2, CHAN_G * V_STEP, LANES), f32),
        pltpu.VMEM((2, COMPS * W_STEP, LANES), f32),
        pltpu.VMEM((CHAN_G, LANES), f32),
        pltpu.VMEM((count * SG, 4 * LANES), bf16),
        pltpu.VMEM((count * SG, 4 * LANES), bf16),
    ]
    operands = [vis, uv, table]
    if gain_args:
        stations, aterm, taper = gain_args
        subs = stations.shape[3]
        tiles = lane_tiles()
        operands = [stations] + operands + [aterm, taper, tiles]
        in_specs = [smem()] + in_specs + [
            pl.BlockSpec(memory_space=pltpu.HBM),
            pl.BlockSpec(taper.shape, lambda i, at: (0, 0)),
            pl.BlockSpec(tiles.shape, lambda i, at: (0, 0)),
        ]
        out_shape += [jax.ShapeDtypeStruct((2, SG, subs, LANES), f32)]
        out_specs += [pl.BlockSpec((2, SG, subs, LANES), lambda i, at: (0, 0, 0, 0))]
        scratch += [pltpu.VMEM((2 * subs, 2, SG * SG + LANES), f32), pltpu.SemaphoreType.DMA((2 * subs,))]
    return pl.pallas_call(
        functools.partial(image_kernel, ks, bool(gain_args)),
        out_shape=out_shape,
        grid_spec=pltpu.PrefetchScalarGridSpec(
            num_scalar_prefetch=1,
            grid=(len(ks),),
            in_specs=[smem(), smem()] + in_specs,
            out_specs=out_specs,
            scratch_shapes=scratch,
        ),
        compiler_params=pltpu.CompilerParams(vmem_limit_bytes=(48 << 20) if gain_args else VMEM_LIMIT),
        cost_estimate=pl.CostEstimate(
            flops=len(ks) * count * FAN * 40000, bytes_accessed=1 << 20, transcendentals=0
        ),
        name="images",
    )(me, valid, scales, *operands)


def subgrid_kernel(chunks_n, me, owner, u_offset, v_start, gain, w_high, w_low, f_rows, *refs):
    chunks = refs[:chunks_n]
    out_ref, d_high, d_low, y_ref, pos, taken = refs[chunks_n:]
    block = chunks[0].shape[0]
    row = lax.broadcasted_iota(jnp.int32, (POS_ROWS, LANES), 0)

    def clear(i, _):
        taken[i] = 0
        return 0

    lax.fori_loop(0, taken.shape[0], clear, 0, unroll=8)
    out_ref[...] = jnp.zeros_like(out_ref)
    pos[...] = jnp.full(pos.shape, NO_PLACE, f32)
    for k in range(chunks_n):
        base = (me[0] ^ k) * block
        for i in range(block):
            gain_re, gain_im = gain[0, :, base + i, :], gain[1, :, base + i, :]
            for pair in range(2):
                image = chunks[k][i, pair * SG : (pair + 1) * SG, :].astype(f32)
                both = jnp.concatenate([image * gain_re, image * gain_im], 1)
                high = both.astype(bf16)
                at = pl.ds(((k * block + i) * 2 + pair) * SG, SG)
                d_high[at, :] = high
                d_low[at, :] = (both - high.astype(f32)).astype(bf16)
    step = 256
    for i in range(d_high.shape[0] // step):
        at = pl.ds(i * step, step)
        high = d_high[at, :]
        y_ref[at, :] = (
            jnp.dot(high, w_high[...], preferred_element_type=f32)
            + jnp.dot(d_low[at, :], w_high[...], preferred_element_type=f32)
            + jnp.dot(high, w_low[...], preferred_element_type=f32)
        )
    for k in range(chunks_n):
        base = (me[0] ^ k) * block
        for i in range(block):
            at = (k * block + i) * 2 * SG
            ys = [y_ref[pl.ds(at + pair * SG, SG), :] for pair in range(2)]
            rows = jnp.concatenate(
                [
                    jnp.concatenate([y[:, :LANES] for y in ys], 1),
                    jnp.concatenate([y[:, LANES:] for y in ys], 1),
                ],
                0,
            )
            high = rows.astype(bf16)
            low = (rows - high.astype(f32)).astype(bf16)
            cells = jnp.dot(
                f_rows[...], jnp.concatenate([high, low, high], 0), preferred_element_type=f32
            ).astype(bf16)
            s = base + i
            dest = owner[0, 0, 0, s]
            slot = jnp.minimum(taken[dest], CAP - 1)
            taken[dest] = slot + 1
            for pair in range(2):
                start = pl.multiple_of((slot * 2 + pair) * SG, SG)
                out_ref[dest, pl.ds(start, SG), :] = cells[:, pair * LANES : (pair + 1) * LANES]
            u, v = u_offset[0, 0, 0, s].astype(f32), v_start[0, 0, 0, s].astype(f32)
            pos[dest] = jnp.where(row == 2 * slot, u, jnp.where(row == 2 * slot + 1, v, pos[dest]))
    out_ref[:, CAP * 2 * SG :, :] = pos[...].astype(bf16)


def subgrids(chunks, me, owner, u_offset, v_start, gain, devices_n):
    count = owner.shape[3]
    return pl.pallas_call(
        functools.partial(subgrid_kernel, len(chunks)),
        out_shape=jax.ShapeDtypeStruct((devices_n, CAP * 2 * SG + POS_ROWS, LANES), bf16),
        in_specs=[smem()] * 4 + [vmem()] * (4 + len(chunks)),
        out_specs=vmem(),
        scratch_shapes=[
            pltpu.VMEM((count * 2 * SG, 2 * LANES), bf16),
            pltpu.VMEM((count * 2 * SG, 2 * LANES), bf16),
            pltpu.VMEM((count * 2 * SG, 2 * LANES), f32),
            pltpu.VMEM((devices_n, POS_ROWS, LANES), f32),
            pltpu.SMEM((devices_n,), jnp.int32),
        ],
        compiler_params=pltpu.CompilerParams(vmem_limit_bytes=24 << 20),
        cost_estimate=pl.CostEstimate(flops=4 * 10**9, bytes_accessed=4 << 20, transcendentals=0),
        name="subgrids",
    )(me, owner, u_offset, v_start, gain, *lane_transform(), row_transform(), *chunks)


def along_v(arrived, places, source, slot, v_index):
    cells = arrived[source, pl.ds(slot * 2 * SG, 2 * SG), :]
    stacked = jnp.concatenate([cells[:, SG * k : SG * (k + 1)] for k in range(POL)], 0)
    v = places[source, pl.ds(2 * slot + 1, 1), :]
    hot = jnp.where(v_index == jnp.concatenate([v, v], 1), 1.0, 0.0).astype(bf16)
    return jnp.dot(stacked, hot, preferred_element_type=f32)


def v_steps():
    rows = lax.broadcasted_iota(jnp.int32, (SG, BAND_V), 0)
    return (lax.broadcasted_iota(jnp.int32, (SG, BAND_V), 1) - rows).astype(f32)


def parts():
    return [
        ((k % 2) * POL + pair * 2 + k // 2, (k * 2 + pair) * SG) for k in range(POL) for pair in range(2)
    ]


def margin_kernel(arrived, out_ref, acc, places, chosen, starts):
    sources = arrived.shape[0]
    batch = 4
    first = TILE_W - SG
    acc[...] = jnp.zeros_like(acc)
    places[...] = arrived[:, CAP * 2 * SG :, :].astype(f32)
    found = jnp.int32(0)
    for source in range(sources):
        for slot in range(CAP):
            u = places[source, 2 * slot, 0].astype(jnp.int32)
            chosen[found] = source * CAP + slot
            starts[found] = u - first
            found = found + ((u > first) & (u < TILE_W)).astype(jnp.int32)
    for i in range(batch):
        chosen[found + i] = 0
        starts[found + i] = 2 * SG
    v_index = v_steps()

    def add(i, _):
        wide = []
        for j in range(batch):
            at = chosen[i * batch + j]
            wide.append(along_v(arrived, places, at // CAP, at % CAP, v_index))
        for j in range(batch):
            rows = pl.ds(starts[i * batch + j], SG)
            for comp, start in parts():
                for side in range(BAND_V // LANES):
                    acc[comp, side, rows, :] += wide[j][
                        start : start + SG, side * LANES : (side + 1) * LANES
                    ]
        return 0

    lax.fori_loop(0, (found + batch - 1) // batch, add, 0)
    for side in range(BAND_V // LANES):
        out_ref[:, :, side * LANES : (side + 1) * LANES] = acc[:, side, SG : 2 * SG, :].astype(bf16)


def margin_of(arrived):
    slots = arrived.shape[0] * CAP
    return pl.pallas_call(
        margin_kernel,
        out_shape=jax.ShapeDtypeStruct((COMPS, SG, BAND_V), bf16),
        in_specs=[vmem()],
        out_specs=vmem(),
        scratch_shapes=[
            pltpu.VMEM((COMPS, BAND_V // LANES, 3 * SG, LANES), f32),
            pltpu.VMEM((arrived.shape[0], POS_ROWS, LANES), f32),
            pltpu.SMEM((slots + 4,), jnp.int32),
            pltpu.SMEM((slots + 4,), jnp.int32),
        ],
        compiler_params=pltpu.CompilerParams(vmem_limit_bytes=16 << 20),
        name="margin",
    )(arrived)


def tile_kernel(arrived, out_ref, head_ref, columns, spread, places, result, sems):
    sources = arrived.shape[0]
    per_lanes = LANES // SG
    places[...] = arrived[:, CAP * 2 * SG :, :].astype(f32)
    lane = lax.broadcasted_iota(jnp.int32, (1, LANES), 1)
    u_index = lax.broadcasted_iota(jnp.int32, (TILE_W, LANES), 0).astype(f32)
    step_a = (lane % SG).astype(f32)
    for j in range(sources * CAP // per_lanes):
        target = None
        for q in range(per_lanes):
            slot = j * per_lanes + q
            u = places[slot // CAP, 2 * (slot % CAP) : 2 * (slot % CAP) + 1, :]
            target = u if target is None else jnp.where(lane < q * SG, target, u)
        hot = jnp.where(u_index == target + step_a, 1.0, 0.0)
        columns[:, j * LANES : (j + 1) * LANES] = hot.astype(bf16)
    v_index = v_steps()
    unrolled = min(32, sources)

    def spread_some(i, _):
        for j in range(unrolled):
            source = i * unrolled + j
            for slot in range(CAP):
                wide = along_v(arrived, places, source, slot, v_index).astype(bf16)
                at = pl.ds(pl.multiple_of((source * CAP + slot) * SG, SG), SG)
                for comp, start in parts():
                    spread[at, comp * BAND_V : (comp + 1) * BAND_V] = wide[start : start + SG]
        return 0

    lax.fori_loop(0, sources // unrolled, spread_some, 0)
    copies = []
    for comp in range(COMPS):
        result[comp] = jnp.dot(
            columns[...], spread[:, comp * BAND_V : (comp + 1) * BAND_V], preferred_element_type=f32
        )
        head_ref[comp] = result[comp, :SG, :]
        rest = pl.ds(SG, TILE_W - SG)
        copies.append(
            pltpu.make_async_copy(result.at[comp, rest], out_ref.at[comp, rest], sems.at[comp])
        )
        copies[-1].start()
    for copy in copies:
        copy.wait()


def tile_of(arrived):
    cells = arrived.shape[0] * CAP * SG
    return pl.pallas_call(
        tile_kernel,
        out_shape=(
            jax.ShapeDtypeStruct((COMPS, TILE_W, BAND_V), f32),
            jax.ShapeDtypeStruct((COMPS, SG, BAND_V), f32),
        ),
        in_specs=[vmem()],
        out_specs=(pl.BlockSpec(memory_space=pl.ANY), vmem()),
        scratch_shapes=[
            pltpu.VMEM((TILE_W, cells), bf16),
            pltpu.VMEM((cells, COMPS * BAND_V), bf16),
            pltpu.VMEM((arrived.shape[0], POS_ROWS, LANES), f32),
            pltpu.VMEM((COMPS, TILE_W, BAND_V), f32),
            pltpu.SemaphoreType.DMA((COMPS,)),
        ],
        compiler_params=pltpu.CompilerParams(vmem_limit_bytes=(10 << 20) + 2 * cells * (COMPS * BAND_V + 2 * TILE_W)),
        cost_estimate=pl.CostEstimate(flops=4 * 10**9, bytes_accessed=4 << 20, transcendentals=0),
        name="tile",
    )(arrived)


def on_device(
    visibilities, uv_rows, chan_scale, valid_rows, aterm, taper, stations, owner, u_offset, v_start
):
    groups_n = lax.axis_size("freq")
    devices_n = groups_n * lax.axis_size("tile")
    me = lax.axis_index("freq")[None].astype(jnp.int32)
    far = list(range(groups_n - 1, 1, -1))
    near = [k for k in (1, 0) if k < groups_n]
    stations, owner, u_offset, v_start = (
        jnp.swapaxes(index, 2, 3) for index in (stations, owner, u_offset, v_start)
    )
    chunks = {}

    def make(ks, gain_args=()):
        made = images(ks, me, valid_rows, chan_scale, visibilities[0], uv_rows, gain_args)
        for k, part in zip(ks, made):
            if k:
                part = lax.ppermute(part, "freq", [(i, i ^ k) for i in range(groups_n)])
            chunks[k] = part
        return made[-1]

    if far:
        make(far)
    gain = make(near, (stations, aterm, taper))
    outgoing = subgrids(
        [chunks[k] for k in range(groups_n)], me, owner, u_offset, v_start, gain, devices_n
    )
    arrived = lax.all_to_all(
        outgoing, ("freq", "tile"), split_axis=0, concat_axis=0, tiled=True
    )
    incoming = lax.ppermute(
        margin_of(arrived), ("freq", "tile"), [(i, (i + 1) % devices_n) for i in range(devices_n)]
    )
    tile, head = tile_of(arrived)
    return tile.at[:, :SG, :].set(head + incoming.astype(f32))


def solution(mesh):
    in_specs = (
        P("tile", None, None, "freq"),
        P("tile", None, "freq"),
        P(),
        P("tile", "freq"),
        P("freq", None, None, None),
        P(),
        P("tile", "freq", None, None),
        P("tile", "freq", None, None),
        P("tile", "freq", None, None),
        P("tile", "freq", None, None),
    )
    out_specs = P(None, ("freq", "tile"), None)
    return jax.shard_map(
        on_device, mesh=mesh, in_specs=in_specs, out_specs=out_specs, check_vma=False
    )
```

```python
import functools
import math

import jax
import jax.numpy as jnp
import ml_dtypes
import numpy as np
from jax import lax
from jax.experimental import pallas as pl
from jax.experimental.pallas import tpu as pltpu
from jax.sharding import PartitionSpec as P

SG = 32
HALF = SG // 2
TSTEP = 128
CHAN_G = 16
FAN = CHAN_G * TSTEP
TILE_W = 256
BAND_V = 256
LANES = 128
COMPS = 8
POL = 4
POS_ROWS = 8
NO_PLACE = 512.0
COARSE = (4, 12)
FINE = 4
SUMS = 2 * FINE * COMPS
CAP = 2
U_STEP = SG + 1
V_STEP = 13
W_STEP = CHAN_G + 1
VMEM_LIMIT = 60 << 20
f32 = jnp.float32
bf16 = jnp.bfloat16


def vmem():
    return pl.BlockSpec(memory_space=pltpu.VMEM)


def smem():
    return pl.BlockSpec(memory_space=pltpu.SMEM)


IMAGE_ROWS = np.array([HALF + i for i in range(HALF)] + [HALF - 1 - i for i in range(HALF)])


def split(matrix):
    high = matrix.astype(np.float32).astype(ml_dtypes.bfloat16)
    low = (matrix - high.astype(np.float64)).astype(np.float32).astype(ml_dtypes.bfloat16)
    return high, low


def fourier():
    cells = np.arange(SG) - HALF
    angles = (cells[:, None] * cells[None, :] % SG) * (2.0 * math.pi / SG)
    return np.cos(angles), -np.sin(angles)


def lane_transform():
    cos, sin = fourier()
    table = np.zeros((2, 2, 2, SG, 2, 2, 2, SG))
    for p in range(2):
        y_re = {(0, 0): cos, (1, 1): -cos, (1, 0): -sin, (0, 1): -sin}
        y_im = {(0, 0): sin, (1, 1): -sin, (1, 0): cos, (0, 1): cos}
        for gain in range(2):
            for part in range(2):
                re, im = y_re[gain, part].T, y_im[gain, part].T
                table[gain, p, part, :, 0, p, 0, :] = re
                table[gain, p, part, :, 0, p, 1, :] = im
                table[gain, p, part, :, 1, p, 0, :] = -im
                table[gain, p, part, :, 1, p, 1, :] = re
    return split(table.reshape(256, 256))


def row_transform():
    cos, sin = fourier()
    high, low = split(np.concatenate([cos[:, IMAGE_ROWS], sin[:, IMAGE_ROWS]], 1))
    return np.concatenate([high, high, low], 1)


def combine_table():
    table = np.zeros((4, 2, SUMS, 2, 2, 2, SG))
    for m in range(SG):
        for a, coarse in enumerate((COARSE[0], -COARSE[0], COARSE[1], -COARSE[1])):
            b = m - HALF + 0.5 - coarse
            if abs(b) > FINE:
                continue
            size, sign = int(abs(b)), 1 if b > 0 else -1
            for p in range(POL):
                re, im = table[a, :, :, p // 2, p % 2, 0, m], table[a, :, :, p // 2, p % 2, 1, m]
                at = size * COMPS
                re[0, at + p], im[0, at + POL + p] = 1, 1
                re[1, at + POL + p], im[1, at + p] = -1, 1
                at += FINE * COMPS
                re[0, at + POL + p], im[0, at + p] = -sign, sign
                re[1, at + p], im[1, at + POL + p] = -sign, -sign
    return table.reshape(4 * LANES, 2 * LANES).astype(ml_dtypes.bfloat16)


def lane_tiles():
    table = np.zeros((POL, SG, POL, POL, SG))
    for q in range(POL):
        for copy in range(POL):
            table[q, :, q, copy, :] = np.eye(SG)
    table = table.reshape(LANES, POL * LANES)
    return np.concatenate([table] * 3, 0).astype(ml_dtypes.bfloat16)


def times(one, two):
    return one[0] * two[0] - one[1] * two[1], one[0] * two[1] + one[1] * two[0]


def squared(one):
    return 1.0 - 2.0 * one[1] * one[1], 2.0 * one[1] * one[0]


def half_angle(theta):
    half = theta * 0.5
    square = half * half
    sin = half * (
        1.0 + square * (-1.0 / 6 + square * (1.0 / 120 + square * (-1.0 / 5040 + square * (1.0 / 362880))))
    )
    cos = 1.0 + square * (
        -0.5 + square * (1.0 / 24 + square * (-1.0 / 720 + square * (1.0 / 40320 + square * (-1.0 / 3628800))))
    )
    return cos, sin


def odd_halves(half, count):
    values, steps = [half], [squared(half)]
    while len(values) < count:
        values += [times(value, steps[-1]) for value in values]
        steps.append(squared(steps[-1]))
    return values, steps


def gain_copies(stations, aterm, rows, sems):
    count = rows.shape[0] // 2
    return [
        pltpu.make_async_copy(
            aterm.at[0, stations[0, 0, i // count, i % count]],
            rows.at[i, :, pl.ds(0, SG * SG)],
            sems.at[i],
        )
        for i in range(2 * count)
    ]


def make_gains(taper, tiles, out_ref, rows):
    count = rows.shape[0] // 2
    blocks = SG * SG // LANES
    parts = []
    for r in range(blocks):
        cols = pl.ds(r * LANES, LANES)
        one_re, one_im = rows[0:count, 0, cols], rows[0:count, 1, cols]
        two_re, two_im = rows[count:, 0, cols], rows[count:, 1, cols]
        shape = jnp.concatenate(
            [taper[POL * r + q : POL * r + q + 1, :] for q in range(POL)], 1
        ) * (1.0 / (math.sqrt(FAN) * SG))
        gain = jnp.concatenate(
            [(one_re * two_re + one_im * two_im) * shape, (one_im * two_re - one_re * two_im) * shape], 0
        )
        high = gain.astype(bf16)
        rest = gain - high.astype(f32)
        mid = rest.astype(bf16)
        low = (rest - mid.astype(f32)).astype(bf16)
        parts.append(jnp.concatenate([high, mid, low], 1))
    tiled = jnp.dot(jnp.concatenate(parts, 0), tiles[...], preferred_element_type=f32)
    for r in range(blocks):
        for q in range(POL):
            row = list(IMAGE_ROWS).index(POL * r + q)
            for part in range(2):
                at = (2 * r + part) * count
                out_ref[part, row] = tiled[at : at + count, q * LANES : (q + 1) * LANES]


def image_kernel(ks, with_gains, me, valid, scales, *refs):
    refs = list(refs)
    take = lambda count: [refs.pop(0) for _ in range(count)]
    stations = take(1)[0] if with_gains else None
    vis_ref, uv_ref, combine = take(3)
    aterm, taper, tiles = take(3) if with_gains else (None, None, None)
    outs = take(len(ks))
    gain_ref = take(1)[0] if with_gains else None
    u_tabs, v_tabs, w_tabs, scale_tab, x_high, x_low = take(6)
    turn = pl.program_id(0)
    copies = gain_copies(stations, aterm, *refs) if with_gains else []

    @pl.when(turn == 0)
    def _():
        for copy in copies:
            copy.start()

    lane = lax.broadcasted_iota(jnp.int32, (CHAN_G, TSTEP), 1)

    def build(s, scale):
        u_tab, v_tab, w_tab = u_tabs.at[s % 2], v_tabs.at[s % 2], w_tabs.at[s % 2]
        part = pl.ds(s * TSTEP, TSTEP)
        live = lane + s * TSTEP < valid[0, 0]
        parts = []
        for c in range(COMPS):
            values = vis_ref[c, :, part].astype(f32)
            parts.append(jnp.where(live, values, 0.0))
        u_half = half_angle(uv_ref[0, 0:1, part] * scale)
        v_half = half_angle(uv_ref[0, 1:2, part] * scale)
        cos, sin = times(u_half, v_half)
        for p in range(POL):
            re, im = parts[p], parts[POL + p]
            w_tab[pl.ds(p * W_STEP, CHAN_G), :] = re * cos + im * sin
            w_tab[pl.ds((POL + p) * W_STEP, CHAN_G), :] = im * cos - re * sin
        for n, value in enumerate(odd_halves(u_half, HALF)[0]):
            u_tab[pl.ds(n, CHAN_G, U_STEP), :] = value[0]
            u_tab[pl.ds(HALF + n, CHAN_G, U_STEP), :] = value[1]
        values, steps = odd_halves(v_half, FINE)
        for n, value in enumerate(values):
            v_tab[pl.ds(4 + n, CHAN_G, V_STEP), :] = value[0]
            v_tab[pl.ds(4 + FINE + n, CHAN_G, V_STEP), :] = value[1]
        for q, value in enumerate((steps[-1], times(steps[-1], squared(steps[-1])))):
            v_tab[pl.ds(2 * q, CHAN_G, V_STEP), :] = value[0]
            v_tab[pl.ds(2 * q + 1, CHAN_G, V_STEP), :] = value[1]
        sums = None
        step = 4
        for start in range(0, CHAN_G, step):
            left, right = [], []
            for h in range(start, start + step):
                u_rows = u_tab[pl.ds(h * U_STEP, SG), :]
                column = [
                    (u_rows * v_tab[pl.ds(h * V_STEP + a, 1), :]).astype(bf16) for a in range(4)
                ]
                left.append(jnp.concatenate(column, 0))
                w_all = w_tab[pl.ds(h, COMPS, W_STEP), :]
                fine = [w_all * v_tab[pl.ds(h * V_STEP + 4 + b, 1), :] for b in range(2 * FINE)]
                right.append(jnp.concatenate(fine, 0).astype(bf16))
            term = lax.dot_general(
                jnp.concatenate(left, 1),
                jnp.concatenate(right, 1),
                (((1,), (1,)), ((), ())),
                preferred_element_type=f32,
            )
            sums = term if sums is None else sums + term
        return sums

    def keep(s, sums):
        for q in range(2):
            cos, sin = sums[2 * q * SG : (2 * q + 1) * SG], sums[(2 * q + 1) * SG : (2 * q + 2) * SG]
            cc, sc, cs, ss = cos[:HALF], cos[HALF:], sin[:HALF], sin[HALF:]
            for d, (zero, one) in enumerate(
                (((cc - ss, cc + ss), (sc + cs, cs - sc)), ((cc + ss, cc - ss), (sc - cs, -sc - cs)))
            ):
                both = jnp.concatenate([jnp.concatenate(zero, 0), jnp.concatenate(one, 0)], 1)
                high = both.astype(bf16)
                at = (2 * q + d) * LANES
                x_high[s * SG : (s + 1) * SG, at : at + LANES] = high
                x_low[s * SG : (s + 1) * SG, at : at + LANES] = (both - high.astype(f32)).astype(bf16)

    group = me[0] ^ (ks[0] - turn)
    for h in range(CHAN_G):
        scale_tab[h : h + 1, :] = jnp.full((1, LANES), scales[group * CHAN_G + h], f32)
    scale = scale_tab[...] * (2.0 * math.pi / SG)
    count = outs[0].shape[0]
    for s in range(count):
        keep(s, build(s, scale))
    image = (
        jnp.dot(x_high[...], combine[...], preferred_element_type=f32)
        + jnp.dot(x_low[...], combine[...], preferred_element_type=f32)
    ).astype(bf16)

    def write(out_ref):
        for s in range(count):
            for pair in range(2):
                out_ref[s, pair * SG : (pair + 1) * SG, :] = image[
                    s * SG : (s + 1) * SG, pair * LANES : (pair + 1) * LANES
                ]

    for i, out_ref in enumerate(outs):
        pl.when(turn == i)(functools.partial(write, out_ref))

    if with_gains:

        @pl.when(turn == len(ks) - 1)
        def _():
            for copy in copies:
                copy.wait()
            make_gains(taper, tiles, gain_ref, refs[0])


def images(ks, me, valid, scales, vis, uv, gain_args=()):
    rows = vis.shape[2]
    count = rows // TSTEP
    block = (COMPS, CHAN_G, rows)
    whole = pl.BlockSpec((count, 2 * SG, LANES), lambda i, at: (0, 0, 0))
    out_shape = [jax.ShapeDtypeStruct((count, 2 * SG, LANES), bf16)] * len(ks)
    out_specs = [whole] * len(ks)
    in_specs = [pl.BlockSpec(block, lambda i, at: (0, at[0] ^ (ks[0] - i), 0))]
    table = combine_table()
    in_specs += [
        pl.BlockSpec((1, 2, rows), lambda i, at: (0, 0, 0)),
        pl.BlockSpec(table.shape, lambda i, at: (0, 0)),
    ]
    scratch = [
        pltpu.VMEM((2, CHAN_G * U_STEP, LANES), f32),
        pltpu.VMEM((2, CHAN_G * V_STEP, LANES), f32),
        pltpu.VMEM((2, COMPS * W_STEP, LANES), f32),
        pltpu.VMEM((CHAN_G, LANES), f32),
        pltpu.VMEM((count * SG, 4 * LANES), bf16),
        pltpu.VMEM((count * SG, 4 * LANES), bf16),
    ]
    operands = [vis, uv, table]
    if gain_args:
        stations, aterm, taper = gain_args
        subs = stations.shape[3]
        tiles = lane_tiles()
        operands = [stations] + operands + [aterm, taper, tiles]
        in_specs = [smem()] + in_specs + [
            pl.BlockSpec(memory_space=pltpu.HBM),
            pl.BlockSpec(taper.shape, lambda i, at: (0, 0)),
            pl.BlockSpec(tiles.shape, lambda i, at: (0, 0)),
        ]
        out_shape += [jax.ShapeDtypeStruct((2, SG, subs, LANES), f32)]
        out_specs += [pl.BlockSpec((2, SG, subs, LANES), lambda i, at: (0, 0, 0, 0))]
        scratch += [pltpu.VMEM((2 * subs, 2, SG * SG + LANES), f32), pltpu.SemaphoreType.DMA((2 * subs,))]
    return pl.pallas_call(
        functools.partial(image_kernel, ks, bool(gain_args)),
        out_shape=out_shape,
        grid_spec=pltpu.PrefetchScalarGridSpec(
            num_scalar_prefetch=1,
            grid=(len(ks),),
            in_specs=[smem(), smem()] + in_specs,
            out_specs=out_specs,
            scratch_shapes=scratch,
        ),
        compiler_params=pltpu.CompilerParams(vmem_limit_bytes=(48 << 20) if gain_args else VMEM_LIMIT),
        cost_estimate=pl.CostEstimate(
            flops=len(ks) * count * FAN * 40000, bytes_accessed=1 << 20, transcendentals=0
        ),
        name="images",
    )(me, valid, scales, *operands)


def subgrid_kernel(chunks_n, me, owner, u_offset, v_start, gain, w_high, w_low, f_rows, *refs):
    chunks = refs[:chunks_n]
    out_ref, d_high, d_low, y_ref, pos, taken = refs[chunks_n:]
    block = chunks[0].shape[0]
    row = lax.broadcasted_iota(jnp.int32, (2, LANES), 0)

    def clear(i, _):
        taken[i] = 0
        return 0

    lax.fori_loop(0, taken.shape[0], clear, 0, unroll=8)
    out_ref[...] = jnp.zeros_like(out_ref)
    pos[...] = jnp.full(pos.shape, NO_PLACE, f32)
    for k in range(chunks_n):
        base = (me[0] ^ k) * block
        for i in range(block):
            gain_re, gain_im = gain[0, :, base + i, :], gain[1, :, base + i, :]
            for pair in range(2):
                image = chunks[k][i, pair * SG : (pair + 1) * SG, :].astype(f32)
                both = jnp.concatenate([image * gain_re, image * gain_im], 1)
                high = both.astype(bf16)
                at = pl.ds(((k * block + i) * 2 + pair) * SG, SG)
                d_high[at, :] = high
                d_low[at, :] = (both - high.astype(f32)).astype(bf16)
    step = 128
    for i in range(d_high.shape[0] // step):
        at = pl.ds(i * step, step)
        high = d_high[at, :]
        y_ref[at, :] = jnp.dot(
            jnp.concatenate([high, d_low[at, :], high], 1),
            jnp.concatenate([w_high[...], w_high[...], w_low[...]], 0),
            preferred_element_type=f32,
        )
    for k in range(chunks_n):
        base = (me[0] ^ k) * block
        for i in range(block):
            at = (k * block + i) * 2 * SG
            ys = [y_ref[pl.ds(at + pair * SG, SG), :] for pair in range(2)]
            rows = jnp.concatenate(
                [
                    jnp.concatenate([y[:, :LANES] for y in ys], 1),
                    jnp.concatenate([y[:, LANES:] for y in ys], 1),
                ],
                0,
            )
            high = rows.astype(bf16)
            low = (rows - high.astype(f32)).astype(bf16)
            cells = jnp.dot(
                f_rows[...], jnp.concatenate([high, low, high], 0), preferred_element_type=f32
            ).astype(bf16)
            s = base + i
            dest = owner[0, 0, 0, s]
            slot = jnp.minimum(taken[dest], CAP - 1)
            taken[dest] = slot + 1
            for pair in range(2):
                start = pl.multiple_of((slot * 2 + pair) * SG, SG)
                out_ref[dest, pl.ds(start, SG), :] = cells[:, pair * LANES : (pair + 1) * LANES]
            u, v = u_offset[0, 0, 0, s].astype(f32), v_start[0, 0, 0, s].astype(f32)
            pos[dest, pl.ds(2 * slot, 2), :] = jnp.where(row == 0, u, v)
    out_ref[:, CAP * 2 * SG :, :] = pos[...].astype(bf16)


def subgrids(chunks, me, owner, u_offset, v_start, gain, devices_n):
    count = owner.shape[3]
    return pl.pallas_call(
        functools.partial(subgrid_kernel, len(chunks)),
        out_shape=jax.ShapeDtypeStruct((devices_n, CAP * 2 * SG + POS_ROWS, LANES), bf16),
        in_specs=[smem()] * 4 + [vmem()] * (4 + len(chunks)),
        out_specs=vmem(),
        scratch_shapes=[
            pltpu.VMEM((count * 2 * SG, 2 * LANES), bf16),
            pltpu.VMEM((count * 2 * SG, 2 * LANES), bf16),
            pltpu.VMEM((count * 2 * SG, 2 * LANES), f32),
            pltpu.VMEM((devices_n, POS_ROWS, LANES), f32),
            pltpu.SMEM((devices_n,), jnp.int32),
        ],
        compiler_params=pltpu.CompilerParams(vmem_limit_bytes=24 << 20),
        cost_estimate=pl.CostEstimate(flops=4 * 10**9, bytes_accessed=4 << 20, transcendentals=0),
        name="subgrids",
    )(me, owner, u_offset, v_start, gain, *lane_transform(), row_transform(), *chunks)


def along_v(arrived, places, source, slot, v_index):
    cells = arrived[source, pl.ds(slot * 2 * SG, 2 * SG), :]
    stacked = jnp.concatenate([cells[:, SG * k : SG * (k + 1)] for k in range(POL)], 0)
    v = places[source, pl.ds(2 * slot + 1, 1), :]
    hot = jnp.where(v_index == jnp.concatenate([v, v], 1), 1.0, 0.0).astype(bf16)
    return jnp.dot(stacked, hot, preferred_element_type=f32)


def v_steps():
    rows = lax.broadcasted_iota(jnp.int32, (SG, BAND_V), 0)
    return (lax.broadcasted_iota(jnp.int32, (SG, BAND_V), 1) - rows).astype(f32)


def parts():
    return [
        ((k % 2) * POL + pair * 2 + k // 2, (k * 2 + pair) * SG) for k in range(POL) for pair in range(2)
    ]


def margin_kernel(arrived, out_ref, acc, places, chosen, starts):
    sources = arrived.shape[0]
    batch = 4
    first = TILE_W - SG
    acc[...] = jnp.zeros_like(acc)
    places[...] = arrived[:, CAP * 2 * SG :, :].astype(f32)
    found = jnp.int32(0)
    for source in range(sources):
        for slot in range(CAP):
            u = places[source, 2 * slot, 0].astype(jnp.int32)
            chosen[found] = source * CAP + slot
            starts[found] = u - first
            found = found + ((u > first) & (u < TILE_W)).astype(jnp.int32)
    for i in range(batch):
        chosen[found + i] = 0
        starts[found + i] = 2 * SG
    v_index = v_steps()

    def add(i, _):
        wide = []
        for j in range(batch):
            at = chosen[i * batch + j]
            wide.append(along_v(arrived, places, at // CAP, at % CAP, v_index))
        for j in range(batch):
            rows = pl.ds(starts[i * batch + j], SG)
            for comp, start in parts():
                for side in range(BAND_V // LANES):
                    acc[comp, side, rows, :] += wide[j][
                        start : start + SG, side * LANES : (side + 1) * LANES
                    ]
        return 0

    lax.fori_loop(0, (found + batch - 1) // batch, add, 0)
    for side in range(BAND_V // LANES):
        out_ref[:, :, side * LANES : (side + 1) * LANES] = acc[:, side, SG : 2 * SG, :].astype(bf16)


def margin_of(arrived):
    slots = arrived.shape[0] * CAP
    return pl.pallas_call(
        margin_kernel,
        out_shape=jax.ShapeDtypeStruct((COMPS, SG, BAND_V), bf16),
        in_specs=[vmem()],
        out_specs=vmem(),
        scratch_shapes=[
            pltpu.VMEM((COMPS, BAND_V // LANES, 3 * SG, LANES), f32),
            pltpu.VMEM((arrived.shape[0], POS_ROWS, LANES), f32),
            pltpu.SMEM((slots + 4,), jnp.int32),
            pltpu.SMEM((slots + 4,), jnp.int32),
        ],
        compiler_params=pltpu.CompilerParams(vmem_limit_bytes=16 << 20),
        name="margin",
    )(arrived)


def tile_kernel(arrived, out_ref, head_ref, columns, spread, places, result, sems):
    sources = arrived.shape[0]
    per_lanes = LANES // SG
    places[...] = arrived[:, CAP * 2 * SG :, :].astype(f32)
    lane = lax.broadcasted_iota(jnp.int32, (1, LANES), 1)
    u_index = lax.broadcasted_iota(jnp.int32, (TILE_W, LANES), 0).astype(f32)
    step_a = (lane % SG).astype(f32)
    for j in range(sources * CAP // per_lanes):
        target = None
        for q in range(per_lanes):
            slot = j * per_lanes + q
            u = places[slot // CAP, 2 * (slot % CAP) : 2 * (slot % CAP) + 1, :]
            target = u if target is None else jnp.where(lane < q * SG, target, u)
        hot = jnp.where(u_index == target + step_a, 1.0, 0.0)
        columns[:, j * LANES : (j + 1) * LANES] = hot.astype(bf16)
    v_index = v_steps()
    unrolled = min(32, sources)

    def spread_some(i, _):
        for j in range(unrolled):
            source = i * unrolled + j
            for slot in range(CAP):
                wide = along_v(arrived, places, source, slot, v_index).astype(bf16)
                at = pl.ds(pl.multiple_of((source * CAP + slot) * SG, SG), SG)
                for comp, start in parts():
                    spread[at, comp * BAND_V : (comp + 1) * BAND_V] = wide[start : start + SG]
        return 0

    lax.fori_loop(0, sources // unrolled, spread_some, 0)
    copies = []
    for comp in range(COMPS):
        result[comp] = jnp.dot(
            columns[...], spread[:, comp * BAND_V : (comp + 1) * BAND_V], preferred_element_type=f32
        )
        head_ref[comp] = result[comp, :SG, :]
        rest = pl.ds(SG, TILE_W - SG)
        copies.append(
            pltpu.make_async_copy(result.at[comp, rest], out_ref.at[comp, rest], sems.at[comp])
        )
        copies[-1].start()
    for copy in copies:
        copy.wait()


def tile_of(arrived):
    cells = arrived.shape[0] * CAP * SG
    return pl.pallas_call(
        tile_kernel,
        out_shape=(
            jax.ShapeDtypeStruct((COMPS, TILE_W, BAND_V), f32),
            jax.ShapeDtypeStruct((COMPS, SG, BAND_V), f32),
        ),
        in_specs=[vmem()],
        out_specs=(pl.BlockSpec(memory_space=pl.ANY), vmem()),
        scratch_shapes=[
            pltpu.VMEM((TILE_W, cells), bf16),
            pltpu.VMEM((cells, COMPS * BAND_V), bf16),
            pltpu.VMEM((arrived.shape[0], POS_ROWS, LANES), f32),
            pltpu.VMEM((COMPS, TILE_W, BAND_V), f32),
            pltpu.SemaphoreType.DMA((COMPS,)),
        ],
        compiler_params=pltpu.CompilerParams(vmem_limit_bytes=(10 << 20) + 2 * cells * (COMPS * BAND_V + 2 * TILE_W)),
        cost_estimate=pl.CostEstimate(flops=4 * 10**9, bytes_accessed=4 << 20, transcendentals=0),
        name="tile",
    )(arrived)


def on_device(
    visibilities, uv_rows, chan_scale, valid_rows, aterm, taper, stations, owner, u_offset, v_start
):
    groups_n = lax.axis_size("freq")
    devices_n = groups_n * lax.axis_size("tile")
    me = lax.axis_index("freq")[None].astype(jnp.int32)
    far = list(range(groups_n - 1, 1, -1))
    near = [k for k in (1, 0) if k < groups_n]
    stations, owner, u_offset, v_start = (
        jnp.swapaxes(index, 2, 3) for index in (stations, owner, u_offset, v_start)
    )
    chunks = {}

    def make(ks, gain_args=()):
        made = images(ks, me, valid_rows, chan_scale, visibilities[0], uv_rows, gain_args)
        for k, part in zip(ks, made):
            if k:
                part = lax.ppermute(part, "freq", [(i, i ^ k) for i in range(groups_n)])
            chunks[k] = part
        return made[-1]

    if far:
        make(far)
    gain = make(near, (stations, aterm, taper))
    outgoing = subgrids(
        [chunks[k] for k in range(groups_n)], me, owner, u_offset, v_start, gain, devices_n
    )
    arrived = lax.all_to_all(
        outgoing, ("freq", "tile"), split_axis=0, concat_axis=0, tiled=True
    )
    incoming = lax.ppermute(
        margin_of(arrived), ("freq", "tile"), [(i, (i + 1) % devices_n) for i in range(devices_n)]
    )
    tile, head = tile_of(arrived)
    return tile.at[:, :SG, :].set(head + incoming.astype(f32))


def solution(mesh):
    in_specs = (
        P("tile", None, None, "freq"),
        P("tile", None, "freq"),
        P(),
        P("tile", "freq"),
        P("freq", None, None, None),
        P(),
        P("tile", "freq", None, None),
        P("tile", "freq", None, None),
        P("tile", "freq", None, None),
        P("tile", "freq", None, None),
    )
    out_specs = P(None, ("freq", "tile"), None)
    return jax.shard_map(
        on_device, mesh=mesh, in_specs=in_specs, out_specs=out_specs, check_vma=False
    )
```

```python
import functools
import math

import jax
import jax.numpy as jnp
import ml_dtypes
import numpy as np
from jax import lax
from jax.experimental import pallas as pl
from jax.experimental.pallas import tpu as pltpu
from jax.sharding import PartitionSpec as P

SG = 32
HALF = SG // 2
TSTEP = 128
CHAN_G = 16
FAN = CHAN_G * TSTEP
TILE_W = 256
BAND_V = 256
LANES = 128
COMPS = 8
POL = 4
POS_ROWS = 8
NO_PLACE = 512.0
COARSE = (4, 12)
FINE = 4
SUMS = 2 * FINE * COMPS
CAP = 2
U_STEP = SG + 1
V_STEP = 13
W_STEP = CHAN_G + 1
VMEM_LIMIT = 60 << 20
f32 = jnp.float32
bf16 = jnp.bfloat16


def vmem():
    return pl.BlockSpec(memory_space=pltpu.VMEM)


def smem():
    return pl.BlockSpec(memory_space=pltpu.SMEM)


IMAGE_ROWS = np.array([HALF + i for i in range(HALF)] + [HALF - 1 - i for i in range(HALF)])


def split(matrix):
    high = matrix.astype(np.float32).astype(ml_dtypes.bfloat16)
    low = (matrix - high.astype(np.float64)).astype(np.float32).astype(ml_dtypes.bfloat16)
    return high, low


def fourier():
    cells = np.arange(SG) - HALF
    angles = (cells[:, None] * cells[None, :] % SG) * (2.0 * math.pi / SG)
    return np.cos(angles), -np.sin(angles)


def lane_transform():
    cos, sin = fourier()
    table = np.zeros((2, 2, 2, SG, 2, 2, 2, SG))
    for p in range(2):
        y_re = {(0, 0): cos, (1, 1): -cos, (1, 0): -sin, (0, 1): -sin}
        y_im = {(0, 0): sin, (1, 1): -sin, (1, 0): cos, (0, 1): cos}
        for gain in range(2):
            for part in range(2):
                re, im = y_re[gain, part].T, y_im[gain, part].T
                table[gain, p, part, :, 0, p, 0, :] = re
                table[gain, p, part, :, 0, p, 1, :] = im
                table[gain, p, part, :, 1, p, 0, :] = -im
                table[gain, p, part, :, 1, p, 1, :] = re
    return split(table.reshape(256, 256))


def row_transform():
    cos, sin = fourier()
    high, low = split(np.concatenate([cos[:, IMAGE_ROWS], sin[:, IMAGE_ROWS]], 1))
    return np.concatenate([high, high, low], 1)


def combine_table():
    table = np.zeros((4, 2, SUMS, 2, 2, 2, SG))
    for m in range(SG):
        for a, coarse in enumerate((COARSE[0], -COARSE[0], COARSE[1], -COARSE[1])):
            b = m - HALF + 0.5 - coarse
            if abs(b) > FINE:
                continue
            size, sign = int(abs(b)), 1 if b > 0 else -1
            for p in range(POL):
                re, im = table[a, :, :, p // 2, p % 2, 0, m], table[a, :, :, p // 2, p % 2, 1, m]
                at = size * COMPS
                re[0, at + p], im[0, at + POL + p] = 1, 1
                re[1, at + POL + p], im[1, at + p] = -1, 1
                at += FINE * COMPS
                re[0, at + POL + p], im[0, at + p] = -sign, sign
                re[1, at + p], im[1, at + POL + p] = -sign, -sign
    return table.reshape(4 * LANES, 2 * LANES).astype(ml_dtypes.bfloat16)


def lane_tiles():
    table = np.zeros((POL, SG, POL, POL, SG))
    for q in range(POL):
        for copy in range(POL):
            table[q, :, q, copy, :] = np.eye(SG)
    table = table.reshape(LANES, POL * LANES)
    return np.concatenate([table] * 3, 0).astype(ml_dtypes.bfloat16)


def times(one, two):
    return one[0] * two[0] - one[1] * two[1], one[0] * two[1] + one[1] * two[0]


def squared(one):
    return 1.0 - 2.0 * one[1] * one[1], 2.0 * one[1] * one[0]


def half_angle(theta):
    half = theta * 0.5
    square = half * half
    sin = half * (
        1.0 + square * (-1.0 / 6 + square * (1.0 / 120 + square * (-1.0 / 5040 + square * (1.0 / 362880))))
    )
    cos = 1.0 + square * (
        -0.5 + square * (1.0 / 24 + square * (-1.0 / 720 + square * (1.0 / 40320 + square * (-1.0 / 3628800))))
    )
    return cos, sin


def odd_halves(half, count):
    values, steps = [half], [squared(half)]
    while len(values) < count:
        values += [times(value, steps[-1]) for value in values]
        steps.append(squared(steps[-1]))
    return values, steps


def gain_copies(stations, aterm, rows, sems):
    count = rows.shape[0] // 2
    return [
        pltpu.make_async_copy(
            aterm.at[0, stations[0, 0, i // count, i % count]],
            rows.at[i, :, pl.ds(0, SG * SG)],
            sems.at[i],
        )
        for i in range(2 * count)
    ]


def make_gains(taper, tiles, out_ref, rows):
    count = rows.shape[0] // 2
    blocks = SG * SG // LANES
    parts = []
    for r in range(blocks):
        cols = pl.ds(r * LANES, LANES)
        one_re, one_im = rows[0:count, 0, cols], rows[0:count, 1, cols]
        two_re, two_im = rows[count:, 0, cols], rows[count:, 1, cols]
        shape = jnp.concatenate(
            [taper[POL * r + q : POL * r + q + 1, :] for q in range(POL)], 1
        ) * (1.0 / (math.sqrt(FAN) * SG))
        gain = jnp.concatenate(
            [(one_re * two_re + one_im * two_im) * shape, (one_im * two_re - one_re * two_im) * shape], 0
        )
        high = gain.astype(bf16)
        rest = gain - high.astype(f32)
        mid = rest.astype(bf16)
        low = (rest - mid.astype(f32)).astype(bf16)
        parts.append(jnp.concatenate([high, mid, low], 1))
    tiled = jnp.dot(jnp.concatenate(parts, 0), tiles[...], preferred_element_type=f32)
    for r in range(blocks):
        for q in range(POL):
            row = list(IMAGE_ROWS).index(POL * r + q)
            for part in range(2):
                at = (2 * r + part) * count
                out_ref[part, row] = tiled[at : at + count, q * LANES : (q + 1) * LANES]


def image_kernel(ks, with_gains, me, valid, scales, *refs):
    refs = list(refs)
    take = lambda count: [refs.pop(0) for _ in range(count)]
    stations = take(1)[0] if with_gains else None
    vis_ref, uv_ref, combine = take(3)
    aterm, taper, tiles = take(3) if with_gains else (None, None, None)
    outs = take(len(ks))
    gain_ref = take(1)[0] if with_gains else None
    u_tabs, v_tabs, w_tabs, scale_tab, x_high, x_low = take(6)
    turn = pl.program_id(0)
    copies = gain_copies(stations, aterm, *refs) if with_gains else []

    @pl.when(turn == 0)
    def _():
        for copy in copies:
            copy.start()

    lane = lax.broadcasted_iota(jnp.int32, (CHAN_G, TSTEP), 1)

    def build(s, scale):
        u_tab, v_tab, w_tab = u_tabs.at[s % 2], v_tabs.at[s % 2], w_tabs.at[s % 2]
        part = pl.ds(s * TSTEP, TSTEP)
        live = lane + s * TSTEP < valid[0, 0]
        parts = []
        for c in range(COMPS):
            values = vis_ref[c, :, part].astype(f32)
            parts.append(jnp.where(live, values, 0.0))
        u_half = half_angle(uv_ref[0, 0:1, part] * scale)
        v_half = half_angle(uv_ref[0, 1:2, part] * scale)
        cos, sin = times(u_half, v_half)
        for p in range(POL):
            re, im = parts[p], parts[POL + p]
            w_tab[pl.ds(p * W_STEP, CHAN_G), :] = re * cos + im * sin
            w_tab[pl.ds((POL + p) * W_STEP, CHAN_G), :] = im * cos - re * sin
        for n, value in enumerate(odd_halves(u_half, HALF)[0]):
            u_tab[pl.ds(n, CHAN_G, U_STEP), :] = value[0]
            u_tab[pl.ds(HALF + n, CHAN_G, U_STEP), :] = value[1]
        values, steps = odd_halves(v_half, FINE)
        for n, value in enumerate(values):
            v_tab[pl.ds(4 + n, CHAN_G, V_STEP), :] = value[0]
            v_tab[pl.ds(4 + FINE + n, CHAN_G, V_STEP), :] = value[1]
        for q, value in enumerate((steps[-1], times(steps[-1], squared(steps[-1])))):
            v_tab[pl.ds(2 * q, CHAN_G, V_STEP), :] = value[0]
            v_tab[pl.ds(2 * q + 1, CHAN_G, V_STEP), :] = value[1]
        sums = None
        step = 4
        for start in range(0, CHAN_G, step):
            left, right = [], []
            for h in range(start, start + step):
                u_rows = u_tab[pl.ds(h * U_STEP, SG), :]
                column = [
                    (u_rows * v_tab[pl.ds(h * V_STEP + a, 1), :]).astype(bf16) for a in range(4)
                ]
                left.append(jnp.concatenate(column, 0))
                w_all = w_tab[pl.ds(h, COMPS, W_STEP), :]
                fine = [w_all * v_tab[pl.ds(h * V_STEP + 4 + b, 1), :] for b in range(2 * FINE)]
                right.append(jnp.concatenate(fine, 0).astype(bf16))
            term = lax.dot_general(
                jnp.concatenate(left, 1),
                jnp.concatenate(right, 1),
                (((1,), (1,)), ((), ())),
                preferred_element_type=f32,
            )
            sums = term if sums is None else sums + term
        return sums

    def keep(s, sums):
        for q in range(2):
            cos, sin = sums[2 * q * SG : (2 * q + 1) * SG], sums[(2 * q + 1) * SG : (2 * q + 2) * SG]
            cc, sc, cs, ss = cos[:HALF], cos[HALF:], sin[:HALF], sin[HALF:]
            for d, (zero, one) in enumerate(
                (((cc - ss, cc + ss), (sc + cs, cs - sc)), ((cc + ss, cc - ss), (sc - cs, -sc - cs)))
            ):
                both = jnp.concatenate([jnp.concatenate(zero, 0), jnp.concatenate(one, 0)], 1)
                high = both.astype(bf16)
                at = (2 * q + d) * LANES
                x_high[s * SG : (s + 1) * SG, at : at + LANES] = high
                x_low[s * SG : (s + 1) * SG, at : at + LANES] = (both - high.astype(f32)).astype(bf16)

    group = me[0] ^ (ks[0] - turn)
    for h in range(CHAN_G):
        scale_tab[h : h + 1, :] = jnp.full((1, LANES), scales[group * CHAN_G + h], f32)
    scale = scale_tab[...] * (2.0 * math.pi / SG)
    count = outs[0].shape[0]
    for s in range(count):
        keep(s, build(s, scale))
    image = (
        jnp.dot(x_high[...], combine[...], preferred_element_type=f32)
        + jnp.dot(x_low[...], combine[...], preferred_element_type=f32)
    ).astype(bf16)

    def write(out_ref):
        for s in range(count):
            for pair in range(2):
                out_ref[s, pair * SG : (pair + 1) * SG, :] = image[
                    s * SG : (s + 1) * SG, pair * LANES : (pair + 1) * LANES
                ]

    for i, out_ref in enumerate(outs):
        pl.when(turn == i)(functools.partial(write, out_ref))

    if with_gains:

        @pl.when(turn == len(ks) - 1)
        def _():
            for copy in copies:
                copy.wait()
            make_gains(taper, tiles, gain_ref, refs[0])


def images(ks, me, valid, scales, vis, uv, gain_args=()):
    rows = vis.shape[2]
    count = rows // TSTEP
    block = (COMPS, CHAN_G, rows)
    whole = pl.BlockSpec((count, 2 * SG, LANES), lambda i, at: (0, 0, 0))
    out_shape = [jax.ShapeDtypeStruct((count, 2 * SG, LANES), bf16)] * len(ks)
    out_specs = [whole] * len(ks)
    in_specs = [pl.BlockSpec(block, lambda i, at: (0, at[0] ^ (ks[0] - i), 0))]
    table = combine_table()
    in_specs += [
        pl.BlockSpec((1, 2, rows), lambda i, at: (0, 0, 0)),
        pl.BlockSpec(table.shape, lambda i, at: (0, 0)),
    ]
    scratch = [
        pltpu.VMEM((2, CHAN_G * U_STEP, LANES), f32),
        pltpu.VMEM((2, CHAN_G * V_STEP, LANES), f32),
        pltpu.VMEM((2, COMPS * W_STEP, LANES), f32),
        pltpu.VMEM((CHAN_G, LANES), f32),
        pltpu.VMEM((count * SG, 4 * LANES), bf16),
        pltpu.VMEM((count * SG, 4 * LANES), bf16),
    ]
    operands = [vis, uv, table]
    if gain_args:
        stations, aterm, taper = gain_args
        subs = stations.shape[3]
        tiles = lane_tiles()
        operands = [stations] + operands + [aterm, taper, tiles]
        in_specs = [smem()] + in_specs + [
            pl.BlockSpec(memory_space=pltpu.HBM),
            pl.BlockSpec(taper.shape, lambda i, at: (0, 0)),
            pl.BlockSpec(tiles.shape, lambda i, at: (0, 0)),
        ]
        out_shape += [jax.ShapeDtypeStruct((2, SG, subs, LANES), f32)]
        out_specs += [pl.BlockSpec((2, SG, subs, LANES), lambda i, at: (0, 0, 0, 0))]
        scratch += [pltpu.VMEM((2 * subs, 2, SG * SG + LANES), f32), pltpu.SemaphoreType.DMA((2 * subs,))]
    return pl.pallas_call(
        functools.partial(image_kernel, ks, bool(gain_args)),
        out_shape=out_shape,
        grid_spec=pltpu.PrefetchScalarGridSpec(
            num_scalar_prefetch=1,
            grid=(len(ks),),
            in_specs=[smem(), smem()] + in_specs,
            out_specs=out_specs,
            scratch_shapes=scratch,
        ),
        compiler_params=pltpu.CompilerParams(vmem_limit_bytes=(48 << 20) if gain_args else VMEM_LIMIT),
        cost_estimate=pl.CostEstimate(
            flops=len(ks) * count * FAN * 40000, bytes_accessed=1 << 20, transcendentals=0
        ),
        name="images",
    )(me, valid, scales, *operands)


def subgrid_kernel(chunks_n, me, owner, u_offset, v_start, gain, w_high, w_low, f_rows, *refs):
    chunks = refs[:chunks_n]
    out_ref, d_high, d_low, y_ref, pos, taken = refs[chunks_n:]
    block = chunks[0].shape[0]
    row = lax.broadcasted_iota(jnp.int32, (2, LANES), 0)

    def clear(i, _):
        taken[i] = 0
        return 0

    lax.fori_loop(0, taken.shape[0], clear, 0, unroll=8)
    out_ref[...] = jnp.zeros_like(out_ref)
    pos[...] = jnp.full(pos.shape, NO_PLACE, f32)
    for k in range(chunks_n):
        base = (me[0] ^ k) * block
        for i in range(block):
            gain_re, gain_im = gain[0, :, base + i, :], gain[1, :, base + i, :]
            for pair in range(2):
                image = chunks[k][i, pair * SG : (pair + 1) * SG, :].astype(f32)
                both = jnp.concatenate([image * gain_re, image * gain_im], 1)
                high = both.astype(bf16)
                at = pl.ds(((k * block + i) * 2 + pair) * SG, SG)
                d_high[at, :] = high
                d_low[at, :] = (both - high.astype(f32)).astype(bf16)
    step = 128
    for i in range(d_high.shape[0] // step):
        at = pl.ds(i * step, step)
        high = d_high[at, :]
        y_ref[at, :] = jnp.dot(
            jnp.concatenate([high, d_low[at, :], high], 1),
            jnp.concatenate([w_high[...], w_high[...], w_low[...]], 0),
            preferred_element_type=f32,
        )
    for k in range(chunks_n):
        base = (me[0] ^ k) * block
        for i in range(block):
            at = (k * block + i) * 2 * SG
            ys = [y_ref[pl.ds(at + pair * SG, SG), :] for pair in range(2)]
            rows = jnp.concatenate(
                [
                    jnp.concatenate([y[:, :LANES] for y in ys], 1),
                    jnp.concatenate([y[:, LANES:] for y in ys], 1),
                ],
                0,
            )
            high = rows.astype(bf16)
            low = (rows - high.astype(f32)).astype(bf16)
            cells = jnp.dot(
                f_rows[...], jnp.concatenate([high, low, high], 0), preferred_element_type=f32
            ).astype(bf16)
            s = base + i
            dest = owner[0, 0, 0, s]
            slot = jnp.minimum(taken[dest], CAP - 1)
            taken[dest] = slot + 1
            for pair in range(2):
                start = pl.multiple_of((slot * 2 + pair) * SG, SG)
                out_ref[dest, pl.ds(start, SG), :] = cells[:, pair * LANES : (pair + 1) * LANES]
            u, v = u_offset[0, 0, 0, s].astype(f32), v_start[0, 0, 0, s].astype(f32)
            pos[dest, pl.ds(2 * slot, 2), :] = jnp.where(row == 0, u, v)
    out_ref[:, CAP * 2 * SG :, :] = pos[...].astype(bf16)


def subgrids(chunks, me, owner, u_offset, v_start, gain, devices_n):
    count = owner.shape[3]
    return pl.pallas_call(
        functools.partial(subgrid_kernel, len(chunks)),
        out_shape=jax.ShapeDtypeStruct((devices_n, CAP * 2 * SG + POS_ROWS, LANES), bf16),
        in_specs=[smem()] * 4 + [vmem()] * (4 + len(chunks)),
        out_specs=vmem(),
        scratch_shapes=[
            pltpu.VMEM((count * 2 * SG, 2 * LANES), bf16),
            pltpu.VMEM((count * 2 * SG, 2 * LANES), bf16),
            pltpu.VMEM((count * 2 * SG, 2 * LANES), f32),
            pltpu.VMEM((devices_n, POS_ROWS, LANES), f32),
            pltpu.SMEM((devices_n,), jnp.int32),
        ],
        compiler_params=pltpu.CompilerParams(vmem_limit_bytes=24 << 20),
        cost_estimate=pl.CostEstimate(flops=4 * 10**9, bytes_accessed=4 << 20, transcendentals=0),
        name="subgrids",
    )(me, owner, u_offset, v_start, gain, *lane_transform(), row_transform(), *chunks)


def along_v(arrived, places, source, slot, v_index):
    cells = arrived[source, pl.ds(slot * 2 * SG, 2 * SG), :]
    stacked = jnp.concatenate([cells[:, SG * k : SG * (k + 1)] for k in range(POL)], 0)
    v = places[source, pl.ds(2 * slot + 1, 1), :]
    hot = jnp.where(v_index == jnp.concatenate([v, v], 1), 1.0, 0.0).astype(bf16)
    return jnp.dot(stacked, hot, preferred_element_type=f32)


def v_steps():
    rows = lax.broadcasted_iota(jnp.int32, (SG, BAND_V), 0)
    return (lax.broadcasted_iota(jnp.int32, (SG, BAND_V), 1) - rows).astype(f32)


def parts():
    return [
        ((k % 2) * POL + pair * 2 + k // 2, (k * 2 + pair) * SG) for k in range(POL) for pair in range(2)
    ]


def margin_kernel(arrived, out_ref, acc, places, chosen, starts):
    sources = arrived.shape[0]
    batch = 8
    first = TILE_W - SG
    acc[...] = jnp.zeros_like(acc)
    places[...] = arrived[:, CAP * 2 * SG :, :].astype(f32)
    found = jnp.int32(0)
    for source in range(sources):
        for slot in range(CAP):
            u = places[source, 2 * slot, 0].astype(jnp.int32)
            chosen[found] = source * CAP + slot
            starts[found] = u - first
            found = found + ((u > first) & (u < TILE_W)).astype(jnp.int32)
    for i in range(batch):
        chosen[found + i] = 0
        starts[found + i] = 2 * SG
    v_index = v_steps()

    def add(i, _):
        wide = []
        for j in range(batch):
            at = chosen[i * batch + j]
            wide.append(along_v(arrived, places, at // CAP, at % CAP, v_index))
        for j in range(batch):
            rows = pl.ds(starts[i * batch + j], SG)
            for comp, start in parts():
                for side in range(BAND_V // LANES):
                    acc[comp, side, rows, :] += wide[j][
                        start : start + SG, side * LANES : (side + 1) * LANES
                    ]
        return 0

    lax.fori_loop(0, (found + batch - 1) // batch, add, 0)
    for side in range(BAND_V // LANES):
        out_ref[:, :, side * LANES : (side + 1) * LANES] = acc[:, side, SG : 2 * SG, :].astype(bf16)


def margin_of(arrived):
    slots = arrived.shape[0] * CAP
    return pl.pallas_call(
        margin_kernel,
        out_shape=jax.ShapeDtypeStruct((COMPS, SG, BAND_V), bf16),
        in_specs=[vmem()],
        out_specs=vmem(),
        scratch_shapes=[
            pltpu.VMEM((COMPS, BAND_V // LANES, 3 * SG, LANES), f32),
            pltpu.VMEM((arrived.shape[0], POS_ROWS, LANES), f32),
            pltpu.SMEM((slots + 8,), jnp.int32),
            pltpu.SMEM((slots + 8,), jnp.int32),
        ],
        compiler_params=pltpu.CompilerParams(vmem_limit_bytes=16 << 20),
        name="margin",
    )(arrived)


def tile_kernel(arrived, out_ref, head_ref, columns, spread, places, result, sems):
    sources = arrived.shape[0]
    per_lanes = LANES // SG
    places[...] = arrived[:, CAP * 2 * SG :, :].astype(f32)
    lane = lax.broadcasted_iota(jnp.int32, (1, LANES), 1)
    u_index = lax.broadcasted_iota(jnp.int32, (TILE_W, LANES), 0).astype(f32)
    step_a = (lane % SG).astype(f32)
    for j in range(sources * CAP // per_lanes):
        target = None
        for q in range(per_lanes):
            slot = j * per_lanes + q
            u = places[slot // CAP, 2 * (slot % CAP) : 2 * (slot % CAP) + 1, :]
            target = u if target is None else jnp.where(lane < q * SG, target, u)
        hot = jnp.where(u_index == target + step_a, 1.0, 0.0)
        columns[:, j * LANES : (j + 1) * LANES] = hot.astype(bf16)
    v_index = v_steps()
    unrolled = min(32, sources)

    def spread_some(i, _):
        for j in range(unrolled):
            source = i * unrolled + j
            for slot in range(CAP):
                wide = along_v(arrived, places, source, slot, v_index).astype(bf16)
                at = pl.ds(pl.multiple_of((source * CAP + slot) * SG, SG), SG)
                for comp, start in parts():
                    spread[at, comp * BAND_V : (comp + 1) * BAND_V] = wide[start : start + SG]
        return 0

    lax.fori_loop(0, sources // unrolled, spread_some, 0)
    copies = []
    for comp in range(COMPS):
        result[comp] = jnp.dot(
            columns[...], spread[:, comp * BAND_V : (comp + 1) * BAND_V], preferred_element_type=f32
        )
        head_ref[comp] = result[comp, :SG, :]
        rest = pl.ds(SG, TILE_W - SG)
        copies.append(
            pltpu.make_async_copy(result.at[comp, rest], out_ref.at[comp, rest], sems.at[comp])
        )
        copies[-1].start()
    for copy in copies:
        copy.wait()


def tile_of(arrived):
    cells = arrived.shape[0] * CAP * SG
    return pl.pallas_call(
        tile_kernel,
        out_shape=(
            jax.ShapeDtypeStruct((COMPS, TILE_W, BAND_V), f32),
            jax.ShapeDtypeStruct((COMPS, SG, BAND_V), f32),
        ),
        in_specs=[vmem()],
        out_specs=(pl.BlockSpec(memory_space=pl.ANY), vmem()),
        scratch_shapes=[
            pltpu.VMEM((TILE_W, cells), bf16),
            pltpu.VMEM((cells, COMPS * BAND_V), bf16),
            pltpu.VMEM((arrived.shape[0], POS_ROWS, LANES), f32),
            pltpu.VMEM((COMPS, TILE_W, BAND_V), f32),
            pltpu.SemaphoreType.DMA((COMPS,)),
        ],
        compiler_params=pltpu.CompilerParams(vmem_limit_bytes=(10 << 20) + 2 * cells * (COMPS * BAND_V + 2 * TILE_W)),
        cost_estimate=pl.CostEstimate(flops=4 * 10**9, bytes_accessed=4 << 20, transcendentals=0),
        name="tile",
    )(arrived)


def on_device(
    visibilities, uv_rows, chan_scale, valid_rows, aterm, taper, stations, owner, u_offset, v_start
):
    groups_n = lax.axis_size("freq")
    devices_n = groups_n * lax.axis_size("tile")
    me = lax.axis_index("freq")[None].astype(jnp.int32)
    far = list(range(groups_n - 1, 1, -1))
    near = [k for k in (1, 0) if k < groups_n]
    stations, owner, u_offset, v_start = (
        jnp.swapaxes(index, 2, 3) for index in (stations, owner, u_offset, v_start)
    )
    chunks = {}

    def make(ks, gain_args=()):
        made = images(ks, me, valid_rows, chan_scale, visibilities[0], uv_rows, gain_args)
        for k, part in zip(ks, made):
            if k:
                part = lax.ppermute(part, "freq", [(i, i ^ k) for i in range(groups_n)])
            chunks[k] = part
        return made[-1]

    if far:
        make(far)
    gain = make(near, (stations, aterm, taper))
    outgoing = subgrids(
        [chunks[k] for k in range(groups_n)], me, owner, u_offset, v_start, gain, devices_n
    )
    arrived = lax.all_to_all(
        outgoing, ("freq", "tile"), split_axis=0, concat_axis=0, tiled=True
    )
    incoming = lax.ppermute(
        margin_of(arrived), ("freq", "tile"), [(i, (i + 1) % devices_n) for i in range(devices_n)]
    )
    tile, head = tile_of(arrived)
    return tile.at[:, :SG, :].set(head + incoming.astype(f32))


def solution(mesh):
    in_specs = (
        P("tile", None, None, "freq"),
        P("tile", None, "freq"),
        P(),
        P("tile", "freq"),
        P("freq", None, None, None),
        P(),
        P("tile", "freq", None, None),
        P("tile", "freq", None, None),
        P("tile", "freq", None, None),
        P("tile", "freq", None, None),
    )
    out_specs = P(None, ("freq", "tile"), None)
    return jax.shard_map(
        on_device, mesh=mesh, in_specs=in_specs, out_specs=out_specs, check_vma=False
    )
```
